32 devices in a mesh: row: 8 (over y, x, core), src: 4 (over z).
Axes of the slice: x: 2, y: 2, z: 4, core: 2. Of those that a mesh axis runs over, the one named last changes fastest.
Arguments:
- traces: bfloat16 [16384, 128, 512], P('row', 'src'), may hold values from -6 to 6
- row_source: int32 [16384], P('row'), may hold values from 0 to 16383, as said below
- slice_data: bfloat16 [2, 16384, 8, 2048], P(None, 'row', None, 'src'), may hold values from -0.03125 to 0.03125
- wavelet_inverse: float32 [2], replicated, may hold values from 0.3 to 0.8
Outputs:
- multiples: float32 [16384, 2, 128], P(('row', 'src'))
- primaries: float32 [16384, 2, 128], P(('row', 'src'))
The draws below stay inside these ranges and needn't reach their ends.
Inputs may be any that keep to these rules, and one draw needn't show every extreme that they name: `row_source`: every recording row is named exactly once; entry e * 2048 + p names a recording row whose index modulo 2048 lies in [e * 256, (e + 1) * 256).
All inputs are finite; a program needn't handle non-finite values.
Results may differ from the reference program's by a relative error of at most 0.0056.
Values may be sent and summed in bfloat16 or wider, within the bound.
No kernel may reach another device: no remote copies, remote signals or barrier semaphores. Data moves between devices by JAX's collectives and lax.ppermute only.
A program may use at most 192 MiB of HBM per device.

```python
import jax
import jax.numpy as jnp

M = 16384
PC = 128
NT = 512
FREQ = 61
ITERS = 3
N_ROW = 8


def draw_row_source(key, part):
    block_rows = M // N_ROW
    group_rows = block_rows // N_ROW
    subkeys = jax.random.split(key, N_ROW)
    shuffles = jax.vmap(lambda subkey: jax.random.permutation(subkey, block_rows))(subkeys)
    flat_order = shuffles.reshape(-1).astype(jnp.int32)
    target = jnp.arange(M, dtype=jnp.int32) // block_rows
    return (flat_order // group_rows * block_rows + target * group_rows + flat_order % group_rows).astype(jnp.int32)


def level_of(key, extent, cuts, smallest, high):
    gain, own = 1.0, jax.random.fold_in(key, 6)
    for position, shards_of in cuts:
        draws = jnp.exp(jax.random.uniform(jax.random.fold_in(own, position), (shards_of,), jnp.float32, smallest / len(cuts), high / len(cuts)))
        gain = gain * jnp.repeat(draws, extent[position] // shards_of).reshape([-1 if axis == position else 1 for axis in range(len(extent))])
    return gain


def noise(key, dims, spread, reach, shards=(), held_as=jnp.bfloat16):
    entries = spread * jax.random.normal(key, dims, jnp.float32)
    if shards:
        entries = entries * level_of(key, dims, shards, -0.22, 0.18)
    return jnp.clip(entries, -reach, reach).astype(held_as)


def setup_inputs(seed: int = 0) -> dict:
    arg_keys = jax.random.split(jax.random.key(seed), 5)
    return {
        "traces": noise(arg_keys[0], (M, PC, NT), 1.0, 6.0, ((0, 8), (1, 4))),
        "row_source": draw_row_source(jax.random.fold_in(arg_keys[4], 71), 0),
        "slice_data": noise(arg_keys[2], (2, M, N_ROW, M // N_ROW), (2 * M) ** -0.5, 0.03125, ((1, 8), (3, 4))),
        "wavelet_inverse": jnp.clip(jax.random.uniform(arg_keys[3], (2,), jnp.float32, 0.3, 0.8), 0.3, 0.8),
    }


def dft_kernel(samples):
    ticks = jnp.arange(samples, dtype=jnp.int32)
    moment = ticks.astype(jnp.float32)
    ramp_len = samples // 8
    rising = 0.5 - 0.5 * jnp.cos(jnp.pi * (moment + 0.5) / ramp_len)
    falling = 0.5 - 0.5 * jnp.cos(jnp.pi * (samples - moment - 0.5) / ramp_len)
    taper = jnp.where(ticks < ramp_len, rising, jnp.where(ticks >= samples - ramp_len, falling, jnp.ones_like(rising)))
    wrapped = ticks * FREQ % samples
    angles = 2.0 * jnp.pi / samples * wrapped.astype(jnp.float32)
    factor = 1.0 / jnp.sqrt(jnp.float32(samples))
    table = jnp.stack([taper * jnp.cos(angles) * factor, -taper * jnp.sin(angles) * factor], axis=1)
    return table.astype(jnp.bfloat16)

def reference(traces, row_source, slice_data, wavelet_inverse):
    kernel = dft_kernel(NT)
    spectra = jnp.dot(traces.reshape(M * PC, NT), kernel, preferred_element_type=jnp.float32).reshape(M, PC, 2)
    spectra = jnp.transpose(spectra, (0, 2, 1)).astype(jnp.bfloat16)
    panel = spectra[row_source]
    real_data = slice_data[0].reshape(M, M)
    imag_data = slice_data[1].reshape(M, M)
    base = panel.astype(jnp.float32)
    wave_real = wavelet_inverse[0]
    wave_imag = wavelet_inverse[1]
    estimate = panel
    pred_real = jnp.zeros((M, PC), jnp.float32)
    pred_imag = jnp.zeros((M, PC), jnp.float32)
    primaries = base
    for iteration in range(ITERS):
        stacked = estimate.reshape(M, 2 * PC)
        real_terms = jnp.dot(real_data, stacked, preferred_element_type=jnp.float32)
        imag_terms = jnp.dot(imag_data, stacked, preferred_element_type=jnp.float32)
        pred_real = real_terms[:, :PC] - imag_terms[:, PC:]
        pred_imag = real_terms[:, PC:] + imag_terms[:, :PC]
        next_real = base[:, 0] - (wave_real * pred_real - wave_imag * pred_imag)
        next_imag = base[:, 1] - (wave_real * pred_imag + wave_imag * pred_real)
        primaries = jnp.stack([next_real, next_imag], axis=1)
        estimate = primaries.astype(jnp.bfloat16)
    multiples = jnp.stack([pred_real, pred_imag], axis=1)
    return (multiples, primaries)
```

```python
import functools

import jax
import jax.numpy as jnp
import ml_dtypes
import numpy as np
from jax import lax
from jax.experimental import pallas as pl
from jax.experimental.pallas import tpu as pltpu
from jax.sharding import PartitionSpec as P

FREQ = 61
ITERS = 3
LANES = 128
VMEM = pl.BlockSpec(memory_space=pltpu.VMEM)
SMEM = pl.BlockSpec(memory_space=pltpu.SMEM)


def dft_table(samples):
    ticks = np.arange(samples, dtype=np.int32)
    moment = ticks.astype(np.float32)
    ramp_len = samples // 8
    pi = np.float32(np.pi)
    half = np.float32(0.5)
    rising = half - half * np.cos(pi * (moment + half) / np.float32(ramp_len))
    falling = half - half * np.cos(pi * (np.float32(samples) - moment - half) / np.float32(ramp_len))
    taper = np.where(
        ticks < ramp_len, rising, np.where(ticks >= samples - ramp_len, falling, np.ones_like(rising))
    )
    wrapped = ticks * FREQ % samples
    angles = np.float32(2.0 * np.pi / samples) * wrapped.astype(np.float32)
    factor = np.float32(1.0) / np.sqrt(np.float32(samples))
    table = np.stack([taper * np.cos(angles) * factor, -taper * np.sin(angles) * factor], axis=1)
    return table.astype(ml_dtypes.bfloat16)


def params(megabytes):
    return pltpu.CompilerParams(vmem_limit_bytes=megabytes * 2**20)


def cost(flops, moved):
    return pl.CostEstimate(flops=int(flops), bytes_accessed=int(moved), transcendentals=0)


def spectra_kernel(packs, place_ref, traces_ref, table_ref, *out_refs):
    block, shots, samples = traces_ref.shape
    width = 2 * shots
    shot = lax.broadcasted_iota(jnp.int32, (1, shots, LANES), 1)
    lane = lax.broadcasted_iota(jnp.int32, (1, shots, LANES), 2)
    own = lane % shots == shot
    chunk = min(block, 16)
    rows = []
    for start in range(0, block, chunk):
        part = traces_ref[start : start + chunk].reshape(chunk * shots, samples)
        terms = jnp.dot(part, table_ref[...], preferred_element_type=jnp.float32)
        rows.append(jnp.sum(jnp.where(own, terms.reshape(chunk, shots, LANES), 0.0), axis=1))
    spectra = jnp.concatenate(rows, axis=0)
    short = block // packs
    column = lax.broadcasted_iota(jnp.int32, (short, LANES), 1)
    packed = spectra[:short]
    for part in range(1, packs):
        packed = jnp.where(column // width == part, spectra[part * short : (part + 1) * short], packed)
    packed = packed.astype(jnp.bfloat16)
    steps = pl.num_programs(0) // len(out_refs)
    for turn, out_ref in enumerate(out_refs):

        @pl.when(pl.program_id(0) // steps == turn)
        def _():
            out_ref[0] = packed


def make_spectra(traces, place, n_row, packs, block):
    block_rows, shots, samples = traces.shape
    steps = block_rows // n_row // block
    short = block // packs
    table = jnp.asarray(np.tile(np.repeat(dft_table(samples), shots, axis=1), (1, packs)))

    def source(step, place_ref):
        return (place_ref[0] ^ (step // steps)) * steps + step % steps, 0, 0

    def target(turn, step, place_ref):
        return jnp.clip(step - turn * steps, 0, steps - 1), 0, 0

    outs = pl.pallas_call(
        functools.partial(spectra_kernel, packs),
        grid_spec=pltpu.PrefetchScalarGridSpec(
            num_scalar_prefetch=1,
            grid=(n_row * steps,),
            in_specs=[
                pl.BlockSpec((block, shots, samples), source),
                pl.BlockSpec((samples, LANES), lambda step, place_ref: (0, 0)),
            ],
            out_specs=[
                pl.BlockSpec((1, short, LANES), functools.partial(target, turn)) for turn in range(n_row)
            ],
        ),
        out_shape=[jax.ShapeDtypeStruct((steps, short, LANES), jnp.bfloat16)] * n_row,
        compiler_params=params(48),
        cost_estimate=cost(2 * traces.size * LANES, 2 * traces.size),
        name="spectra",
    )(place, traces, table)
    return [out.reshape(steps * short, LANES) for out in outs]


def order_kernel(packs, n_src, place_ref, code_ref, *refs):
    pieces, out_refs = refs[:-n_src], refs[-n_src:]
    width = LANES // packs
    held = jnp.concatenate([ref[...] for ref in pieces], axis=0)
    rolled = [held] + [
        pltpu.roll(held.astype(jnp.float32), turn * width, 1).astype(jnp.bfloat16) for turn in range(1, packs)
    ]
    table = jnp.concatenate(rolled, axis=1)
    depth = table.shape[0]
    slice_rows = code_ref.shape[0] // n_src
    short = slice_rows // packs
    column = lax.broadcasted_iota(jnp.int32, (short, LANES), 1)
    for turn, out_ref in enumerate(out_refs):
        first = pl.multiple_of((place_ref[1] ^ turn) * slice_rows, slice_rows)
        packed = None
        for part in range(packs):
            code = code_ref[pl.ds(pl.multiple_of(first + part * short, short), short), :]
            position, side = code // packs, code % packs
            hits = []
            for start in range(0, depth, LANES):
                hits.append(jnp.where(position == column + start, 1.0, 0.0).astype(jnp.bfloat16))
            chosen = jnp.concatenate(hits, axis=1)[:, :depth]
            rows = jnp.dot(chosen, table, preferred_element_type=jnp.float32)
            moved = rows[:, :LANES]
            for turned in range(1, packs):
                moved = jnp.where(
                    (part - side + packs) % packs == turned, rows[:, turned * LANES : (turned + 1) * LANES], moved
                )
            packed = moved if packed is None else jnp.where(column // width == part, moved, packed)
        out_ref[...] = packed.astype(jnp.bfloat16)


def make_order(code, pieces, place, n_src, packs):
    slice_rows = code.shape[0] // n_src
    return pl.pallas_call(
        functools.partial(order_kernel, packs, n_src),
        in_specs=[SMEM] + [VMEM] * (1 + len(pieces)),
        out_specs=[VMEM] * n_src,
        out_shape=[jax.ShapeDtypeStruct((slice_rows // packs, LANES), jnp.bfloat16)] * n_src,
        compiler_params=params(48),
        cost_estimate=cost(2 * code.shape[0] * len(pieces) * pieces[0].size * packs, 4 * code.size),
        name="order",
    )(place, code, *pieces)


def panel_kernel(packs, place_ref, *refs):
    pieces, panel_ref = refs[:-1], refs[-1]
    short = pieces[0].shape[0]
    width = LANES // packs
    shots = width // 2
    columns = panel_ref.shape[1]
    whole_shots = columns // 2
    lane = lax.broadcasted_iota(jnp.int32, (LANES, packs * columns), 0)
    target = lax.broadcasted_iota(jnp.int32, (LANES, packs * columns), 1)
    goes = lane // width * columns + lane % width // shots * whole_shots + lane % shots
    total = None
    for turn, piece in enumerate(pieces):
        shift = (place_ref[1] ^ turn) * shots
        chosen = jnp.where(target == goes + shift, 1.0, 0.0).astype(jnp.bfloat16)
        term = jnp.dot(piece[...], chosen, preferred_element_type=jnp.float32)
        total = term if total is None else total + term
    for part in range(packs):
        panel_ref[part * short : (part + 1) * short, :] = total[:, part * columns : (part + 1) * columns].astype(
            jnp.bfloat16
        )


def make_panel(pieces, place, packs):
    short = pieces[0].shape[0]
    columns = len(pieces) * (LANES // packs)
    return pl.pallas_call(
        functools.partial(panel_kernel, packs),
        in_specs=[SMEM] + [VMEM] * len(pieces),
        out_specs=VMEM,
        out_shape=jax.ShapeDtypeStruct((short * packs, columns), jnp.bfloat16),
        compiler_params=params(32),
        cost_estimate=cost(2 * len(pieces) * short * LANES * packs * columns, 4 * short * packs * columns),
        name="panel",
    )(place, *pieces)


def relay_kernel(data_ref, out_ref):
    blocks, offsets = data_ref.shape[2:]
    turned = jnp.swapaxes(data_ref[0], 0, 1)
    for block in range(blocks):
        out_ref[:, block * offsets : (block + 1) * offsets] = turned[block]


def relay(slice_data, part, step_rows):
    _, block_rows, blocks, offsets = slice_data.shape
    return pl.pallas_call(
        relay_kernel,
        grid=(block_rows // step_rows,),
        in_specs=[pl.BlockSpec((1, step_rows, blocks, offsets), lambda step: (part, step, 0, 0))],
        out_specs=pl.BlockSpec((step_rows, blocks * offsets), lambda step: (step, 0)),
        out_shape=jax.ShapeDtypeStruct((block_rows, blocks * offsets), jnp.bfloat16),
        compiler_params=params(32),
        cost_estimate=cost(0, 2 * slice_data.size),
        name="relay",
    )(slice_data)


def terms_kernel(turns, place_ref, real_ref, imag_ref, *refs):
    pieces = refs[: -1 - len(turns)]
    out_refs, held = refs[-1 - len(turns) : -1], refs[-1]
    offsets, columns = pieces[0].shape
    depth = held.shape[0] // 2
    shots = columns // 2

    @pl.when(pl.program_id(0) == 0)
    def _():
        for turn, piece in enumerate(pieces):
            first = pl.multiple_of((place_ref[0] ^ turn) * offsets, offsets)
            held[pl.ds(first, offsets), :] = piece[...]
            second = pl.multiple_of(first + depth, offsets)
            held[pl.ds(second, offsets), :shots] = -piece[:, shots:]
            held[pl.ds(second, offsets), shots:] = piece[:, :shots]

    total = jnp.dot(real_ref[...], held[:depth], preferred_element_type=jnp.float32)
    total += jnp.dot(imag_ref[...], held[depth:], preferred_element_type=jnp.float32)
    steps = pl.num_programs(0) // len(turns)
    for number, out_ref in enumerate(out_refs):

        @pl.when(pl.program_id(0) // steps == number)
        def _():
            out_ref[...] = total.astype(out_ref.dtype)


def make_terms(real_data, imag_data, pieces, place, turns, slice_rows):
    depth = real_data.shape[1]
    offsets, columns = pieces[0].shape
    tile = min(slice_rows, 128)
    steps = slice_rows // tile

    def source(step, place_ref):
        index = step // steps
        turn = turns[-1]
        for number in range(len(turns) - 1):
            turn = jnp.where(index == number, turns[number], turn)
        return (place_ref[1] ^ turn) * steps + step % steps, 0

    def target(number, step, place_ref):
        return jnp.clip(step - number * steps, 0, steps - 1), 0

    whole = pl.BlockSpec((offsets, columns), lambda step, place_ref: (0, 0))
    rows = len(turns) * slice_rows
    return pl.pallas_call(
        functools.partial(terms_kernel, turns),
        grid_spec=pltpu.PrefetchScalarGridSpec(
            num_scalar_prefetch=1,
            grid=(len(turns) * steps,),
            in_specs=[pl.BlockSpec((tile, depth), source)] * 2 + [whole] * len(pieces),
            out_specs=[
                pl.BlockSpec((tile, columns), functools.partial(target, number)) for number in range(len(turns))
            ],
            scratch_shapes=[pltpu.VMEM((2 * depth, columns), jnp.bfloat16)],
        ),
        out_shape=[
            jax.ShapeDtypeStruct((slice_rows, columns), jnp.bfloat16 if turn else jnp.float32) for turn in turns
        ],
        compiler_params=params(48),
        cost_estimate=cost(4 * rows * depth * columns, 4 * rows * depth),
        name="terms",
    )(place, real_data, imag_data, *pieces)


def update(wave_ref, own_ref, others, panel_ref):
    predicted = own_ref[...]
    for other in others:
        predicted += other[...].astype(jnp.float32)
    shots = predicted.shape[1] // 2
    base = panel_ref[...].astype(jnp.float32)
    real, imag = predicted[:, :shots], predicted[:, shots:]
    next_real = base[:, :shots] - (wave_ref[0] * real - wave_ref[1] * imag)
    next_imag = base[:, shots:] - (wave_ref[0] * imag + wave_ref[1] * real)
    return real, imag, next_real, next_imag


def estimate_kernel(wave_ref, own_ref, *refs):
    *others, panel_ref, out_ref = refs
    shots = out_ref.shape[1] // 2
    _, _, next_real, next_imag = update(wave_ref, own_ref, others, panel_ref)
    out_ref[:, :shots] = next_real.astype(jnp.bfloat16)
    out_ref[:, shots:] = next_imag.astype(jnp.bfloat16)


def last_kernel(wave_ref, own_ref, *refs):
    *others, panel_ref, multiples_ref, primaries_ref = refs
    real, imag, next_real, next_imag = update(wave_ref, own_ref, others, panel_ref)
    multiples_ref[:, 0, :] = real
    multiples_ref[:, 1, :] = imag
    primaries_ref[:, 0, :] = next_real
    primaries_ref[:, 1, :] = next_imag


def make_update(wavelet, own, others, panel, last):
    rows, columns = panel.shape
    if last:
        shape = [jax.ShapeDtypeStruct((rows, 2, columns // 2), jnp.float32)] * 2
    else:
        shape = jax.ShapeDtypeStruct((rows, columns), jnp.bfloat16)
    return pl.pallas_call(
        last_kernel if last else estimate_kernel,
        in_specs=[SMEM] + [VMEM] * (2 + len(others)),
        out_specs=[VMEM] * 2 if last else VMEM,
        out_shape=shape,
        compiler_params=params(32),
        cost_estimate=cost(16 * rows * columns, 16 * rows * columns),
        name="update",
    )(wavelet, own, *others, panel)


def swap(array, axis, bits):
    size = lax.axis_size(axis)
    return lax.ppermute(array, axis, [(index, index ^ bits) for index in range(size)])


def spread(array, axis):
    size = lax.axis_size(axis)
    pieces = {0: array}
    for turn in range(2, size, 2):
        pieces[turn] = swap(array, axis, turn)
    for turn in range(0, size, 2):
        pieces[turn + 1] = swap(pieces[turn], axis, 1)
    return [pieces[turn] for turn in range(size)]


def body(traces, row_source, slice_data, wavelet_inverse):
    block_rows, shots, _ = traces.shape
    n_row, n_src = lax.axis_size("row"), lax.axis_size("src")
    row, src = lax.axis_index("row"), lax.axis_index("src")
    place = jnp.stack([row, src]).astype(jnp.int32)
    packs = LANES // (2 * shots)
    group_rows = block_rows // n_row
    slice_rows = block_rows // n_src
    block = min(group_rows, 128)
    short = block // packs

    spectra = make_spectra(traces, place, n_row, packs, block)
    arrived = [spectra[0]] + [swap(spectra[turn], "row", turn) for turn in range(1, n_row)]

    inside = row_source % group_rows
    position = (row_source // block_rows ^ row) * (group_rows // packs) + inside // block * short + inside % short
    code = position * packs + inside % block // short
    code = jnp.broadcast_to(code[:, None], (block_rows, LANES))
    ordered = make_order(code, arrived, place, n_src, packs)
    located = [ordered[0]] + [swap(ordered[turn], "src", turn) for turn in range(1, n_src)]
    panel = make_panel(located, place, packs)

    step_rows = min(block_rows, 128)
    real_data = relay(slice_data, 0, step_rows)
    imag_data = relay(slice_data, 1, step_rows)

    half = n_src // 2
    far = tuple(range(half, n_src))
    near = tuple(range(half - 1, -1, -1))
    estimate = panel
    for iteration in range(ITERS):
        pieces = spread(estimate, "row")
        terms = dict(zip(far, make_terms(real_data, imag_data, pieces, place, far, slice_rows)))
        arriving = [swap(terms[turn], "src", turn) for turn in far]
        terms.update(zip(near, make_terms(real_data, imag_data, pieces, place, near, slice_rows)))
        arriving += [swap(terms[turn], "src", turn) for turn in near if turn]
        estimate = make_update(wavelet_inverse, terms[0], arriving, panel, iteration == ITERS - 1)
    return tuple(estimate)


def solution(mesh):
    in_specs = (P("row", "src", None), P("row"), P(None, "row", None, "src"), P())
    out_specs = (P(("row", "src"), None, None), P(("row", "src"), None, None))
    return jax.shard_map(body, mesh=mesh, in_specs=in_specs, out_specs=out_specs, check_vma=False)
```

```python
import functools

import jax
import jax.numpy as jnp
import ml_dtypes
import numpy as np
from jax import lax
from jax.experimental import pallas as pl
from jax.experimental.pallas import tpu as pltpu
from jax.sharding import PartitionSpec as P

FREQ = 61
ITERS = 3
LANES = 128
SPLITS = 2
VMEM = pl.BlockSpec(memory_space=pltpu.VMEM)
ANY = pl.BlockSpec(memory_space=pl.ANY)
SMEM = pl.BlockSpec(memory_space=pltpu.SMEM)


def dft_table(samples):
    ticks = np.arange(samples, dtype=np.int32)
    moment = ticks.astype(np.float32)
    ramp_len = samples // 8
    pi = np.float32(np.pi)
    half = np.float32(0.5)
    rising = half - half * np.cos(pi * (moment + half) / np.float32(ramp_len))
    falling = half - half * np.cos(pi * (np.float32(samples) - moment - half) / np.float32(ramp_len))
    taper = np.where(
        ticks < ramp_len, rising, np.where(ticks >= samples - ramp_len, falling, np.ones_like(rising))
    )
    wrapped = ticks * FREQ % samples
    angles = np.float32(2.0 * np.pi / samples) * wrapped.astype(np.float32)
    factor = np.float32(1.0) / np.sqrt(np.float32(samples))
    table = np.stack([taper * np.cos(angles) * factor, -taper * np.sin(angles) * factor], axis=1)
    return table.astype(ml_dtypes.bfloat16)


def params(megabytes):
    return pltpu.CompilerParams(vmem_limit_bytes=megabytes * 2**20)


def cost(flops, moved):
    return pl.CostEstimate(flops=int(flops), bytes_accessed=int(moved), transcendentals=0)


def spectra_kernel(packs, place_ref, traces_ref, table_ref, *out_refs):
    block, shots, samples = traces_ref.shape
    width = 2 * shots
    half = block // 2
    shot = lax.broadcasted_iota(jnp.int32, (1, shots, 2 * LANES), 1)
    lane = lax.broadcasted_iota(jnp.int32, (1, shots, 2 * LANES), 2)
    own = lane % shots == shot
    sides = [traces_ref[side * half : (side + 1) * half].reshape(half * shots, samples) for side in range(2)]
    terms = jnp.dot(jnp.concatenate(sides, axis=1), table_ref[...], preferred_element_type=jnp.float32)
    rows = jnp.sum(jnp.where(own, terms.reshape(half, shots, 2 * LANES), 0.0), axis=1)
    spectra = jnp.concatenate([rows[:, :LANES], rows[:, LANES:]], axis=0)
    short = block // packs
    column = lax.broadcasted_iota(jnp.int32, (short, LANES), 1)
    packed = spectra[:short]
    for part in range(1, packs):
        packed = jnp.where(column // width == part, spectra[part * short : (part + 1) * short], packed)
    packed = packed.astype(jnp.bfloat16)
    steps = pl.num_programs(0) // len(out_refs)
    for turn, out_ref in enumerate(out_refs):

        @pl.when(pl.program_id(0) // steps == turn)
        def _():
            out_ref[0] = packed


def make_spectra(traces, place, n_row, packs, block):
    block_rows, shots, samples = traces.shape
    steps = block_rows // n_row // block
    short = block // packs
    columns = np.tile(np.repeat(dft_table(samples), shots, axis=1), (1, packs))
    table = jnp.asarray(np.block([[columns, 0 * columns], [0 * columns, columns]]))

    def source(step, place_ref):
        return (place_ref[0] ^ (step // steps)) * steps + step % steps, 0, 0

    def target(turn, step, place_ref):
        return jnp.clip(step - turn * steps, 0, steps - 1), 0, 0

    outs = pl.pallas_call(
        functools.partial(spectra_kernel, packs),
        grid_spec=pltpu.PrefetchScalarGridSpec(
            num_scalar_prefetch=1,
            grid=(n_row * steps,),
            in_specs=[
                pl.BlockSpec((block, shots, samples), source),
                pl.BlockSpec((2 * samples, 2 * LANES), lambda step, place_ref: (0, 0)),
            ],
            out_specs=[
                pl.BlockSpec((1, short, LANES), functools.partial(target, turn)) for turn in range(n_row)
            ],
        ),
        out_shape=[jax.ShapeDtypeStruct((steps, short, LANES), jnp.bfloat16)] * n_row,
        compiler_params=params(48),
        cost_estimate=cost(2 * traces.size * LANES, 2 * traces.size),
        name="spectra",
    )(place, traces, table)
    return [out.reshape(steps * short, LANES) for out in outs]


def order_kernel(packs, n_src, place_ref, code_ref, *refs):
    pieces, out_refs = refs[: -n_src - 1], refs[-n_src:]
    width = LANES // packs
    held = jnp.concatenate([ref[...] for ref in pieces], axis=0)
    rolled = [held] + [
        pltpu.roll(held.astype(jnp.float32), turn * width, 1).astype(jnp.bfloat16) for turn in range(1, packs)
    ]
    table = jnp.concatenate(rolled, axis=1)
    depth = table.shape[0]
    slice_rows = code_ref.shape[0] // n_src
    short = slice_rows // packs
    column = lax.broadcasted_iota(jnp.int32, (short, LANES), 1)
    for turn, out_ref in enumerate(out_refs):
        first = pl.multiple_of((place_ref[1] ^ turn) * slice_rows, slice_rows)
        packed = None
        for part in range(packs):
            code = code_ref[pl.ds(pl.multiple_of(first + part * short, short), short), :]
            position, side = code // packs, code % packs
            hits = []
            for start in range(0, depth, LANES):
                hits.append(jnp.where(position == column + start, 1.0, 0.0).astype(jnp.bfloat16))
            chosen = jnp.concatenate(hits, axis=1)[:, :depth]
            rows = jnp.dot(chosen, table, preferred_element_type=jnp.float32)
            moved = rows[:, :LANES]
            for turned in range(1, packs):
                moved = jnp.where(
                    (part - side + packs) % packs == turned, rows[:, turned * LANES : (turned + 1) * LANES], moved
                )
            packed = moved if packed is None else jnp.where(column // width == part, moved, packed)
        out_ref[...] = packed.astype(jnp.bfloat16)


def make_order(code, pieces, place, n_src, packs, after):
    slice_rows = code.shape[0] // n_src
    return pl.pallas_call(
        functools.partial(order_kernel, packs, n_src),
        in_specs=[SMEM] + [VMEM] * (1 + len(pieces)) + [ANY],
        out_specs=[VMEM] * n_src,
        out_shape=[jax.ShapeDtypeStruct((slice_rows // packs, LANES), jnp.bfloat16)] * n_src,
        compiler_params=params(6),
        cost_estimate=cost(2 * code.shape[0] * len(pieces) * pieces[0].size * packs, 4 * code.size),
        name="order",
    )(place, code, *pieces, after)


def panel_kernel(packs, split, n_src, place_ref, *refs):
    pieces, panel_ref = refs[:n_src], refs[-1]
    short = pieces[0].shape[0]
    width = LANES // packs
    shots = width // 2
    columns = panel_ref.shape[1]
    kept = columns // 2
    lane = lax.broadcasted_iota(jnp.int32, (LANES, packs * columns), 0)
    target = lax.broadcasted_iota(jnp.int32, (LANES, packs * columns), 1)
    total = None
    for turn, piece in enumerate(pieces):
        shot = (place_ref[1] ^ turn) * shots + lane % shots
        goes = lane // width * columns + lane % width // shots * kept + shot % kept
        chosen = jnp.where((target == goes) & (shot // kept == split), 1.0, 0.0).astype(jnp.bfloat16)
        term = jnp.dot(piece[...], chosen, preferred_element_type=jnp.float32)
        total = term if total is None else total + term
    for part in range(packs):
        panel_ref[part * short : (part + 1) * short, :] = total[:, part * columns : (part + 1) * columns].astype(
            jnp.bfloat16
        )


def make_panel(pieces, place, packs, split, after):
    short = pieces[0].shape[0]
    columns = len(pieces) * (LANES // packs) // SPLITS
    return pl.pallas_call(
        functools.partial(panel_kernel, packs, split, len(pieces)),
        in_specs=[SMEM] + [VMEM] * len(pieces) + [ANY] * len(after),
        out_specs=VMEM,
        out_shape=jax.ShapeDtypeStruct((short * packs, columns), jnp.bfloat16),
        compiler_params=params(4),
        cost_estimate=cost(2 * len(pieces) * short * LANES * packs * columns, 4 * short * packs * columns),
        name="panel",
    )(place, *pieces, *after)


def relay_kernel(data_ref, after_ref, out_ref, token_ref):
    token_ref[...] = jnp.zeros_like(token_ref)
    step_rows, blocks, offsets = data_ref.shape[1:]
    turned = jnp.swapaxes(data_ref[0], 0, 1)
    first = pl.multiple_of(pl.program_id(0) * step_rows, step_rows)
    for block in range(blocks):
        out_ref[pl.ds(first, step_rows), block * offsets : (block + 1) * offsets] = turned[block]


def relay(slice_data, part, step_rows, after):
    _, block_rows, blocks, offsets = slice_data.shape
    return pl.pallas_call(
        relay_kernel,
        grid=(block_rows // step_rows,),
        in_specs=[pl.BlockSpec((1, step_rows, blocks, offsets), lambda step: (part, step, 0, 0)), ANY],
        out_specs=[VMEM] * 2,
        out_shape=[
            jax.ShapeDtypeStruct((block_rows, blocks * offsets), jnp.bfloat16),
            jax.ShapeDtypeStruct((8, LANES), jnp.float32),
        ],
        compiler_params=params(12),
        cost_estimate=cost(0, 2 * slice_data.size),
        name="relay",
    )(slice_data, after)


def turn_round(array, sign):
    lane = lax.broadcasted_iota(jnp.int32, array.shape, 1)
    kept = array.shape[1] // 2
    return jnp.where((lane < kept) == (sign > 0), -pltpu.roll(array, kept, 1), pltpu.roll(array, kept, 1))


def terms_kernel(turns, n_pieces, place_ref, real_ref, imag_ref, *refs):
    pieces = refs[:n_pieces]
    out_refs, held = refs[-1 - len(turns) : -1], refs[-1]
    offsets = pieces[0].shape[0]
    depth = held.shape[0] // 2
    for turn, piece in enumerate(pieces):
        first = pl.multiple_of((place_ref[0] ^ turn) * offsets, offsets)
        held[pl.ds(first, offsets), :] = piece[...]
        second = pl.multiple_of(first + depth, offsets)
        held[pl.ds(second, offsets), :] = turn_round(piece[...].astype(jnp.float32), 1).astype(jnp.bfloat16)
    for turn, out_ref in zip(turns, out_refs):
        rows = out_ref.shape[0]
        first = pl.multiple_of((place_ref[1] ^ turn) * rows, rows)
        total = jnp.dot(real_ref[pl.ds(first, rows), :], held[:depth], preferred_element_type=jnp.float32)
        total += jnp.dot(imag_ref[pl.ds(first, rows), :], held[depth:], preferred_element_type=jnp.float32)
        out_ref[...] = total.astype(out_ref.dtype)


def make_terms(real_data, imag_data, pieces, place, turns, slice_rows, after):
    depth = real_data.shape[1]
    columns = pieces[0].shape[1]
    rows = len(turns) * slice_rows
    return pl.pallas_call(
        functools.partial(terms_kernel, turns, len(pieces)),
        in_specs=[SMEM] + [VMEM] * (2 + len(pieces)) + [ANY] * len(after),
        out_specs=[VMEM] * len(turns),
        out_shape=[
            jax.ShapeDtypeStruct((slice_rows, columns), jnp.bfloat16 if turn else jnp.float32) for turn in turns
        ],
        scratch_shapes=[pltpu.VMEM((2 * depth, columns), jnp.bfloat16)],
        compiler_params=params(8),
        cost_estimate=cost(4 * rows * depth * columns * 2, 4 * rows * depth),
        name="terms",
    )(place, real_data, imag_data, *pieces, *after)


def update(wave_ref, own_ref, others, panel_ref):
    predicted = own_ref[...]
    for other in others:
        predicted += other[...].astype(jnp.float32)
    scaled = wave_ref[0] * predicted + wave_ref[1] * turn_round(predicted, 1)
    return predicted, panel_ref[...].astype(jnp.float32) - scaled


def estimate_kernel(wave_ref, own_ref, *refs):
    *others, panel_ref, out_ref = refs
    out_ref[...] = update(wave_ref, own_ref, others, panel_ref)[1].astype(jnp.bfloat16)


def last_kernel(wave_ref, *refs):
    *given, multiples_ref, primaries_ref = refs
    count = len(given) // SPLITS
    for split in range(SPLITS):
        own_ref, *others, panel_ref = given[split * count : (split + 1) * count]
        predicted, primaries = update(wave_ref, own_ref, others, panel_ref)
        kept = predicted.shape[1] // 2
        shots = slice(split * kept, (split + 1) * kept)
        multiples_ref[:, 0, shots] = predicted[:, :kept]
        multiples_ref[:, 1, shots] = predicted[:, kept:]
        primaries_ref[:, 0, shots] = primaries[:, :kept]
        primaries_ref[:, 1, shots] = primaries[:, kept:]


def make_update(wavelet, given):
    rows, columns = given[-1].shape
    return pl.pallas_call(
        estimate_kernel,
        in_specs=[SMEM] + [VMEM] * len(given),
        out_specs=VMEM,
        out_shape=jax.ShapeDtypeStruct((rows, columns), jnp.bfloat16),
        compiler_params=params(4),
        cost_estimate=cost(16 * rows * columns, 16 * rows * columns),
        name="update",
    )(wavelet, *given)


def make_last(wavelet, given):
    rows, columns = given[-1].shape
    return pl.pallas_call(
        last_kernel,
        in_specs=[SMEM] + [VMEM] * len(given),
        out_specs=[VMEM] * 2,
        out_shape=[jax.ShapeDtypeStruct((rows, 2, SPLITS * columns // 2), jnp.float32)] * 2,
        compiler_params=params(8),
        cost_estimate=cost(32 * rows * columns, 32 * rows * columns),
        name="last",
    )(wavelet, *given)


def swap(array, axis, bits):
    size = lax.axis_size(axis)
    return lax.ppermute(array, axis, [(index, index ^ bits) for index in range(size)])


def spread(array, axis):
    size = lax.axis_size(axis)
    pieces = {0: array}
    for turn in range(2, size, 2):
        pieces[turn] = swap(array, axis, turn)
    for turn in range(0, size, 2):
        pieces[turn + 1] = swap(pieces[turn], axis, 1)
    return [pieces[turn] for turn in range(size)]


def body(traces, row_source, slice_data, wavelet_inverse):
    block_rows, shots, _ = traces.shape
    n_row, n_src = lax.axis_size("row"), lax.axis_size("src")
    row, src = lax.axis_index("row"), lax.axis_index("src")
    place = jnp.stack([row, src]).astype(jnp.int32)
    packs = LANES // (2 * shots)
    group_rows = block_rows // n_row
    slice_rows = block_rows // n_src
    block = min(group_rows, 128)
    short = block // packs

    spectra = make_spectra(traces, place, n_row, packs, block)
    arrived = [spectra[0]] + [swap(spectra[turn], "row", turn) for turn in range(1, n_row)]

    inside = row_source % group_rows
    position = (row_source // block_rows ^ row) * (group_rows // packs) + inside // block * short + inside % short
    code = position * packs + inside % block // short
    code = jnp.broadcast_to(code[:, None], (block_rows, LANES))
    step_rows = min(block_rows, 128)
    real_data, real_token = relay(slice_data, 0, step_rows, spectra[0])
    ordered = make_order(code, arrived, place, n_src, packs, real_token)
    located = [ordered[0]] + [swap(ordered[turn], "src", turn) for turn in range(1, n_src)]
    imag_data, imag_token = relay(slice_data, 1, step_rows, ordered[0])
    panels = [make_panel(located, place, packs, 0, [imag_token])]
    first_pieces = spread(panels[0], "row")
    for split in range(1, SPLITS):
        panels.append(make_panel(located, place, packs, split, first_pieces))

    far = tuple(range(n_src // 2, n_src))
    near = tuple(range(n_src // 2 - 1, -1, -1))
    estimates = list(panels)
    given = [None] * SPLITS
    after = []
    for iteration in range(ITERS):
        for split in range(SPLITS):
            pieces = spread(estimates[split], "row") if iteration or split else first_pieces
            terms = dict(zip(far, make_terms(real_data, imag_data, pieces, place, far, slice_rows, after)))
            arriving = [swap(terms[turn], "src", turn) for turn in far]
            before = (split + 1) % SPLITS
            after = [terms[far[0]]]
            if given[before] is not None and not (iteration == ITERS - 1 and split):
                estimates[before] = make_update(wavelet_inverse, given[before])
                after = [estimates[before]]
            terms.update(
                zip(near, make_terms(real_data, imag_data, pieces, place, near, slice_rows, after))
            )
            after = [terms[0]]
            arriving += [swap(terms[turn], "src", turn) for turn in near if turn]
            given[split] = [terms[0], *arriving, panels[split]]
    return tuple(make_last(wavelet_inverse, sum(given, [])))


def solution(mesh):
    in_specs = (P("row", "src", None), P("row"), P(None, "row", None, "src"), P())
    out_specs = (P(("row", "src"), None, None), P(("row", "src"), None, None))
    return jax.shard_map(body, mesh=mesh, in_specs=in_specs, out_specs=out_specs, check_vma=False)
```

```python
import functools

import jax
import jax.numpy as jnp
import ml_dtypes
import numpy as np
from jax import lax
from jax.experimental import pallas as pl
from jax.experimental.pallas import tpu as pltpu
from jax.sharding import PartitionSpec as P

FREQ = 61
ITERS = 3
LANES = 128
BUFFERS = 4
VMEM = pl.BlockSpec(memory_space=pltpu.VMEM)
ANY = pl.BlockSpec(memory_space=pl.ANY)
SMEM = pl.BlockSpec(memory_space=pltpu.SMEM)


def dft_table(samples):
    ticks = np.arange(samples, dtype=np.int32)
    moment = ticks.astype(np.float32)
    ramp_len = samples // 8
    pi = np.float32(np.pi)
    half = np.float32(0.5)
    rising = half - half * np.cos(pi * (moment + half) / np.float32(ramp_len))
    falling = half - half * np.cos(pi * (np.float32(samples) - moment - half) / np.float32(ramp_len))
    taper = np.where(
        ticks < ramp_len, rising, np.where(ticks >= samples - ramp_len, falling, np.ones_like(rising))
    )
    wrapped = ticks * FREQ % samples
    angles = np.float32(2.0 * np.pi / samples) * wrapped.astype(np.float32)
    factor = np.float32(1.0) / np.sqrt(np.float32(samples))
    table = np.stack([taper * np.cos(angles) * factor, -taper * np.sin(angles) * factor], axis=1)
    return table.astype(ml_dtypes.bfloat16)


def params(megabytes):
    return pltpu.CompilerParams(vmem_limit_bytes=megabytes * 2**20)


def cost(flops, moved):
    return pl.CostEstimate(flops=int(flops), bytes_accessed=int(moved), transcendentals=0)


def streamed(steps, source, held, sems, work):
    slots = held.shape[0]

    def copy(step):
        slot = step % slots
        return pltpu.make_async_copy(source(step), held.at[slot], sems.at[slot])

    for step in range(min(slots - 1, steps)):
        copy(step).start()

    @pl.loop(0, steps)
    def _(step):
        @pl.when(step + slots - 1 < steps)
        def _():
            copy(step + slots - 1).start()

        copy(step).wait()
        work(step, held.at[step % slots])


def spectra_kernel(packs, n_row, place_ref, traces_ref, table_ref, *refs):
    out_refs, held, sems = refs[:n_row], refs[n_row], refs[n_row + 1]
    block = held.shape[1]
    steps = traces_ref.shape[0] // n_row // block

    def source(step):
        first = ((place_ref[0] ^ (step // steps)) * steps + step % steps) * block
        return traces_ref.at[pl.ds(pl.multiple_of(first, block), block)]

    def work(step, traces):
        packed = spectra_of(packs, traces, table_ref)
        for turn, out_ref in enumerate(out_refs):

            @pl.when(step // steps == turn)
            def _():
                out_ref[step % steps] = packed

    streamed(n_row * steps, source, held, sems, work)


def spectra_of(packs, traces_ref, table_ref):
    block, shots, samples = traces_ref.shape
    width = 2 * shots
    half = block // 2
    shot = lax.broadcasted_iota(jnp.int32, (1, shots, 2 * LANES), 1)
    lane = lax.broadcasted_iota(jnp.int32, (1, shots, 2 * LANES), 2)
    own = lane % shots == shot
    sides = [traces_ref[side * half : (side + 1) * half].reshape(half * shots, samples) for side in range(2)]
    terms = jnp.dot(jnp.concatenate(sides, axis=1), table_ref[...], preferred_element_type=jnp.float32)
    rows = jnp.sum(jnp.where(own, terms.reshape(half, shots, 2 * LANES), 0.0), axis=1)
    spectra = jnp.concatenate([rows[:, :LANES], rows[:, LANES:]], axis=0)
    short = block // packs
    column = lax.broadcasted_iota(jnp.int32, (short, LANES), 1)
    packed = spectra[:short]
    for part in range(1, packs):
        packed = jnp.where(column // width == part, spectra[part * short : (part + 1) * short], packed)
    return packed.astype(jnp.bfloat16)


def make_spectra(traces, place, n_row, packs, block):
    block_rows, shots, samples = traces.shape
    steps = block_rows // n_row // block
    short = block // packs
    columns = np.tile(np.repeat(dft_table(samples), shots, axis=1), (1, packs))
    table = jnp.asarray(np.block([[columns, 0 * columns], [0 * columns, columns]]))

    outs = pl.pallas_call(
        functools.partial(spectra_kernel, packs, n_row),
        in_specs=[SMEM, ANY, VMEM],
        out_specs=[VMEM] * n_row,
        out_shape=[jax.ShapeDtypeStruct((steps, short, LANES), jnp.bfloat16)] * n_row,
        scratch_shapes=[
            pltpu.VMEM((BUFFERS, block, shots, samples), jnp.bfloat16),
            pltpu.SemaphoreType.DMA((BUFFERS,)),
        ],
        compiler_params=params(48),
        cost_estimate=cost(2 * traces.size * LANES, 2 * traces.size),
        name="spectra",
    )(place, traces, table)
    return [out.reshape(steps * short, LANES) for out in outs]


def order_kernel(packs, n_src, place_ref, code_ref, *refs):
    pieces, out_refs = refs[: -n_src - 1], refs[-n_src:]
    width = LANES // packs
    held = jnp.concatenate([ref[...] for ref in pieces], axis=0)
    rolled = [held] + [
        pltpu.roll(held.astype(jnp.float32), turn * width, 1).astype(jnp.bfloat16) for turn in range(1, packs)
    ]
    table = jnp.concatenate(rolled, axis=1)
    depth = table.shape[0]
    slice_rows = code_ref.shape[0] // n_src
    short = slice_rows // packs
    column = lax.broadcasted_iota(jnp.int32, (short, LANES), 1)
    for turn, out_ref in enumerate(out_refs):
        first = pl.multiple_of((place_ref[1] ^ turn) * slice_rows, slice_rows)
        packed = None
        for part in range(packs):
            code = code_ref[pl.ds(pl.multiple_of(first + part * short, short), short), :]
            position, side = code // packs, code % packs
            hits = []
            for start in range(0, depth, LANES):
                hits.append(jnp.where(position == column + start, 1.0, 0.0).astype(jnp.bfloat16))
            chosen = jnp.concatenate(hits, axis=1)[:, :depth]
            rows = jnp.dot(chosen, table, preferred_element_type=jnp.float32)
            moved = rows[:, :LANES]
            for turned in range(1, packs):
                moved = jnp.where(
                    (part - side + packs) % packs == turned, rows[:, turned * LANES : (turned + 1) * LANES], moved
                )
            packed = moved if packed is None else jnp.where(column // width == part, moved, packed)
        out_ref[...] = packed.astype(jnp.bfloat16)


def make_order(code, pieces, place, n_src, packs, after):
    slice_rows = code.shape[0] // n_src
    return pl.pallas_call(
        functools.partial(order_kernel, packs, n_src),
        in_specs=[SMEM] + [VMEM] * (1 + len(pieces)) + [ANY],
        out_specs=[VMEM] * n_src,
        out_shape=[jax.ShapeDtypeStruct((slice_rows // packs, LANES), jnp.bfloat16)] * n_src,
        compiler_params=params(6),
        cost_estimate=cost(2 * code.shape[0] * len(pieces) * pieces[0].size * packs, 4 * code.size),
        name="order",
    )(place, code, *pieces, after)


def panel_kernel(packs, place_ref, *refs):
    pieces, panel_ref = refs[:-2], refs[-1]
    short = pieces[0].shape[0]
    width = LANES // packs
    shots = width // 2
    columns = panel_ref.shape[1]
    lane = lax.broadcasted_iota(jnp.int32, (LANES, packs * columns), 0)
    target = lax.broadcasted_iota(jnp.int32, (LANES, packs * columns), 1)
    total = None
    for turn, piece in enumerate(pieces):
        shot = (place_ref[1] ^ turn) * shots + lane % shots
        goes = lane // width * columns + lane % width // shots * (columns // 2) + shot
        chosen = jnp.where(target == goes, 1.0, 0.0).astype(jnp.bfloat16)
        term = jnp.dot(piece[...], chosen, preferred_element_type=jnp.float32)
        total = term if total is None else total + term
    for part in range(packs):
        panel_ref[part * short : (part + 1) * short, :] = total[:, part * columns : (part + 1) * columns].astype(
            jnp.bfloat16
        )


def make_panel(pieces, place, packs, after):
    rows = pieces[0].shape[0] * packs
    columns = len(pieces) * (LANES // packs)
    return pl.pallas_call(
        functools.partial(panel_kernel, packs),
        in_specs=[SMEM] + [VMEM] * len(pieces) + [ANY],
        out_specs=VMEM,
        out_shape=jax.ShapeDtypeStruct((rows, columns), jnp.bfloat16),
        compiler_params=params(4),
        cost_estimate=cost(2 * len(pieces) * rows * LANES * columns, 4 * rows * columns),
        name="panel",
    )(place, *pieces, after)


def relay_kernel(part, data_ref, after_ref, out_ref, token_ref, held, sems):
    token_ref[...] = jnp.zeros_like(token_ref)
    step_rows = held.shape[1]

    def source(step):
        return data_ref.at[part, pl.ds(pl.multiple_of(step * step_rows, step_rows), step_rows)]

    def work(step, data):
        rows = pl.ds(pl.multiple_of(step * step_rows, step_rows), step_rows)
        out_ref[:, rows, :] = jnp.swapaxes(data[...], 0, 1)

    streamed(data_ref.shape[1] // step_rows, source, held, sems, work)


def relay(slice_data, part, after):
    _, block_rows, blocks, offsets = slice_data.shape
    step_rows = min(block_rows, 128)
    return pl.pallas_call(
        functools.partial(relay_kernel, part),
        in_specs=[ANY, ANY],
        out_specs=[VMEM] * 2,
        out_shape=[
            jax.ShapeDtypeStruct((blocks, block_rows, offsets), jnp.bfloat16),
            jax.ShapeDtypeStruct((8, LANES), jnp.float32),
        ],
        scratch_shapes=[
            pltpu.VMEM((BUFFERS, step_rows, blocks, offsets), jnp.bfloat16),
            pltpu.SemaphoreType.DMA((BUFFERS,)),
        ],
        compiler_params=params(12),
        cost_estimate=cost(0, 2 * slice_data.size),
        name="relay",
    )(slice_data, after)


def terms_kernel(turns, n_pieces, place_ref, real_ref, imag_ref, *refs):
    pieces, out_refs = refs[:n_pieces], refs[-len(turns) :]
    columns = pieces[0].shape[1]
    kept = columns // 2
    for turn, out_ref in zip(turns, out_refs):
        size = out_ref.shape[0]
        rows = pl.ds(pl.multiple_of((place_ref[1] ^ turn) * size, size), size)
        total = jnp.zeros((2 * size, columns), jnp.float32)
        for number, piece in enumerate(pieces):
            block = place_ref[0] ^ number
            both = jnp.concatenate([real_ref[block, rows, :], imag_ref[block, rows, :]], axis=0)
            total += jnp.dot(both, piece[...], preferred_element_type=jnp.float32)
        by_real, by_imag = total[:size], total[size:]
        out_ref[:, :kept] = (by_real[:, :kept] - by_imag[:, kept:]).astype(out_ref.dtype)
        out_ref[:, kept:] = (by_real[:, kept:] + by_imag[:, :kept]).astype(out_ref.dtype)


def make_terms(real_data, imag_data, pieces, place, turns, slice_rows, after):
    depth = real_data.shape[0] * real_data.shape[2]
    columns = pieces[0].shape[1]
    rows = len(turns) * slice_rows
    return pl.pallas_call(
        functools.partial(terms_kernel, turns, len(pieces)),
        in_specs=[SMEM] + [VMEM] * (2 + len(pieces)) + [ANY] * len(after),
        out_specs=[VMEM] * len(turns),
        out_shape=[
            jax.ShapeDtypeStruct((slice_rows, columns), jnp.bfloat16 if turn else jnp.float32) for turn in turns
        ],
        compiler_params=params(8),
        cost_estimate=cost(4 * rows * depth * columns, 4 * rows * depth),
        name="terms",
    )(place, real_data, imag_data, *pieces, *after)


def update(wave_ref, own_ref, others, panel_ref):
    predicted = own_ref[...]
    for other in others:
        predicted += other[...].astype(jnp.float32)
    kept = predicted.shape[1] // 2
    turned = jnp.concatenate([-predicted[:, kept:], predicted[:, :kept]], axis=1)
    scaled = wave_ref[0] * predicted + wave_ref[1] * turned
    return predicted, panel_ref[...].astype(jnp.float32) - scaled


def estimate_kernel(wave_ref, own_ref, *refs):
    *others, panel_ref, out_ref = refs
    out_ref[...] = update(wave_ref, own_ref, others, panel_ref)[1].astype(jnp.bfloat16)


def last_kernel(wave_ref, own_ref, *refs):
    *others, panel_ref, multiples_ref, primaries_ref = refs
    predicted, primaries = update(wave_ref, own_ref, others, panel_ref)
    kept = predicted.shape[1] // 2
    multiples_ref[:, 0, :] = predicted[:, :kept]
    multiples_ref[:, 1, :] = predicted[:, kept:]
    primaries_ref[:, 0, :] = primaries[:, :kept]
    primaries_ref[:, 1, :] = primaries[:, kept:]


def make_update(wavelet, own, others, panel, last):
    rows, columns = panel.shape
    if last:
        shape = [jax.ShapeDtypeStruct((rows, 2, columns // 2), jnp.float32)] * 2
    else:
        shape = jax.ShapeDtypeStruct((rows, columns), jnp.bfloat16)
    return pl.pallas_call(
        last_kernel if last else estimate_kernel,
        in_specs=[SMEM] + [VMEM] * (2 + len(others)),
        out_specs=[VMEM] * 2 if last else VMEM,
        out_shape=shape,
        compiler_params=params(8),
        cost_estimate=cost(16 * rows * columns, 16 * rows * columns),
        name="update",
    )(wavelet, own, *others, panel)


def swap(array, axis, bits):
    size = lax.axis_size(axis)
    return lax.ppermute(array, axis, [(index, index ^ bits) for index in range(size)])


def spread(array, axis):
    size = lax.axis_size(axis)
    pieces = {0: array}
    for turn in range(2, size, 2):
        pieces[turn] = swap(array, axis, turn)
    for turn in range(0, size, 2):
        pieces[turn + 1] = swap(pieces[turn], axis, 1)
    return [pieces[turn] for turn in range(size)]


def body(traces, row_source, slice_data, wavelet_inverse):
    block_rows, shots, _ = traces.shape
    n_row, n_src = lax.axis_size("row"), lax.axis_size("src")
    row, src = lax.axis_index("row"), lax.axis_index("src")
    place = jnp.stack([row, src]).astype(jnp.int32)
    packs = LANES // (2 * shots)
    group_rows = block_rows // n_row
    slice_rows = block_rows // n_src
    block = min(group_rows, 128)
    short = block // packs

    spectra = make_spectra(traces, place, n_row, packs, block)
    arrived = [spectra[0]] + [swap(spectra[turn], "row", turn) for turn in range(1, n_row)]

    inside = row_source % group_rows
    position = (row_source // block_rows ^ row) * (group_rows // packs) + inside // block * short + inside % short
    code = position * packs + inside % block // short
    code = jnp.broadcast_to(code[:, None], (block_rows, LANES))
    real_data, real_token = relay(slice_data, 0, spectra[0])
    ordered = make_order(code, arrived, place, n_src, packs, real_token)
    located = [ordered[0]] + [swap(ordered[turn], "src", turn) for turn in range(1, n_src)]
    imag_data, imag_token = relay(slice_data, 1, ordered[0])
    panel = make_panel(located, place, packs, imag_token)

    half = n_src // 2
    estimate = panel
    for iteration in range(ITERS):
        pieces = spread(estimate, "row")
        arriving, after = [], []
        for turn in range(n_src - 1, half - 1, -1):
            after = make_terms(real_data, imag_data, pieces, place, (turn,), slice_rows, [])
            arriving.append(swap(after[0], "src", turn))
        near = tuple(range(half - 1, -1, -1))
        terms = make_terms(real_data, imag_data, pieces, place, near, slice_rows, [])
        arriving += [swap(part, "src", turn) for turn, part in zip(near[:-1], terms)]
        estimate = make_update(wavelet_inverse, terms[-1], arriving, panel, iteration == ITERS - 1)
    return tuple(estimate)


def solution(mesh):
    in_specs = (P("row", "src", None), P("row"), P(None, "row", None, "src"), P())
    out_specs = (P(("row", "src"), None, None), P(("row", "src"), None, None))
    return jax.shard_map(body, mesh=mesh, in_specs=in_specs, out_specs=out_specs, check_vma=False)
```

```python
import functools

import jax
import jax.numpy as jnp
import ml_dtypes
import numpy as np
from jax import lax
from jax.experimental import pallas as pl
from jax.experimental.pallas import tpu as pltpu
from jax.sharding import PartitionSpec as P

FREQ = 61
ITERS = 3
LANES = 128
BUFFERS = 4
VMEM = pl.BlockSpec(memory_space=pltpu.VMEM)
ANY = pl.BlockSpec(memory_space=pl.ANY)
SMEM = pl.BlockSpec(memory_space=pltpu.SMEM)


def dft_table(samples):
    ticks = np.arange(samples, dtype=np.int32)
    moment = ticks.astype(np.float32)
    ramp_len = samples // 8
    pi = np.float32(np.pi)
    half = np.float32(0.5)
    rising = half - half * np.cos(pi * (moment + half) / np.float32(ramp_len))
    falling = half - half * np.cos(pi * (np.float32(samples) - moment - half) / np.float32(ramp_len))
    taper = np.where(
        ticks < ramp_len, rising, np.where(ticks >= samples - ramp_len, falling, np.ones_like(rising))
    )
    wrapped = ticks * FREQ % samples
    angles = np.float32(2.0 * np.pi / samples) * wrapped.astype(np.float32)
    factor = np.float32(1.0) / np.sqrt(np.float32(samples))
    table = np.stack([taper * np.cos(angles) * factor, -taper * np.sin(angles) * factor], axis=1)
    return table.astype(ml_dtypes.bfloat16)


def params(megabytes):
    return pltpu.CompilerParams(vmem_limit_bytes=megabytes * 2**20)


def cost(flops, moved):
    return pl.CostEstimate(flops=int(flops), bytes_accessed=int(moved), transcendentals=0)


def streamed(steps, source, held, sems, work):
    slots = held.shape[0]

    def copy(step):
        slot = step % slots
        return pltpu.make_async_copy(source(step), held.at[slot], sems.at[slot])

    for step in range(min(slots - 1, steps)):
        copy(step).start()

    @pl.loop(0, steps)
    def _(step):
        @pl.when(step + slots - 1 < steps)
        def _():
            copy(step + slots - 1).start()

        copy(step).wait()
        work(step, held.at[step % slots])


def spectra_kernel(packs, n_row, place_ref, traces_ref, table_ref, *refs):
    out_refs, held, sems = refs[:n_row], refs[n_row], refs[n_row + 1]
    block = held.shape[1]
    steps = traces_ref.shape[0] // n_row // block

    def source(step):
        first = ((place_ref[0] ^ (step // steps)) * steps + step % steps) * block
        return traces_ref.at[pl.ds(pl.multiple_of(first, block), block)]

    def work(step, traces):
        packed = spectra_of(packs, traces, table_ref)
        for turn, out_ref in enumerate(out_refs):

            @pl.when(step // steps == turn)
            def _():
                out_ref[step % steps] = packed

    streamed(n_row * steps, source, held, sems, work)


def spectra_of(packs, traces_ref, table_ref):
    block, shots, samples = traces_ref.shape
    width = 2 * shots
    half = block // 2
    shot = lax.broadcasted_iota(jnp.int32, (1, shots, 2 * LANES), 1)
    lane = lax.broadcasted_iota(jnp.int32, (1, shots, 2 * LANES), 2)
    own = lane % shots == shot
    sides = [traces_ref[side * half : (side + 1) * half].reshape(half * shots, samples) for side in range(2)]
    terms = jnp.dot(jnp.concatenate(sides, axis=1), table_ref[...], preferred_element_type=jnp.float32)
    rows = jnp.sum(jnp.where(own, terms.reshape(half, shots, 2 * LANES), 0.0), axis=1)
    spectra = jnp.concatenate([rows[:, :LANES], rows[:, LANES:]], axis=0)
    short = block // packs
    column = lax.broadcasted_iota(jnp.int32, (short, LANES), 1)
    packed = spectra[:short]
    for part in range(1, packs):
        packed = jnp.where(column // width == part, spectra[part * short : (part + 1) * short], packed)
    return packed.astype(jnp.bfloat16)


def make_spectra(traces, place, n_row, packs, block):
    block_rows, shots, samples = traces.shape
    steps = block_rows // n_row // block
    short = block // packs
    columns = np.tile(np.repeat(dft_table(samples), shots, axis=1), (1, packs))
    table = jnp.asarray(np.block([[columns, 0 * columns], [0 * columns, columns]]))

    outs = pl.pallas_call(
        functools.partial(spectra_kernel, packs, n_row),
        in_specs=[SMEM, ANY, VMEM],
        out_specs=[VMEM] * n_row,
        out_shape=[jax.ShapeDtypeStruct((steps, short, LANES), jnp.bfloat16)] * n_row,
        scratch_shapes=[
            pltpu.VMEM((BUFFERS, block, shots, samples), jnp.bfloat16),
            pltpu.SemaphoreType.DMA((BUFFERS,)),
        ],
        compiler_params=params(48),
        cost_estimate=cost(2 * traces.size * LANES, 2 * traces.size),
        name="spectra",
    )(place, traces, table)
    return [out.reshape(steps * short, LANES) for out in outs]


def order_kernel(packs, n_src, place_ref, code_ref, *refs):
    pieces, out_refs = refs[:-n_src], refs[-n_src:]
    width = LANES // packs
    held = jnp.concatenate([ref[...] for ref in pieces], axis=0)
    rolled = [held] + [
        pltpu.roll(held.astype(jnp.float32), turn * width, 1).astype(jnp.bfloat16) for turn in range(1, packs)
    ]
    table = jnp.concatenate(rolled, axis=1)
    depth = table.shape[0]
    slice_rows = code_ref.shape[0] // n_src
    short = slice_rows // packs
    column = lax.broadcasted_iota(jnp.int32, (short, LANES), 1)
    for turn, out_ref in enumerate(out_refs):
        first = pl.multiple_of((place_ref[1] ^ turn) * slice_rows, slice_rows)
        packed = None
        for part in range(packs):
            code = code_ref[pl.ds(pl.multiple_of(first + part * short, short), short), :]
            position, side = code // packs, code % packs
            hits = []
            for start in range(0, depth, LANES):
                hits.append(jnp.where(position == column + start, 1.0, 0.0).astype(jnp.bfloat16))
            chosen = jnp.concatenate(hits, axis=1)[:, :depth]
            rows = jnp.dot(chosen, table, preferred_element_type=jnp.float32)
            moved = rows[:, :LANES]
            for turned in range(1, packs):
                moved = jnp.where(
                    (part - side + packs) % packs == turned, rows[:, turned * LANES : (turned + 1) * LANES], moved
                )
            packed = moved if packed is None else jnp.where(column // width == part, moved, packed)
        out_ref[...] = packed.astype(jnp.bfloat16)


def make_order(code, pieces, place, n_src, packs):
    slice_rows = code.shape[0] // n_src
    return pl.pallas_call(
        functools.partial(order_kernel, packs, n_src),
        in_specs=[SMEM] + [VMEM] * (1 + len(pieces)),
        out_specs=[VMEM] * n_src,
        out_shape=[jax.ShapeDtypeStruct((slice_rows // packs, LANES), jnp.bfloat16)] * n_src,
        compiler_params=params(8),
        cost_estimate=cost(2 * code.shape[0] * len(pieces) * pieces[0].size * packs, 4 * code.size),
        name="order",
    )(place, code, *pieces)


def panel_kernel(packs, place_ref, *refs):
    pieces, panel_ref = refs[:-2], refs[-1]
    short = pieces[0].shape[0]
    width = LANES // packs
    shots = width // 2
    columns = panel_ref.shape[1]
    lane = lax.broadcasted_iota(jnp.int32, (LANES, packs * columns), 0)
    target = lax.broadcasted_iota(jnp.int32, (LANES, packs * columns), 1)
    total = None
    for turn, piece in enumerate(pieces):
        shot = (place_ref[1] ^ turn) * shots + lane % shots
        goes = lane // width * columns + lane % width // shots * (columns // 2) + shot
        chosen = jnp.where(target == goes, 1.0, 0.0).astype(jnp.bfloat16)
        term = jnp.dot(piece[...], chosen, preferred_element_type=jnp.float32)
        total = term if total is None else total + term
    for part in range(packs):
        panel_ref[part * short : (part + 1) * short, :] = total[:, part * columns : (part + 1) * columns].astype(
            jnp.bfloat16
        )


def make_panel(pieces, place, packs, after):
    rows = pieces[0].shape[0] * packs
    columns = len(pieces) * (LANES // packs)
    return pl.pallas_call(
        functools.partial(panel_kernel, packs),
        in_specs=[SMEM] + [VMEM] * len(pieces) + [ANY],
        out_specs=VMEM,
        out_shape=jax.ShapeDtypeStruct((rows, columns), jnp.bfloat16),
        compiler_params=params(8),
        cost_estimate=cost(2 * len(pieces) * rows * LANES * columns, 4 * rows * columns),
        name="panel",
    )(place, *pieces, after)


def relay_kernel(part, data_ref, after_ref, out_ref, token_ref, held, sems):
    token_ref[...] = jnp.zeros_like(token_ref)
    step_rows = held.shape[1]

    def source(step):
        return data_ref.at[part, pl.ds(pl.multiple_of(step * step_rows, step_rows), step_rows)]

    def work(step, data):
        rows = pl.ds(pl.multiple_of(step * step_rows, step_rows), step_rows)
        out_ref[:, rows, :] = jnp.swapaxes(data[...], 0, 1)

    streamed(data_ref.shape[1] // step_rows, source, held, sems, work)


def relay(slice_data, part, after):
    _, block_rows, blocks, offsets = slice_data.shape
    step_rows = min(block_rows, 128)
    return pl.pallas_call(
        functools.partial(relay_kernel, part),
        in_specs=[ANY, ANY],
        out_specs=[VMEM] * 2,
        out_shape=[
            jax.ShapeDtypeStruct((blocks, block_rows, offsets), jnp.bfloat16),
            jax.ShapeDtypeStruct((8, LANES), jnp.float32),
        ],
        scratch_shapes=[
            pltpu.VMEM((BUFFERS, step_rows, blocks, offsets), jnp.bfloat16),
            pltpu.SemaphoreType.DMA((BUFFERS,)),
        ],
        compiler_params=params(12),
        cost_estimate=cost(0, 2 * slice_data.size),
        name="relay",
    )(slice_data, after)


def terms_kernel(turn, n_pieces, place_ref, real_ref, imag_ref, *refs):
    pieces, out_refs = refs[:n_pieces], refs[n_pieces:]
    columns = pieces[0].shape[1]
    kept = columns // 2
    size = out_refs[0].shape[0]
    rows = pl.ds(pl.multiple_of((place_ref[1] ^ turn) * size, size), size)
    total = jnp.zeros((2 * size, columns), jnp.float32)
    for number, piece in enumerate(pieces):
        block = place_ref[0] ^ number
        both = jnp.concatenate([real_ref[block, rows, :], imag_ref[block, rows, :]], axis=0)
        total += jnp.dot(both, piece[...], preferred_element_type=jnp.float32)
    by_real, by_imag = total[:size], total[size:]
    for out_ref in out_refs:
        out_ref[:, :kept] = (by_real[:, :kept] - by_imag[:, kept:]).astype(out_ref.dtype)
        out_ref[:, kept:] = (by_real[:, kept:] + by_imag[:, :kept]).astype(out_ref.dtype)


def make_terms(real_data, imag_data, pieces, place, turn, slice_rows, types):
    depth = real_data.shape[0] * real_data.shape[2]
    columns = pieces[0].shape[1]
    return pl.pallas_call(
        functools.partial(terms_kernel, turn, len(pieces)),
        in_specs=[SMEM] + [VMEM] * (2 + len(pieces)),
        out_specs=[VMEM] * len(types),
        out_shape=[jax.ShapeDtypeStruct((slice_rows, columns), kind) for kind in types],
        compiler_params=params(8),
        cost_estimate=cost(4 * slice_rows * depth * columns, 4 * slice_rows * depth),
        name="terms",
    )(place, real_data, imag_data, *pieces)


def add_kernel(own_ref, other_ref, out_ref):
    out_ref[...] = (own_ref[...] + other_ref[...].astype(jnp.float32)).astype(out_ref.dtype)


def make_sum(own, other):
    return pl.pallas_call(
        add_kernel,
        in_specs=[VMEM] * 2,
        out_specs=VMEM,
        out_shape=jax.ShapeDtypeStruct(other.shape, other.dtype),
        compiler_params=params(8),
        cost_estimate=cost(other.size, 8 * other.size),
        name="sum",
    )(own, other)


def pick_kernel(place_ref, even_ref, odd_ref, *refs):
    out_ref = refs[-1]

    @pl.when(place_ref[0] % 2 == 0)
    def _():
        out_ref[...] = even_ref[...]

    @pl.when(place_ref[0] % 2 == 1)
    def _():
        out_ref[...] = odd_ref[...]


def make_pick(place, even, odd, after):
    return pl.pallas_call(
        pick_kernel,
        in_specs=[SMEM] + [VMEM] * 2 + [ANY] * len(after),
        out_specs=VMEM,
        out_shape=jax.ShapeDtypeStruct(even.shape, even.dtype),
        compiler_params=params(8),
        cost_estimate=cost(0, 4 * even.size),
        name="pick",
    )(place, even, odd, *after)


def update(place_ref, wave_ref, own_ref, others, panel_ref, folded):
    predicted = own_ref[...]
    for number, other in enumerate(others):
        term = other[...].astype(jnp.float32)
        if folded and number == 0:
            inner = place_ref[1] % 2 != place_ref[1] // 2 % 2
            term = jnp.where(inner, 0.0, term)
        predicted += term
    kept = predicted.shape[1] // 2
    turned = jnp.concatenate([-predicted[:, kept:], predicted[:, :kept]], axis=1)
    scaled = wave_ref[0] * predicted + wave_ref[1] * turned
    return predicted, panel_ref[...].astype(jnp.float32) - scaled


def estimate_kernel(folded, place_ref, wave_ref, own_ref, *refs):
    *others, panel_ref, out_ref = refs
    primaries = update(place_ref, wave_ref, own_ref, others, panel_ref, folded)[1]
    out_ref[...] = primaries.astype(jnp.bfloat16)


def last_kernel(folded, place_ref, wave_ref, own_ref, *refs):
    *others, panel_ref, multiples_ref, primaries_ref = refs
    predicted, primaries = update(place_ref, wave_ref, own_ref, others, panel_ref, folded)
    kept = predicted.shape[1] // 2
    multiples_ref[:, 0, :] = predicted[:, :kept]
    multiples_ref[:, 1, :] = predicted[:, kept:]
    primaries_ref[:, 0, :] = primaries[:, :kept]
    primaries_ref[:, 1, :] = primaries[:, kept:]


def make_update(place, wavelet, own, others, panel, folded, last):
    rows, columns = panel.shape
    if last:
        shape = [jax.ShapeDtypeStruct((rows, 2, columns // 2), jnp.float32)] * 2
    else:
        shape = jax.ShapeDtypeStruct((rows, columns), jnp.bfloat16)
    return pl.pallas_call(
        functools.partial(last_kernel if last else estimate_kernel, folded),
        in_specs=[SMEM] * 2 + [VMEM] * (2 + len(others)),
        out_specs=[VMEM] * 2 if last else VMEM,
        out_shape=shape,
        compiler_params=params(8),
        cost_estimate=cost(16 * rows * columns, 16 * rows * columns),
        name="update",
    )(place, wavelet, own, *others, panel)


def swap(array, axis, bits):
    size = lax.axis_size(axis)
    return lax.ppermute(array, axis, [(index, index ^ bits) for index in range(size)])


def spread(array, place, after):
    size = lax.axis_size("row")
    pieces = {0: array}
    turns = sorted(range(2, size, 2), key=lambda turn: (turn.bit_count(), turn))
    for turn in turns:
        high, low = 1 << turn.bit_length() - 1, turn & -turn
        if high == low:
            pieces[turn] = swap(array, "row", turn)
            continue
        chosen = make_pick(place, pieces[turn ^ high], pieces[turn ^ low], after)
        pairs = [(index, index ^ (low if index % 2 else high)) for index in range(size)]
        pieces[turn] = lax.ppermute(chosen, "row", pairs)
    for turn in range(0, size, 2):
        pieces[turn + 1] = swap(pieces[turn], "row", 1)
    return [pieces[turn] for turn in range(size)]


def exchange(make, n_src):
    bf16, f32 = jnp.bfloat16, jnp.float32
    if n_src != 4:
        arriving = [swap(make(turn, [bf16])[0], "src", turn) for turn in range(n_src - 1, 0, -1)]
        return make(0, [f32])[0], arriving, False
    first = lax.ppermute(make(2, [bf16])[0], "src", [(0, 1), (1, 3), (3, 2), (2, 0)])
    sent, kept = make(3, [bf16, f32])
    near = make(1, [bf16])[0]
    beside = swap(near, "src", 1)
    outer = lax.ppermute(sent, "src", [(0, 3), (3, 0)])
    inner = lax.ppermute(make_sum(kept, first), "src", [(1, 2), (2, 1)])
    return make(0, [f32])[0], [first, beside, outer, inner], True


def body(traces, row_source, slice_data, wavelet_inverse):
    block_rows, shots, _ = traces.shape
    n_row, n_src = lax.axis_size("row"), lax.axis_size("src")
    row, src = lax.axis_index("row"), lax.axis_index("src")
    place = jnp.stack([row, src]).astype(jnp.int32)
    packs = LANES // (2 * shots)
    group_rows = block_rows // n_row
    slice_rows = block_rows // n_src
    block = min(group_rows, 128)
    short = block // packs

    spectra = make_spectra(traces, place, n_row, packs, block)
    arrived = [spectra[0]] + [swap(spectra[turn], "row", turn) for turn in range(1, n_row)]

    inside = row_source % group_rows
    position = (row_source // block_rows ^ row) * (group_rows // packs) + inside // block * short + inside % short
    code = position * packs + inside % block // short
    code = jnp.broadcast_to(code[:, None], (block_rows, LANES))
    real_data, real_token = relay(slice_data, 0, spectra[0])
    ordered = make_order(code, arrived, place, n_src, packs)
    located = [ordered[0]] + [swap(ordered[turn], "src", turn) for turn in range(1, n_src)]
    imag_data, token = relay(slice_data, 1, ordered[0])
    panel = make_panel(located, place, packs, token)

    estimate, after = panel, [real_token]
    for iteration in range(ITERS):
        pieces = spread(estimate, place, after)
        after = []
        own, arriving, folded = exchange(
            lambda turn, types: make_terms(real_data, imag_data, pieces, place, turn, slice_rows, types), n_src
        )
        estimate = make_update(place, wavelet_inverse, own, arriving, panel, folded, iteration == ITERS - 1)
    return tuple(estimate)


def solution(mesh):
    in_specs = (P("row", "src", None), P("row"), P(None, "row", None, "src"), P())
    out_specs = (P(("row", "src"), None, None), P(("row", "src"), None, None))
    return jax.shard_map(body, mesh=mesh, in_specs=in_specs, out_specs=out_specs, check_vma=False)
```

```python
import functools

import jax
import jax.numpy as jnp
import ml_dtypes
import numpy as np
from jax import lax
from jax.experimental import pallas as pl
from jax.experimental.pallas import tpu as pltpu
from jax.sharding import PartitionSpec as P

FREQ = 61
ITERS = 3
LANES = 128
BUFFERS = 4
VMEM = pl.BlockSpec(memory_space=pltpu.VMEM)
ANY = pl.BlockSpec(memory_space=pl.ANY)
SMEM = pl.BlockSpec(memory_space=pltpu.SMEM)


def dft_table(samples):
    ticks = np.arange(samples, dtype=np.int32)
    moment = ticks.astype(np.float32)
    ramp_len = samples // 8
    pi = np.float32(np.pi)
    half = np.float32(0.5)
    rising = half - half * np.cos(pi * (moment + half) / np.float32(ramp_len))
    falling = half - half * np.cos(pi * (np.float32(samples) - moment - half) / np.float32(ramp_len))
    taper = np.where(
        ticks < ramp_len, rising, np.where(ticks >= samples - ramp_len, falling, np.ones_like(rising))
    )
    wrapped = ticks * FREQ % samples
    angles = np.float32(2.0 * np.pi / samples) * wrapped.astype(np.float32)
    factor = np.float32(1.0) / np.sqrt(np.float32(samples))
    table = np.stack([taper * np.cos(angles) * factor, -taper * np.sin(angles) * factor], axis=1)
    return table.astype(ml_dtypes.bfloat16)


def params(megabytes):
    return pltpu.CompilerParams(vmem_limit_bytes=megabytes * 2**20)


def cost(flops, moved):
    return pl.CostEstimate(flops=int(flops), bytes_accessed=int(moved), transcendentals=0)


def streamed(steps, source, held, sems, work, ready=None):
    slots = held.shape[0]

    def copy(step):
        slot = step % slots
        return pltpu.make_async_copy(source(step), held.at[slot], sems.at[slot])

    for step in range(min(slots - 1, steps)):
        copy(step).start()
    if ready is not None:
        ready()

    @pl.loop(0, steps)
    def _(step):
        @pl.when(step + slots - 1 < steps)
        def _():
            copy(step + slots - 1).start()

        copy(step).wait()
        work(step, held.at[step % slots])


def spectra_kernel(packs, n_row, place_ref, traces_ref, table_ref, *refs):
    out_refs = refs[:n_row]
    held, sems, table, table_sem = refs[n_row:]
    block = held.shape[1]
    steps = traces_ref.shape[0] // n_row // block

    def source(step):
        first = ((place_ref[0] ^ (step // steps)) * steps + step % steps) * block
        return traces_ref.at[pl.ds(pl.multiple_of(first, block), block)]

    def work(step, traces):
        packed = spectra_of(packs, traces, table)
        for turn, out_ref in enumerate(out_refs):

            @pl.when(step // steps == turn)
            def _():
                out_ref[step % steps] = packed

    def ready():
        copy = pltpu.make_async_copy(table_ref, table, table_sem)
        copy.start()
        copy.wait()

    streamed(n_row * steps, source, held, sems, work, ready)


def spectra_of(packs, traces_ref, table_ref):
    block, shots, samples = traces_ref.shape
    width = 2 * shots
    half = block // 2
    shot = lax.broadcasted_iota(jnp.int32, (1, shots, 2 * LANES), 1)
    lane = lax.broadcasted_iota(jnp.int32, (1, shots, 2 * LANES), 2)
    own = lane % shots == shot
    sides = [traces_ref[side * half : (side + 1) * half].reshape(half * shots, samples) for side in range(2)]
    terms = jnp.dot(jnp.concatenate(sides, axis=1), table_ref[...], preferred_element_type=jnp.float32)
    rows = jnp.sum(jnp.where(own, terms.reshape(half, shots, 2 * LANES), 0.0), axis=1)
    spectra = jnp.concatenate([rows[:, :LANES], rows[:, LANES:]], axis=0)
    short = block // packs
    column = lax.broadcasted_iota(jnp.int32, (short, LANES), 1)
    packed = spectra[:short]
    for part in range(1, packs):
        packed = jnp.where(column // width == part, spectra[part * short : (part + 1) * short], packed)
    return packed.astype(jnp.bfloat16)


def make_spectra(traces, place, n_row, packs, block):
    block_rows, shots, samples = traces.shape
    steps = block_rows // n_row // block
    short = block // packs
    columns = np.tile(np.repeat(dft_table(samples), shots, axis=1), (1, packs))
    table = jnp.asarray(np.block([[columns, 0 * columns], [0 * columns, columns]]))

    outs = pl.pallas_call(
        functools.partial(spectra_kernel, packs, n_row),
        in_specs=[SMEM, ANY, ANY],
        out_specs=[VMEM] * n_row,
        out_shape=[jax.ShapeDtypeStruct((steps, short, LANES), jnp.bfloat16)] * n_row,
        scratch_shapes=[
            pltpu.VMEM((2 * BUFFERS, block, shots, samples), jnp.bfloat16),
            pltpu.SemaphoreType.DMA((2 * BUFFERS,)),
            pltpu.VMEM(table.shape, table.dtype),
            pltpu.SemaphoreType.DMA,
        ],
        compiler_params=params(48),
        cost_estimate=cost(2 * traces.size * LANES, 2 * traces.size),
        name="spectra",
    )(place, traces, table)
    return [out.reshape(steps * short, LANES) for out in outs]


def order_kernel(packs, n_src, place_ref, code_ref, *refs):
    pieces, out_refs = refs[:-n_src], refs[-n_src:]
    width = LANES // packs
    held = jnp.concatenate([ref[...] for ref in pieces], axis=0)
    rolled = [held] + [
        pltpu.roll(held.astype(jnp.float32), turn * width, 1).astype(jnp.bfloat16) for turn in range(1, packs)
    ]
    table = jnp.concatenate(rolled, axis=1)
    depth = table.shape[0]
    slice_rows = code_ref.shape[0] // n_src
    short = slice_rows // packs
    column = lax.broadcasted_iota(jnp.int32, (short, LANES), 1)
    for turn, out_ref in enumerate(out_refs):
        first = pl.multiple_of((place_ref[1] ^ turn) * slice_rows, slice_rows)
        packed = None
        for part in range(packs):
            code = code_ref[pl.ds(pl.multiple_of(first + part * short, short), short), :]
            position, side = code // packs, code % packs
            hits = []
            for start in range(0, depth, LANES):
                hits.append(jnp.where(position == column + start, 1.0, 0.0).astype(jnp.bfloat16))
            chosen = jnp.concatenate(hits, axis=1)[:, :depth]
            rows = jnp.dot(chosen, table, preferred_element_type=jnp.float32)
            moved = rows[:, :LANES]
            for turned in range(1, packs):
                moved = jnp.where(
                    (part - side + packs) % packs == turned, rows[:, turned * LANES : (turned + 1) * LANES], moved
                )
            packed = moved if packed is None else jnp.where(column // width == part, moved, packed)
        out_ref[...] = packed.astype(jnp.bfloat16)


def make_order(code, pieces, place, n_src, packs):
    slice_rows = code.shape[0] // n_src
    return pl.pallas_call(
        functools.partial(order_kernel, packs, n_src),
        in_specs=[SMEM] + [VMEM] * (1 + len(pieces)),
        out_specs=[VMEM] * n_src,
        out_shape=[jax.ShapeDtypeStruct((slice_rows // packs, LANES), jnp.bfloat16)] * n_src,
        compiler_params=params(8),
        cost_estimate=cost(2 * code.shape[0] * len(pieces) * pieces[0].size * packs, 4 * code.size),
        name="order",
    )(place, code, *pieces)


def panel_kernel(packs, place_ref, *refs):
    pieces, panel_ref = refs[:-2], refs[-1]
    short = pieces[0].shape[0]
    width = LANES // packs
    shots = width // 2
    columns = panel_ref.shape[1]
    lane = lax.broadcasted_iota(jnp.int32, (LANES, packs * columns), 0)
    target = lax.broadcasted_iota(jnp.int32, (LANES, packs * columns), 1)
    total = None
    for turn, piece in enumerate(pieces):
        shot = (place_ref[1] ^ turn) * shots + lane % shots
        goes = lane // width * columns + lane % width // shots * (columns // 2) + shot
        chosen = jnp.where(target == goes, 1.0, 0.0).astype(jnp.bfloat16)
        term = jnp.dot(piece[...], chosen, preferred_element_type=jnp.float32)
        total = term if total is None else total + term
    for part in range(packs):
        panel_ref[part * short : (part + 1) * short, :] = total[:, part * columns : (part + 1) * columns].astype(
            jnp.bfloat16
        )


def make_panel(pieces, place, packs, after):
    rows = pieces[0].shape[0] * packs
    columns = len(pieces) * (LANES // packs)
    return pl.pallas_call(
        functools.partial(panel_kernel, packs),
        in_specs=[SMEM] + [VMEM] * len(pieces) + [ANY],
        out_specs=VMEM,
        out_shape=jax.ShapeDtypeStruct((rows, columns), jnp.bfloat16),
        compiler_params=params(8),
        cost_estimate=cost(2 * len(pieces) * rows * LANES * columns, 4 * rows * columns),
        name="panel",
    )(place, *pieces, after)


def relay_kernel(part, data_ref, after_ref, out_ref, token_ref, held, sems):
    token_ref[...] = jnp.zeros_like(token_ref)
    step_rows = held.shape[1]

    def source(step):
        return data_ref.at[part, pl.ds(pl.multiple_of(step * step_rows, step_rows), step_rows)]

    def work(step, data):
        rows = pl.ds(pl.multiple_of(step * step_rows, step_rows), step_rows)
        out_ref[:, rows, :] = jnp.swapaxes(data[...], 0, 1)

    streamed(data_ref.shape[1] // step_rows, source, held, sems, work)


def relay(slice_data, part, after):
    _, block_rows, blocks, offsets = slice_data.shape
    step_rows = min(block_rows, 128)
    return pl.pallas_call(
        functools.partial(relay_kernel, part),
        in_specs=[ANY, ANY],
        out_specs=[VMEM] * 2,
        out_shape=[
            jax.ShapeDtypeStruct((blocks, block_rows, offsets), jnp.bfloat16),
            jax.ShapeDtypeStruct((8, LANES), jnp.float32),
        ],
        scratch_shapes=[
            pltpu.VMEM((BUFFERS, step_rows, blocks, offsets), jnp.bfloat16),
            pltpu.SemaphoreType.DMA((BUFFERS,)),
        ],
        compiler_params=params(12),
        cost_estimate=cost(0, 2 * slice_data.size),
        name="relay",
    )(slice_data, after)


def terms_kernel(turns, numbers, begun, place_ref, real_ref, imag_ref, *refs):
    pieces = refs[: len(numbers)]
    partial = refs[len(numbers) : len(numbers) + begun]
    out_refs = refs[len(numbers) + begun :]
    columns = pieces[0].shape[1]
    kept = columns // 2
    size = out_refs[0].shape[0]
    each = len(out_refs) // len(turns)
    for index, turn in enumerate(turns):
        rows = pl.ds(pl.multiple_of((place_ref[1] ^ turn) * size, size), size)
        total = jnp.zeros((2 * size, columns), jnp.float32)
        for number, piece in zip(numbers, pieces):
            block = place_ref[0] ^ number
            both = jnp.concatenate([real_ref[block, rows, :], imag_ref[block, rows, :]], axis=0)
            total += jnp.dot(both, piece[...], preferred_element_type=jnp.float32)
        by_real, by_imag = total[:size], total[size:]
        real = by_real[:, :kept] - by_imag[:, kept:]
        imag = by_real[:, kept:] + by_imag[:, :kept]
        if begun:
            real += partial[index][:, :kept]
            imag += partial[index][:, kept:]
        for out_ref in out_refs[index * each : (index + 1) * each]:
            out_ref[:, :kept] = real.astype(out_ref.dtype)
            out_ref[:, kept:] = imag.astype(out_ref.dtype)


def make_terms(data, place, pieces, turns, partial, slice_rows, types):
    real_data, imag_data = data
    numbers = tuple(pieces)
    offsets, columns = pieces[numbers[0]].shape
    size = len(turns) * slice_rows * len(numbers) * offsets
    return pl.pallas_call(
        functools.partial(terms_kernel, turns, numbers, len(partial)),
        in_specs=[SMEM] + [VMEM] * (2 + len(numbers) + len(partial)),
        out_specs=[VMEM] * len(types) * len(turns),
        out_shape=[jax.ShapeDtypeStruct((slice_rows, columns), kind) for kind in types] * len(turns),
        compiler_params=params(8),
        cost_estimate=cost(4 * size * columns, 4 * size),
        name="terms",
    )(place, real_data, imag_data, *pieces.values(), *partial)


def add_kernel(own_ref, other_ref, out_ref):
    out_ref[...] = (own_ref[...] + other_ref[...].astype(jnp.float32)).astype(out_ref.dtype)


def make_sum(own, other):
    return pl.pallas_call(
        add_kernel,
        in_specs=[VMEM] * 2,
        out_specs=VMEM,
        out_shape=jax.ShapeDtypeStruct(other.shape, other.dtype),
        compiler_params=params(8),
        cost_estimate=cost(other.size, 8 * other.size),
        name="sum",
    )(own, other)


def update(place_ref, wave_ref, own_ref, others, panel_ref, folded):
    predicted = own_ref[...]
    for number, other in enumerate(others):
        term = other[...].astype(jnp.float32)
        if folded and number == 0:
            inner = place_ref[1] % 2 != place_ref[1] // 2 % 2
            term = jnp.where(inner, 0.0, term)
        predicted += term
    kept = predicted.shape[1] // 2
    turned = jnp.concatenate([-predicted[:, kept:], predicted[:, :kept]], axis=1)
    scaled = wave_ref[0] * predicted + wave_ref[1] * turned
    return predicted, panel_ref[...].astype(jnp.float32) - scaled


def estimate_kernel(folded, place_ref, wave_ref, own_ref, *refs):
    *others, panel_ref, out_ref = refs
    primaries = update(place_ref, wave_ref, own_ref, others, panel_ref, folded)[1]
    out_ref[...] = primaries.astype(jnp.bfloat16)


def last_kernel(folded, place_ref, wave_ref, own_ref, *refs):
    *others, panel_ref, multiples_ref, primaries_ref = refs
    predicted, primaries = update(place_ref, wave_ref, own_ref, others, panel_ref, folded)
    kept = predicted.shape[1] // 2
    multiples_ref[:, 0, :] = predicted[:, :kept]
    multiples_ref[:, 1, :] = predicted[:, kept:]
    primaries_ref[:, 0, :] = primaries[:, :kept]
    primaries_ref[:, 1, :] = primaries[:, kept:]


def make_update(place, wavelet, own, others, panel, folded, last):
    rows, columns = panel.shape
    if last:
        shape = [jax.ShapeDtypeStruct((rows, 2, columns // 2), jnp.float32)] * 2
    else:
        shape = jax.ShapeDtypeStruct((rows, columns), jnp.bfloat16)
    return pl.pallas_call(
        functools.partial(last_kernel if last else estimate_kernel, folded),
        in_specs=[SMEM] * 2 + [VMEM] * (2 + len(others)),
        out_specs=[VMEM] * 2 if last else VMEM,
        out_shape=shape,
        compiler_params=params(8),
        cost_estimate=cost(16 * rows * columns, 16 * rows * columns),
        name="update",
    )(place, wavelet, own, *others, panel)


def swap(array, axis, bits):
    size = lax.axis_size(axis)
    return lax.ppermute(array, axis, [(index, index ^ bits) for index in range(size)])


def exchange(n_src, far, near, own):
    bf16, f32 = jnp.bfloat16, jnp.float32
    half = n_src // 2
    if n_src != 4:
        arriving = [swap(far(turn, [bf16])[0], "src", turn) for turn in range(n_src - 1, half - 1, -1)]
        arriving += [swap(near(turn, [bf16])[0], "src", turn) for turn in range(half - 1, 0, -1)]
        return own(0, [f32])[0], arriving, False
    first = lax.ppermute(far(2, [bf16])[0], "src", [(0, 1), (1, 3), (3, 2), (2, 0)])
    sent, kept = far(3, [bf16, f32])
    beside = near(1, [bf16])[0]
    sent, beside = lax.optimization_barrier((sent, beside))
    outer = lax.ppermute(sent, "src", [(0, 3), (3, 0)])
    both = make_sum(kept, first)
    both, beside = lax.optimization_barrier((both, beside))
    inner = lax.ppermute(both, "src", [(1, 2), (2, 1)])
    beside = swap(beside, "src", 1)
    return own(0, [f32])[0], [first, outer, inner, beside], True


def iterate(estimate, data, place, n_row, n_src, slice_rows):
    f32 = jnp.float32
    half = n_src // 2
    direct = {turn: swap(estimate, "row", turn) for turn in range(n_row - 2, 0, -2)}
    first = {0: estimate, 1: swap(estimate, "row", 1)}
    turns = tuple(range(n_src - 1, -1, -1))
    begun = make_terms(data, place, first, turns, [], slice_rows, [f32])
    held = lax.optimization_barrier((*direct.values(), *begun))
    direct = dict(zip(direct, held))
    begun = dict(zip(turns, held[len(direct) :]))
    passed = {turn + 1: swap(piece, "row", 1) for turn, piece in direct.items()}
    turns = tuple(range(n_src - 1, half - 1, -1))
    sums = make_terms(data, place, direct, turns, [begun[turn] for turn in turns], slice_rows, [f32])
    later = dict(zip(turns, sums))

    def far(turn, types):
        return make_terms(data, place, passed, (turn,), [later[turn]], slice_rows, types)

    def near(turn, types):
        return make_terms(data, place, {**direct, **passed}, (turn,), [begun[turn]], slice_rows, types)

    return exchange(n_src, far, near, near)


def body(traces, row_source, slice_data, wavelet_inverse):
    block_rows, shots, _ = traces.shape
    n_row, n_src = lax.axis_size("row"), lax.axis_size("src")
    row, src = lax.axis_index("row"), lax.axis_index("src")
    place = jnp.stack([row, src]).astype(jnp.int32)
    packs = LANES // (2 * shots)
    group_rows = block_rows // n_row
    slice_rows = block_rows // n_src
    block = min(group_rows, 64)
    short = block // packs

    spectra = make_spectra(traces, place, n_row, packs, block)
    arrived = [spectra[0]] + [swap(spectra[turn], "row", turn) for turn in range(1, n_row)]

    inside = row_source % group_rows
    position = (row_source // block_rows ^ row) * (group_rows // packs) + inside // block * short + inside % short
    code = position * packs + inside % block // short
    code = jnp.broadcast_to(code[:, None], (block_rows, LANES))
    real_data, _ = relay(slice_data, 0, spectra[0])
    ordered = make_order(code, arrived, place, n_src, packs)
    located = [ordered[0]] + [swap(ordered[turn], "src", turn) for turn in range(1, n_src)]
    imag_data, token = relay(slice_data, 1, ordered[0])
    panel = make_panel(located, place, packs, token)

    estimate = panel
    for iteration in range(ITERS):
        own, arriving, folded = iterate(estimate, (real_data, imag_data), place, n_row, n_src, slice_rows)
        estimate = make_update(place, wavelet_inverse, own, arriving, panel, folded, iteration == ITERS - 1)
    return tuple(estimate)


def solution(mesh):
    in_specs = (P("row", "src", None), P("row"), P(None, "row", None, "src"), P())
    out_specs = (P(("row", "src"), None, None), P(("row", "src"), None, None))
    return jax.shard_map(body, mesh=mesh, in_specs=in_specs, out_specs=out_specs, check_vma=False)
```

```python
import functools

import jax
import jax.numpy as jnp
import ml_dtypes
import numpy as np
from jax import lax
from jax.experimental import pallas as pl
from jax.experimental.pallas import tpu as pltpu
from jax.sharding import PartitionSpec as P

FREQ = 61
ITERS = 3
LANES = 128
BUFFERS = 4
VMEM = pl.BlockSpec(memory_space=pltpu.VMEM)
ANY = pl.BlockSpec(memory_space=pl.ANY)
SMEM = pl.BlockSpec(memory_space=pltpu.SMEM)


def dft_table(samples):
    ticks = np.arange(samples, dtype=np.int32)
    moment = ticks.astype(np.float32)
    ramp_len = samples // 8
    pi = np.float32(np.pi)
    half = np.float32(0.5)
    rising = half - half * np.cos(pi * (moment + half) / np.float32(ramp_len))
    falling = half - half * np.cos(pi * (np.float32(samples) - moment - half) / np.float32(ramp_len))
    taper = np.where(
        ticks < ramp_len, rising, np.where(ticks >= samples - ramp_len, falling, np.ones_like(rising))
    )
    wrapped = ticks * FREQ % samples
    angles = np.float32(2.0 * np.pi / samples) * wrapped.astype(np.float32)
    factor = np.float32(1.0) / np.sqrt(np.float32(samples))
    table = np.stack([taper * np.cos(angles) * factor, -taper * np.sin(angles) * factor], axis=1)
    return table.astype(ml_dtypes.bfloat16)


def params(megabytes):
    return pltpu.CompilerParams(vmem_limit_bytes=megabytes * 2**20)


def cost(flops, moved):
    return pl.CostEstimate(flops=int(flops), bytes_accessed=int(moved), transcendentals=0)


def streamed(steps, source, held, sems, work, ready=None):
    slots = held.shape[0]

    def copy(step):
        slot = step % slots
        return pltpu.make_async_copy(source(step), held.at[slot], sems.at[slot])

    for step in range(min(slots - 1, steps)):
        copy(step).start()
    if ready is not None:
        ready()

    @pl.loop(0, steps)
    def _(step):
        @pl.when(step + slots - 1 < steps)
        def _():
            copy(step + slots - 1).start()

        copy(step).wait()
        work(step, held.at[step % slots])


def spectra_kernel(packs, n_row, place_ref, traces_ref, table_ref, *refs):
    out_refs = refs[:n_row]
    held, sems, table, table_sem = refs[n_row:]
    block = held.shape[1]
    steps = traces_ref.shape[0] // n_row // block

    def source(step):
        first = ((place_ref[0] ^ (step // steps)) * steps + step % steps) * block
        return traces_ref.at[pl.ds(pl.multiple_of(first, block), block)]

    def work(step, traces):
        packed = spectra_of(packs, traces, table)
        for turn, out_ref in enumerate(out_refs):

            @pl.when(step // steps == turn)
            def _():
                out_ref[step % steps] = packed

    def ready():
        copy = pltpu.make_async_copy(table_ref, table, table_sem)
        copy.start()
        copy.wait()

    streamed(n_row * steps, source, held, sems, work, ready)


def spectra_of(packs, traces_ref, table_ref):
    block, shots, samples = traces_ref.shape
    width = 2 * shots
    half = block // 2
    shot = lax.broadcasted_iota(jnp.int32, (1, shots, 2 * LANES), 1)
    lane = lax.broadcasted_iota(jnp.int32, (1, shots, 2 * LANES), 2)
    own = lane % shots == shot
    sides = [traces_ref[side * half : (side + 1) * half].reshape(half * shots, samples) for side in range(2)]
    terms = jnp.dot(jnp.concatenate(sides, axis=1), table_ref[...], preferred_element_type=jnp.float32)
    rows = jnp.sum(jnp.where(own, terms.reshape(half, shots, 2 * LANES), 0.0), axis=1)
    spectra = jnp.concatenate([rows[:, :LANES], rows[:, LANES:]], axis=0)
    short = block // packs
    column = lax.broadcasted_iota(jnp.int32, (short, LANES), 1)
    packed = spectra[:short]
    for part in range(1, packs):
        packed = jnp.where(column // width == part, spectra[part * short : (part + 1) * short], packed)
    return packed.astype(jnp.bfloat16)


def make_spectra(traces, place, n_row, packs, block):
    block_rows, shots, samples = traces.shape
    steps = block_rows // n_row // block
    short = block // packs
    columns = np.tile(np.repeat(dft_table(samples), shots, axis=1), (1, packs))
    table = jnp.asarray(np.block([[columns, 0 * columns], [0 * columns, columns]]))

    outs = pl.pallas_call(
        functools.partial(spectra_kernel, packs, n_row),
        in_specs=[SMEM, ANY, pl.BlockSpec(memory_space=pltpu.HBM)],
        out_specs=[VMEM] * n_row,
        out_shape=[jax.ShapeDtypeStruct((steps, short, LANES), jnp.bfloat16)] * n_row,
        scratch_shapes=[
            pltpu.VMEM((BUFFERS, block, shots, samples), jnp.bfloat16),
            pltpu.SemaphoreType.DMA((BUFFERS,)),
            pltpu.VMEM(table.shape, table.dtype),
            pltpu.SemaphoreType.DMA,
        ],
        compiler_params=params(48),
        cost_estimate=cost(2 * traces.size * LANES, 2 * traces.size),
        name="spectra",
    )(place, traces, table)
    return [out.reshape(steps * short, LANES) for out in outs]


def order_kernel(packs, n_src, place_ref, code_ref, *refs):
    pieces, out_refs = refs[:-n_src], refs[-n_src:]
    width = LANES // packs
    held = jnp.concatenate([ref[...] for ref in pieces], axis=0)
    rolled = [held] + [
        pltpu.roll(held.astype(jnp.float32), turn * width, 1).astype(jnp.bfloat16) for turn in range(1, packs)
    ]
    table = jnp.concatenate(rolled, axis=1)
    depth = table.shape[0]
    slice_rows = code_ref.shape[0] // n_src
    short = slice_rows // packs
    column = lax.broadcasted_iota(jnp.int32, (short, LANES), 1)
    for turn, out_ref in enumerate(out_refs):
        first = pl.multiple_of((place_ref[1] ^ turn) * slice_rows, slice_rows)
        packed = None
        for part in range(packs):
            code = code_ref[pl.ds(pl.multiple_of(first + part * short, short), short), :]
            position, side = code // packs, code % packs
            hits = []
            for start in range(0, depth, LANES):
                hits.append(jnp.where(position == column + start, 1.0, 0.0).astype(jnp.bfloat16))
            chosen = jnp.concatenate(hits, axis=1)[:, :depth]
            rows = jnp.dot(chosen, table, preferred_element_type=jnp.float32)
            moved = rows[:, :LANES]
            for turned in range(1, packs):
                moved = jnp.where(
                    (part - side + packs) % packs == turned, rows[:, turned * LANES : (turned + 1) * LANES], moved
                )
            packed = moved if packed is None else jnp.where(column // width == part, moved, packed)
        out_ref[...] = packed.astype(jnp.bfloat16)


def make_order(code, pieces, place, n_src, packs):
    slice_rows = code.shape[0] // n_src
    return pl.pallas_call(
        functools.partial(order_kernel, packs, n_src),
        in_specs=[SMEM] + [VMEM] * (1 + len(pieces)),
        out_specs=[VMEM] * n_src,
        out_shape=[jax.ShapeDtypeStruct((slice_rows // packs, LANES), jnp.bfloat16)] * n_src,
        compiler_params=params(8),
        cost_estimate=cost(2 * code.shape[0] * len(pieces) * pieces[0].size * packs, 4 * code.size),
        name="order",
    )(place, code, *pieces)


def panel_kernel(packs, place_ref, *refs):
    pieces, panel_ref = refs[:-2], refs[-1]
    short = pieces[0].shape[0]
    width = LANES // packs
    shots = width // 2
    columns = panel_ref.shape[1]
    lane = lax.broadcasted_iota(jnp.int32, (LANES, packs * columns), 0)
    target = lax.broadcasted_iota(jnp.int32, (LANES, packs * columns), 1)
    total = None
    for turn, piece in enumerate(pieces):
        shot = (place_ref[1] ^ turn) * shots + lane % shots
        goes = lane // width * columns + lane % width // shots * (columns // 2) + shot
        chosen = jnp.where(target == goes, 1.0, 0.0).astype(jnp.bfloat16)
        term = jnp.dot(piece[...], chosen, preferred_element_type=jnp.float32)
        total = term if total is None else total + term
    for part in range(packs):
        panel_ref[part * short : (part + 1) * short, :] = total[:, part * columns : (part + 1) * columns].astype(
            jnp.bfloat16
        )


def make_panel(pieces, place, packs, after):
    rows = pieces[0].shape[0] * packs
    columns = len(pieces) * (LANES // packs)
    return pl.pallas_call(
        functools.partial(panel_kernel, packs),
        in_specs=[SMEM] + [VMEM] * len(pieces) + [ANY],
        out_specs=VMEM,
        out_shape=jax.ShapeDtypeStruct((rows, columns), jnp.bfloat16),
        compiler_params=params(8),
        cost_estimate=cost(2 * len(pieces) * rows * LANES * columns, 4 * rows * columns),
        name="panel",
    )(place, *pieces, after)


def relay_kernel(part, data_ref, after_ref, out_ref, token_ref, held, sems):
    token_ref[...] = jnp.zeros_like(token_ref)
    step_rows = held.shape[1]

    def source(step):
        return data_ref.at[part, pl.ds(pl.multiple_of(step * step_rows, step_rows), step_rows)]

    def work(step, data):
        rows = pl.ds(pl.multiple_of(step * step_rows, step_rows), step_rows)
        out_ref[:, rows, :] = jnp.swapaxes(data[...], 0, 1)

    streamed(data_ref.shape[1] // step_rows, source, held, sems, work)


def relay(slice_data, part, after):
    _, block_rows, blocks, offsets = slice_data.shape
    step_rows = min(block_rows, 128)
    return pl.pallas_call(
        functools.partial(relay_kernel, part),
        in_specs=[ANY, ANY],
        out_specs=[VMEM] * 2,
        out_shape=[
            jax.ShapeDtypeStruct((blocks, block_rows, offsets), jnp.bfloat16),
            jax.ShapeDtypeStruct((8, LANES), jnp.float32),
        ],
        scratch_shapes=[
            pltpu.VMEM((BUFFERS, step_rows, blocks, offsets), jnp.bfloat16),
            pltpu.SemaphoreType.DMA((BUFFERS,)),
        ],
        compiler_params=params(12),
        cost_estimate=cost(0, 2 * slice_data.size),
        name="relay",
    )(slice_data, after)


def terms_kernel(turns, numbers, begun, place_ref, real_ref, imag_ref, *refs):
    pieces = refs[: len(numbers)]
    partial = refs[len(numbers) : len(numbers) + begun]
    out_refs = refs[len(numbers) + begun :]
    columns = pieces[0].shape[1]
    kept = columns // 2
    size = out_refs[0].shape[0]
    each = len(out_refs) // len(turns)
    for index, turn in enumerate(turns):
        rows = pl.ds(pl.multiple_of((place_ref[1] ^ turn) * size, size), size)
        total = jnp.zeros((2 * size, columns), jnp.float32)
        for number, piece in zip(numbers, pieces):
            block = place_ref[0] ^ number
            both = jnp.concatenate([real_ref[block, rows, :], imag_ref[block, rows, :]], axis=0)
            total += jnp.dot(both, piece[...], preferred_element_type=jnp.float32)
        by_real, by_imag = total[:size], total[size:]
        real = by_real[:, :kept] - by_imag[:, kept:]
        imag = by_real[:, kept:] + by_imag[:, :kept]
        if begun:
            real += partial[index][:, :kept]
            imag += partial[index][:, kept:]
        for out_ref in out_refs[index * each : (index + 1) * each]:
            out_ref[:, :kept] = real.astype(out_ref.dtype)
            out_ref[:, kept:] = imag.astype(out_ref.dtype)


def make_terms(data, place, pieces, turns, partial, slice_rows, types):
    real_data, imag_data = data
    numbers = tuple(pieces)
    offsets, columns = pieces[numbers[0]].shape
    size = len(turns) * slice_rows * len(numbers) * offsets
    return pl.pallas_call(
        functools.partial(terms_kernel, turns, numbers, len(partial)),
        in_specs=[SMEM] + [VMEM] * (2 + len(numbers) + len(partial)),
        out_specs=[VMEM] * len(types) * len(turns),
        out_shape=[jax.ShapeDtypeStruct((slice_rows, columns), kind) for kind in types] * len(turns),
        compiler_params=params(8),
        cost_estimate=cost(4 * size * columns, 4 * size),
        name="terms",
    )(place, real_data, imag_data, *pieces.values(), *partial)


def add_kernel(own_ref, other_ref, out_ref):
    out_ref[...] = (own_ref[...] + other_ref[...].astype(jnp.float32)).astype(out_ref.dtype)


def make_sum(own, other):
    return pl.pallas_call(
        add_kernel,
        in_specs=[VMEM] * 2,
        out_specs=VMEM,
        out_shape=jax.ShapeDtypeStruct(other.shape, other.dtype),
        compiler_params=params(8),
        cost_estimate=cost(other.size, 8 * other.size),
        name="sum",
    )(own, other)


def update(place_ref, wave_ref, own_ref, others, panel_ref, folded):
    predicted = own_ref[...]
    for number, other in enumerate(others):
        term = other[...].astype(jnp.float32)
        if folded and number == 0:
            inner = place_ref[1] % 2 != place_ref[1] // 2 % 2
            term = jnp.where(inner, 0.0, term)
        predicted += term
    kept = predicted.shape[1] // 2
    turned = jnp.concatenate([-predicted[:, kept:], predicted[:, :kept]], axis=1)
    scaled = wave_ref[0] * predicted + wave_ref[1] * turned
    return predicted, panel_ref[...].astype(jnp.float32) - scaled


def estimate_kernel(folded, place_ref, wave_ref, own_ref, *refs):
    *others, panel_ref, out_ref = refs
    primaries = update(place_ref, wave_ref, own_ref, others, panel_ref, folded)[1]
    out_ref[...] = primaries.astype(jnp.bfloat16)


def last_kernel(folded, place_ref, wave_ref, own_ref, *refs):
    *others, panel_ref, multiples_ref, primaries_ref = refs
    predicted, primaries = update(place_ref, wave_ref, own_ref, others, panel_ref, folded)
    kept = predicted.shape[1] // 2
    multiples_ref[:, 0, :] = predicted[:, :kept]
    multiples_ref[:, 1, :] = predicted[:, kept:]
    primaries_ref[:, 0, :] = primaries[:, :kept]
    primaries_ref[:, 1, :] = primaries[:, kept:]


def make_update(place, wavelet, own, others, panel, folded, last):
    rows, columns = panel.shape
    if last:
        shape = [jax.ShapeDtypeStruct((rows, 2, columns // 2), jnp.float32)] * 2
    else:
        shape = jax.ShapeDtypeStruct((rows, columns), jnp.bfloat16)
    return pl.pallas_call(
        functools.partial(last_kernel if last else estimate_kernel, folded),
        in_specs=[SMEM] * 2 + [VMEM] * (2 + len(others)),
        out_specs=[VMEM] * 2 if last else VMEM,
        out_shape=shape,
        compiler_params=params(8),
        cost_estimate=cost(16 * rows * columns, 16 * rows * columns),
        name="update",
    )(place, wavelet, own, *others, panel)


def swap(array, axis, bits):
    size = lax.axis_size(axis)
    return lax.ppermute(array, axis, [(index, index ^ bits) for index in range(size)])


def exchange(n_src, make):
    bf16, f32 = jnp.bfloat16, jnp.float32
    if n_src != 4:
        arriving = [swap(make(turn, [bf16])[0], "src", turn) for turn in range(n_src - 1, 0, -1)]
        return make(0, [f32])[0], arriving, False
    first = lax.ppermute(make(2, [bf16])[0], "src", [(0, 1), (1, 3), (3, 2), (2, 0)])
    sent, kept = make(3, [bf16, f32])
    near = make(1, [bf16])[0]
    both, near = lax.optimization_barrier((make_sum(kept, first), near))
    beside = swap(near, "src", 1)
    outer = lax.ppermute(sent, "src", [(0, 3), (3, 0)])
    inner = lax.ppermute(both, "src", [(1, 2), (2, 1)])
    return make(0, [f32])[0], [first, beside, outer, inner], True


def iterate(estimate, data, place, n_row, n_src, slice_rows):
    direct = {turn: swap(estimate, "row", turn) for turn in range(2, n_row, 2)}
    first = {0: estimate, 1: swap(estimate, "row", 1)}
    turns = tuple(range(n_src))
    begun = make_terms(data, place, first, turns, [], slice_rows, [jnp.float32])
    held = lax.optimization_barrier((*direct.values(), *begun))
    direct, begun = dict(zip(direct, held)), held[len(direct) :]
    passed = {turn + 1: swap(piece, "row", 1) for turn, piece in direct.items()}

    def make(turn, types):
        return make_terms(data, place, {**direct, **passed}, (turn,), [begun[turn]], slice_rows, types)

    return exchange(n_src, make)


def body(traces, row_source, slice_data, wavelet_inverse):
    block_rows, shots, _ = traces.shape
    n_row, n_src = lax.axis_size("row"), lax.axis_size("src")
    row, src = lax.axis_index("row"), lax.axis_index("src")
    place = jnp.stack([row, src]).astype(jnp.int32)
    packs = LANES // (2 * shots)
    group_rows = block_rows // n_row
    slice_rows = block_rows // n_src
    block = min(group_rows, 128)
    short = block // packs

    spectra = make_spectra(traces, place, n_row, packs, block)
    arrived = [spectra[0]] + [swap(spectra[turn], "row", turn) for turn in range(1, n_row)]

    inside = row_source % group_rows
    position = (row_source // block_rows ^ row) * (group_rows // packs) + inside // block * short + inside % short
    code = position * packs + inside % block // short
    code = jnp.broadcast_to(code[:, None], (block_rows, LANES))
    real_data, _ = relay(slice_data, 0, spectra[0])
    ordered = make_order(code, arrived, place, n_src, packs)
    located = [ordered[0]] + [swap(ordered[turn], "src", turn) for turn in range(1, n_src)]
    imag_data, token = relay(slice_data, 1, ordered[0])
    panel = make_panel(located, place, packs, token)

    estimate = panel
    for iteration in range(ITERS):
        own, arriving, folded = iterate(estimate, (real_data, imag_data), place, n_row, n_src, slice_rows)
        estimate = make_update(place, wavelet_inverse, own, arriving, panel, folded, iteration == ITERS - 1)
    return tuple(estimate)


def solution(mesh):
    in_specs = (P("row", "src", None), P("row"), P(None, "row", None, "src"), P())
    out_specs = (P(("row", "src"), None, None), P(("row", "src"), None, None))
    return jax.shard_map(body, mesh=mesh, in_specs=in_specs, out_specs=out_specs, check_vma=False)
```

```python
import functools

import jax
import jax.numpy as jnp
import ml_dtypes
import numpy as np
from jax import lax
from jax.experimental import pallas as pl
from jax.experimental.pallas import tpu as pltpu
from jax.sharding import PartitionSpec as P

FREQ = 61
ITERS = 3
LANES = 128
BUFFERS = 4
VMEM = pl.BlockSpec(memory_space=pltpu.VMEM)
ANY = pl.BlockSpec(memory_space=pl.ANY)
SMEM = pl.BlockSpec(memory_space=pltpu.SMEM)


def dft_table(samples):
    ticks = np.arange(samples, dtype=np.int32)
    moment = ticks.astype(np.float32)
    ramp_len = samples // 8
    pi = np.float32(np.pi)
    half = np.float32(0.5)
    rising = half - half * np.cos(pi * (moment + half) / np.float32(ramp_len))
    falling = half - half * np.cos(pi * (np.float32(samples) - moment - half) / np.float32(ramp_len))
    taper = np.where(
        ticks < ramp_len, rising, np.where(ticks >= samples - ramp_len, falling, np.ones_like(rising))
    )
    wrapped = ticks * FREQ % samples
    angles = np.float32(2.0 * np.pi / samples) * wrapped.astype(np.float32)
    factor = np.float32(1.0) / np.sqrt(np.float32(samples))
    table = np.stack([taper * np.cos(angles) * factor, -taper * np.sin(angles) * factor], axis=1)
    return table.astype(ml_dtypes.bfloat16)


def params(megabytes):
    return pltpu.CompilerParams(vmem_limit_bytes=megabytes * 2**20)


def cost(flops, moved):
    return pl.CostEstimate(flops=int(flops), bytes_accessed=int(moved), transcendentals=0)


def streamed(steps, source, held, sems, work, ready=None):
    slots = held.shape[0]

    def copy(step):
        slot = step % slots
        return pltpu.make_async_copy(source(step), held.at[slot], sems.at[slot])

    for step in range(min(slots - 1, steps)):
        copy(step).start()
    if ready is not None:
        ready()

    @pl.loop(0, steps)
    def _(step):
        @pl.when(step + slots - 1 < steps)
        def _():
            copy(step + slots - 1).start()

        copy(step).wait()
        work(step, held.at[step % slots])


def spectra_kernel(packs, n_row, place_ref, traces_ref, table_ref, *refs):
    out_refs = refs[:n_row]
    held, sems, table, table_sem = refs[n_row:]
    block = held.shape[1]
    steps = traces_ref.shape[0] // n_row // block

    def source(step):
        first = ((place_ref[0] ^ (step // steps)) * steps + step % steps) * block
        return traces_ref.at[pl.ds(pl.multiple_of(first, block), block)]

    def work(step, traces):
        packed = spectra_of(packs, traces, table)
        for turn, out_ref in enumerate(out_refs):

            @pl.when(step // steps == turn)
            def _():
                out_ref[step % steps] = packed

    def ready():
        copy = pltpu.make_async_copy(table_ref, table, table_sem)
        copy.start()
        copy.wait()

    streamed(n_row * steps, source, held, sems, work, ready)


def spectra_of(packs, traces_ref, table_ref):
    block, shots, samples = traces_ref.shape
    width = 2 * shots
    half = block // 2
    shot = lax.broadcasted_iota(jnp.int32, (1, shots, 2 * LANES), 1)
    lane = lax.broadcasted_iota(jnp.int32, (1, shots, 2 * LANES), 2)
    own = lane % shots == shot
    sides = [traces_ref[side * half : (side + 1) * half].reshape(half * shots, samples) for side in range(2)]
    terms = jnp.dot(jnp.concatenate(sides, axis=1), table_ref[...], preferred_element_type=jnp.float32)
    rows = jnp.sum(jnp.where(own, terms.reshape(half, shots, 2 * LANES), 0.0), axis=1)
    spectra = jnp.concatenate([rows[:, :LANES], rows[:, LANES:]], axis=0)
    short = block // packs
    column = lax.broadcasted_iota(jnp.int32, (short, LANES), 1)
    packed = spectra[:short]
    for part in range(1, packs):
        packed = jnp.where(column // width == part, spectra[part * short : (part + 1) * short], packed)
    return packed.astype(jnp.bfloat16)


def make_spectra(traces, place, n_row, packs, block):
    block_rows, shots, samples = traces.shape
    steps = block_rows // n_row // block
    short = block // packs
    columns = np.tile(np.repeat(dft_table(samples), shots, axis=1), (1, packs))
    table = jnp.asarray(np.block([[columns, 0 * columns], [0 * columns, columns]]))

    outs = pl.pallas_call(
        functools.partial(spectra_kernel, packs, n_row),
        in_specs=[SMEM, ANY, pl.BlockSpec(memory_space=pltpu.HBM)],
        out_specs=[VMEM] * n_row,
        out_shape=[jax.ShapeDtypeStruct((steps, short, LANES), jnp.bfloat16)] * n_row,
        scratch_shapes=[
            pltpu.VMEM((BUFFERS, block, shots, samples), jnp.bfloat16),
            pltpu.SemaphoreType.DMA((BUFFERS,)),
            pltpu.VMEM(table.shape, table.dtype),
            pltpu.SemaphoreType.DMA,
        ],
        compiler_params=params(48),
        cost_estimate=cost(2 * traces.size * LANES, 2 * traces.size),
        name="spectra",
    )(place, traces, table)
    return [out.reshape(steps * short, LANES) for out in outs]


def order_kernel(packs, n_src, place_ref, code_ref, *refs):
    pieces, out_refs = refs[:-n_src], refs[-n_src:]
    width = LANES // packs
    held = jnp.concatenate([ref[...] for ref in pieces], axis=0)
    rolled = [held] + [
        pltpu.roll(held.astype(jnp.float32), turn * width, 1).astype(jnp.bfloat16) for turn in range(1, packs)
    ]
    table = jnp.concatenate(rolled, axis=1)
    depth = table.shape[0]
    slice_rows = code_ref.shape[0] // n_src
    short = slice_rows // packs
    column = lax.broadcasted_iota(jnp.int32, (short, LANES), 1)
    for turn, out_ref in enumerate(out_refs):
        first = pl.multiple_of((place_ref[1] ^ turn) * slice_rows, slice_rows)
        packed = None
        for part in range(packs):
            code = code_ref[pl.ds(pl.multiple_of(first + part * short, short), short), :]
            position, side = code // packs, code % packs
            hits = []
            for start in range(0, depth, LANES):
                hits.append(jnp.where(position == column + start, 1.0, 0.0).astype(jnp.bfloat16))
            chosen = jnp.concatenate(hits, axis=1)[:, :depth]
            rows = jnp.dot(chosen, table, preferred_element_type=jnp.float32)
            moved = rows[:, :LANES]
            for turned in range(1, packs):
                moved = jnp.where(
                    (part - side + packs) % packs == turned, rows[:, turned * LANES : (turned + 1) * LANES], moved
                )
            packed = moved if packed is None else jnp.where(column // width == part, moved, packed)
        out_ref[...] = packed.astype(jnp.bfloat16)


def make_order(code, pieces, place, n_src, packs):
    slice_rows = code.shape[0] // n_src
    return pl.pallas_call(
        functools.partial(order_kernel, packs, n_src),
        in_specs=[SMEM] + [VMEM] * (1 + len(pieces)),
        out_specs=[VMEM] * n_src,
        out_shape=[jax.ShapeDtypeStruct((slice_rows // packs, LANES), jnp.bfloat16)] * n_src,
        compiler_params=params(8),
        cost_estimate=cost(2 * code.shape[0] * len(pieces) * pieces[0].size * packs, 4 * code.size),
        name="order",
    )(place, code, *pieces)


def panel_kernel(packs, place_ref, *refs):
    pieces, panel_ref = refs[:-2], refs[-1]
    short = pieces[0].shape[0]
    width = LANES // packs
    shots = width // 2
    columns = panel_ref.shape[1]
    lane = lax.broadcasted_iota(jnp.int32, (LANES, packs * columns), 0)
    target = lax.broadcasted_iota(jnp.int32, (LANES, packs * columns), 1)
    total = None
    for turn, piece in enumerate(pieces):
        shot = (place_ref[1] ^ turn) * shots + lane % shots
        goes = lane // width * columns + lane % width // shots * (columns // 2) + shot
        chosen = jnp.where(target == goes, 1.0, 0.0).astype(jnp.bfloat16)
        term = jnp.dot(piece[...], chosen, preferred_element_type=jnp.float32)
        total = term if total is None else total + term
    for part in range(packs):
        panel_ref[part * short : (part + 1) * short, :] = total[:, part * columns : (part + 1) * columns].astype(
            jnp.bfloat16
        )


def make_panel(pieces, place, packs, after):
    rows = pieces[0].shape[0] * packs
    columns = len(pieces) * (LANES // packs)
    return pl.pallas_call(
        functools.partial(panel_kernel, packs),
        in_specs=[SMEM] + [VMEM] * len(pieces) + [ANY],
        out_specs=VMEM,
        out_shape=jax.ShapeDtypeStruct((rows, columns), jnp.bfloat16),
        compiler_params=params(8),
        cost_estimate=cost(2 * len(pieces) * rows * LANES * columns, 4 * rows * columns),
        name="panel",
    )(place, *pieces, after)


def relay_kernel(part, data_ref, after_ref, out_ref, token_ref, held, sems):
    token_ref[...] = jnp.zeros_like(token_ref)
    step_rows = held.shape[1]

    def source(step):
        return data_ref.at[part, pl.ds(pl.multiple_of(step * step_rows, step_rows), step_rows)]

    def work(step, data):
        rows = pl.ds(pl.multiple_of(step * step_rows, step_rows), step_rows)
        out_ref[:, rows, :] = jnp.swapaxes(data[...], 0, 1)

    streamed(data_ref.shape[1] // step_rows, source, held, sems, work)


def relay(slice_data, part, after):
    _, block_rows, blocks, offsets = slice_data.shape
    step_rows = min(block_rows, 128)
    return pl.pallas_call(
        functools.partial(relay_kernel, part),
        in_specs=[ANY, ANY],
        out_specs=[VMEM] * 2,
        out_shape=[
            jax.ShapeDtypeStruct((blocks, block_rows, offsets), jnp.bfloat16),
            jax.ShapeDtypeStruct((8, LANES), jnp.float32),
        ],
        scratch_shapes=[
            pltpu.VMEM((BUFFERS, step_rows, blocks, offsets), jnp.bfloat16),
            pltpu.SemaphoreType.DMA((BUFFERS,)),
        ],
        compiler_params=params(12),
        cost_estimate=cost(0, 2 * slice_data.size),
        name="relay",
    )(slice_data, after)


def terms_kernel(turns, numbers, begun, place_ref, real_ref, imag_ref, *refs):
    pieces = refs[: len(numbers)]
    partial = refs[len(numbers) : len(numbers) + begun]
    out_refs = refs[len(numbers) + begun :]
    columns = pieces[0].shape[1]
    kept = columns // 2
    size = out_refs[0].shape[0]
    each = len(out_refs) // len(turns)
    for index, turn in enumerate(turns):
        rows = pl.ds(pl.multiple_of((place_ref[1] ^ turn) * size, size), size)
        total = jnp.zeros((2 * size, columns), jnp.float32)
        for number, piece in zip(numbers, pieces):
            block = place_ref[0] ^ number
            both = jnp.concatenate([real_ref[block, rows, :], imag_ref[block, rows, :]], axis=0)
            total += jnp.dot(both, piece[...], preferred_element_type=jnp.float32)
        by_real, by_imag = total[:size], total[size:]
        real = by_real[:, :kept] - by_imag[:, kept:]
        imag = by_real[:, kept:] + by_imag[:, :kept]
        if begun:
            real += partial[index][:, :kept]
            imag += partial[index][:, kept:]
        for out_ref in out_refs[index * each : (index + 1) * each]:
            out_ref[:, :kept] = real.astype(out_ref.dtype)
            out_ref[:, kept:] = imag.astype(out_ref.dtype)


def make_terms(data, place, pieces, turns, partial, slice_rows, types):
    real_data, imag_data = data
    numbers = tuple(pieces)
    offsets, columns = pieces[numbers[0]].shape
    size = len(turns) * slice_rows * len(numbers) * offsets
    return pl.pallas_call(
        functools.partial(terms_kernel, turns, numbers, len(partial)),
        in_specs=[SMEM] + [VMEM] * (2 + len(numbers) + len(partial)),
        out_specs=[VMEM] * len(types) * len(turns),
        out_shape=[jax.ShapeDtypeStruct((slice_rows, columns), kind) for kind in types] * len(turns),
        compiler_params=params(8),
        cost_estimate=cost(4 * size * columns, 4 * size),
        name="terms",
    )(place, real_data, imag_data, *pieces.values(), *partial)


def add_kernel(own_ref, other_ref, out_ref):
    out_ref[...] = (own_ref[...] + other_ref[...].astype(jnp.float32)).astype(out_ref.dtype)


def make_sum(own, other):
    return pl.pallas_call(
        add_kernel,
        in_specs=[VMEM] * 2,
        out_specs=VMEM,
        out_shape=jax.ShapeDtypeStruct(other.shape, other.dtype),
        compiler_params=params(8),
        cost_estimate=cost(other.size, 8 * other.size),
        name="sum",
    )(own, other)


def update(place_ref, wave_ref, own_ref, others, panel_ref, folded):
    predicted = own_ref[...]
    for number, other in enumerate(others):
        term = other[...].astype(jnp.float32)
        if folded and number == 0:
            inner = place_ref[1] % 2 != place_ref[1] // 2 % 2
            term = jnp.where(inner, 0.0, term)
        predicted += term
    kept = predicted.shape[1] // 2
    turned = jnp.concatenate([-predicted[:, kept:], predicted[:, :kept]], axis=1)
    scaled = wave_ref[0] * predicted + wave_ref[1] * turned
    return predicted, panel_ref[...].astype(jnp.float32) - scaled


def estimate_kernel(folded, place_ref, wave_ref, own_ref, *refs):
    *others, panel_ref, out_ref = refs
    primaries = update(place_ref, wave_ref, own_ref, others, panel_ref, folded)[1]
    out_ref[...] = primaries.astype(jnp.bfloat16)


def last_kernel(folded, place_ref, wave_ref, own_ref, *refs):
    *others, panel_ref, multiples_ref, primaries_ref = refs
    predicted, primaries = update(place_ref, wave_ref, own_ref, others, panel_ref, folded)
    kept = predicted.shape[1] // 2
    multiples_ref[:, 0, :] = predicted[:, :kept]
    multiples_ref[:, 1, :] = predicted[:, kept:]
    primaries_ref[:, 0, :] = primaries[:, :kept]
    primaries_ref[:, 1, :] = primaries[:, kept:]


def make_update(place, wavelet, own, others, panel, folded, last):
    rows, columns = panel.shape
    if last:
        shape = [jax.ShapeDtypeStruct((rows, 2, columns // 2), jnp.float32)] * 2
    else:
        shape = jax.ShapeDtypeStruct((rows, columns), jnp.bfloat16)
    return pl.pallas_call(
        functools.partial(last_kernel if last else estimate_kernel, folded),
        in_specs=[SMEM] * 2 + [VMEM] * (2 + len(others)),
        out_specs=[VMEM] * 2 if last else VMEM,
        out_shape=shape,
        compiler_params=params(8),
        cost_estimate=cost(16 * rows * columns, 16 * rows * columns),
        name="update",
    )(place, wavelet, own, *others, panel)


def swap(array, axis, bits):
    size = lax.axis_size(axis)
    return lax.ppermute(array, axis, [(index, index ^ bits) for index in range(size)])


def exchange(n_src, make):
    bf16, f32 = jnp.bfloat16, jnp.float32
    if n_src != 4:
        arriving = [swap(make(turn, [bf16])[0], "src", turn) for turn in range(n_src - 1, 0, -1)]
        return make(0, [f32])[0], arriving, False
    first = lax.ppermute(make(2, [bf16])[0], "src", [(0, 1), (1, 3), (3, 2), (2, 0)])
    sent, kept = make(3, [bf16, f32])
    beside = swap(make(1, [bf16])[0], "src", 1)
    outer = lax.ppermute(sent, "src", [(0, 3), (3, 0)])
    inner = lax.ppermute(make_sum(kept, first), "src", [(1, 2), (2, 1)])
    return make(0, [f32])[0], [first, beside, outer, inner], True


def iterate(estimate, data, place, n_row, n_src, slice_rows, fresh):
    turns = range(2, n_row, 2)
    direct = {turn: swap(estimate, "row", turn) for turn in (reversed(turns) if fresh else turns)}
    if fresh:
        real_data, *held = lax.optimization_barrier((data[0], *direct.values()))
        data, direct = (real_data, data[1]), dict(zip(direct, held))
    passed = {turn + 1: swap(piece, "row", 1) for turn, piece in {0: estimate, **direct}.items()}
    early = {0: estimate, 1: passed[1], **direct}
    late = {turn: passed[turn] for turn in range(n_row - 1, 1, -2)}
    begun = make_terms(data, place, early, (n_src // 2,), [], slice_rows, [jnp.float32])

    def make(turn, types):
        if turn == n_src // 2:
            return make_terms(data, place, late, (turn,), begun, slice_rows, types)
        return make_terms(data, place, {**early, **late}, (turn,), [], slice_rows, types)

    return *exchange(n_src, make), data


def body(traces, row_source, slice_data, wavelet_inverse):
    block_rows, shots, _ = traces.shape
    n_row, n_src = lax.axis_size("row"), lax.axis_size("src")
    row, src = lax.axis_index("row"), lax.axis_index("src")
    place = jnp.stack([row, src]).astype(jnp.int32)
    packs = LANES // (2 * shots)
    group_rows = block_rows // n_row
    slice_rows = block_rows // n_src
    block = min(group_rows, 128)
    short = block // packs

    spectra = make_spectra(traces, place, n_row, packs, block)
    arrived = [spectra[0]] + [swap(spectra[turn], "row", turn) for turn in range(1, n_row)]

    inside = row_source % group_rows
    position = (row_source // block_rows ^ row) * (group_rows // packs) + inside // block * short + inside % short
    code = position * packs + inside % block // short
    code = jnp.broadcast_to(code[:, None], (block_rows, LANES))
    real_data, _ = relay(slice_data, 0, spectra[0])
    ordered = make_order(code, arrived, place, n_src, packs)
    located = [ordered[0]] + [swap(ordered[turn], "src", turn) for turn in range(1, n_src)]
    imag_data, token = relay(slice_data, 1, ordered[0])
    panel = make_panel(located, place, packs, token)

    estimate = panel
    data = real_data, imag_data
    for iteration in range(ITERS):
        own, arriving, folded, data = iterate(estimate, data, place, n_row, n_src, slice_rows, iteration == 0)
        estimate = make_update(place, wavelet_inverse, own, arriving, panel, folded, iteration == ITERS - 1)
    return tuple(estimate)


def solution(mesh):
    in_specs = (P("row", "src", None), P("row"), P(None, "row", None, "src"), P())
    out_specs = (P(("row", "src"), None, None), P(("row", "src"), None, None))
    return jax.shard_map(body, mesh=mesh, in_specs=in_specs, out_specs=out_specs, check_vma=False)
```

```python
import functools

import jax
import jax.numpy as jnp
import ml_dtypes
import numpy as np
from jax import lax
from jax.experimental import pallas as pl
from jax.experimental.pallas import tpu as pltpu
from jax.sharding import PartitionSpec as P

FREQ = 61
ITERS = 3
LANES = 128
BUFFERS = 4
VMEM = pl.BlockSpec(memory_space=pltpu.VMEM)
ANY = pl.BlockSpec(memory_space=pl.ANY)
SMEM = pl.BlockSpec(memory_space=pltpu.SMEM)


def dft_table(samples):
    ticks = np.arange(samples, dtype=np.int32)
    moment = ticks.astype(np.float32)
    ramp_len = samples // 8
    pi = np.float32(np.pi)
    half = np.float32(0.5)
    rising = half - half * np.cos(pi * (moment + half) / np.float32(ramp_len))
    falling = half - half * np.cos(pi * (np.float32(samples) - moment - half) / np.float32(ramp_len))
    taper = np.where(
        ticks < ramp_len, rising, np.where(ticks >= samples - ramp_len, falling, np.ones_like(rising))
    )
    wrapped = ticks * FREQ % samples
    angles = np.float32(2.0 * np.pi / samples) * wrapped.astype(np.float32)
    factor = np.float32(1.0) / np.sqrt(np.float32(samples))
    table = np.stack([taper * np.cos(angles) * factor, -taper * np.sin(angles) * factor], axis=1)
    return table.astype(ml_dtypes.bfloat16)


def params(megabytes):
    return pltpu.CompilerParams(vmem_limit_bytes=megabytes * 2**20)


def cost(flops, moved):
    return pl.CostEstimate(flops=int(flops), bytes_accessed=int(moved), transcendentals=0)


def streamed(steps, source, held, sems, work, ready=None):
    slots = held.shape[0]

    def copy(step):
        slot = step % slots
        return pltpu.make_async_copy(source(step), held.at[slot], sems.at[slot])

    for step in range(min(slots - 1, steps)):
        copy(step).start()
    if ready is not None:
        ready()

    @pl.loop(0, steps)
    def _(step):
        @pl.when(step + slots - 1 < steps)
        def _():
            copy(step + slots - 1).start()

        copy(step).wait()
        work(step, held.at[step % slots])


def spectra_kernel(packs, n_row, place_ref, traces_ref, table_ref, *refs):
    out_refs = refs[:n_row]
    held, sems, wide, table, table_sem = refs[n_row:]
    block = held.shape[1]
    steps = traces_ref.shape[0] // n_row // block

    def source(step):
        first = ((place_ref[0] ^ (step // steps)) * steps + step % steps) * block
        return traces_ref.at[pl.ds(pl.multiple_of(first, block), block)]

    def work(step, traces):
        packed = spectra_of(packs, traces, table)
        for turn, out_ref in enumerate(out_refs):

            @pl.when(step // steps == turn)
            def _():
                out_ref[step % steps] = packed

    def ready():
        copy = pltpu.make_async_copy(table_ref, wide, table_sem)
        copy.start()
        copy.wait()
        table[...] = wide[...].astype(table.dtype)

    streamed(n_row * steps, source, held, sems, work, ready)


def spectra_of(packs, traces_ref, table_ref):
    block, shots, samples = traces_ref.shape
    width = 2 * shots
    shot = lax.broadcasted_iota(jnp.int32, (1, shots, LANES), 1)
    lane = lax.broadcasted_iota(jnp.int32, (1, shots, LANES), 2)
    own = lane % shots == shot
    traces = traces_ref[...].reshape(block * shots, samples)
    terms = jnp.dot(traces, table_ref[...], preferred_element_type=jnp.float32)
    spectra = jnp.sum(jnp.where(own, terms.reshape(block, shots, LANES), 0.0), axis=1)
    short = block // packs
    column = lax.broadcasted_iota(jnp.int32, (short, LANES), 1)
    packed = spectra[:short]
    for part in range(1, packs):
        packed = jnp.where(column // width == part, spectra[part * short : (part + 1) * short], packed)
    return packed.astype(jnp.bfloat16)


def make_spectra(traces, place, n_row, packs, block):
    block_rows, shots, samples = traces.shape
    steps = block_rows // n_row // block
    short = block // packs
    columns = np.tile(np.repeat(dft_table(samples), shots, axis=1), (1, packs))
    table = jnp.asarray(columns.astype(np.float32))

    outs = pl.pallas_call(
        functools.partial(spectra_kernel, packs, n_row),
        in_specs=[SMEM, ANY, pl.BlockSpec(memory_space=pltpu.HBM)],
        out_specs=[VMEM] * n_row,
        out_shape=[jax.ShapeDtypeStruct((steps, short, LANES), jnp.bfloat16)] * n_row,
        scratch_shapes=[
            pltpu.VMEM((BUFFERS, block, shots, samples), jnp.bfloat16),
            pltpu.SemaphoreType.DMA((BUFFERS,)),
            pltpu.VMEM(table.shape, jnp.float32),
            pltpu.VMEM(table.shape, jnp.bfloat16),
            pltpu.SemaphoreType.DMA,
        ],
        compiler_params=params(48),
        cost_estimate=cost(2 * traces.size * LANES, 2 * traces.size),
        name="spectra",
    )(place, traces, table)
    return [out.reshape(steps * short, LANES) for out in outs]


def hits_kernel(packs, code_ref, after_ref, out_ref):
    rows, depth = out_ref.shape
    step = min(rows, 256)
    column = lax.broadcasted_iota(jnp.int32, (step, LANES), 1)
    for first in range(0, rows, step):
        position = code_ref[first : first + step, :] // packs
        for start in range(0, depth, LANES):
            size = min(LANES, depth - start)
            hit = jnp.where(position == column + start, 1.0, 0.0).astype(out_ref.dtype)
            out_ref[first : first + step, start : start + size] = hit[:, :size]


def make_hits(code, depth, packs, after):
    rows = code.shape[0]
    return pl.pallas_call(
        functools.partial(hits_kernel, packs),
        in_specs=[VMEM, ANY],
        out_specs=VMEM,
        out_shape=jax.ShapeDtypeStruct((rows, depth), jnp.bfloat16),
        compiler_params=params(12),
        cost_estimate=cost(rows * depth, 2 * rows * depth),
        name="hits",
    )(code, after)


def order_kernel(packs, n_src, place_ref, code_ref, hits_ref, *refs):
    pieces, out_refs = refs[:-n_src], refs[-n_src:]
    width = LANES // packs
    held = jnp.concatenate([ref[...] for ref in pieces], axis=0)
    rolled = [held] + [
        pltpu.roll(held.astype(jnp.float32), turn * width, 1).astype(jnp.bfloat16) for turn in range(1, packs)
    ]
    table = jnp.concatenate(rolled, axis=1)
    slice_rows = code_ref.shape[0] // n_src
    short = slice_rows // packs
    column = lax.broadcasted_iota(jnp.int32, (short, LANES), 1)
    for turn, out_ref in enumerate(out_refs):
        first = pl.multiple_of((place_ref[1] ^ turn) * slice_rows, slice_rows)
        packed = None
        for part in range(packs):
            chosen = pl.ds(pl.multiple_of(first + part * short, short), short)
            side = code_ref[chosen, :] % packs
            rows = jnp.dot(hits_ref[chosen, :], table, preferred_element_type=jnp.float32)
            moved = rows[:, :LANES]
            for turned in range(1, packs):
                moved = jnp.where(
                    (part - side + packs) % packs == turned, rows[:, turned * LANES : (turned + 1) * LANES], moved
                )
            packed = moved if packed is None else jnp.where(column // width == part, moved, packed)
        out_ref[...] = packed.astype(jnp.bfloat16)


def make_order(code, hits, pieces, place, n_src, packs):
    slice_rows = code.shape[0] // n_src
    return pl.pallas_call(
        functools.partial(order_kernel, packs, n_src),
        in_specs=[SMEM] + [VMEM] * (2 + len(pieces)),
        out_specs=[VMEM] * n_src,
        out_shape=[jax.ShapeDtypeStruct((slice_rows // packs, LANES), jnp.bfloat16)] * n_src,
        compiler_params=params(12),
        cost_estimate=cost(2 * hits.size * LANES * packs, 4 * code.size),
        name="order",
    )(place, code, hits, *pieces)


def panel_kernel(packs, place_ref, *refs):
    pieces, panel_ref = refs[:-2], refs[-1]
    short = pieces[0].shape[0]
    width = LANES // packs
    shots = width // 2
    columns = panel_ref.shape[1]
    lane = lax.broadcasted_iota(jnp.int32, (LANES, packs * columns), 0)
    target = lax.broadcasted_iota(jnp.int32, (LANES, packs * columns), 1)
    total = None
    for turn, piece in enumerate(pieces):
        shot = (place_ref[1] ^ turn) * shots + lane % shots
        goes = lane // width * columns + lane % width // shots * (columns // 2) + shot
        chosen = jnp.where(target == goes, 1.0, 0.0).astype(jnp.bfloat16)
        term = jnp.dot(piece[...], chosen, preferred_element_type=jnp.float32)
        total = term if total is None else total + term
    for part in range(packs):
        panel_ref[part * short : (part + 1) * short, :] = total[:, part * columns : (part + 1) * columns].astype(
            jnp.bfloat16
        )


def make_panel(pieces, place, packs, after):
    rows = pieces[0].shape[0] * packs
    columns = len(pieces) * (LANES // packs)
    return pl.pallas_call(
        functools.partial(panel_kernel, packs),
        in_specs=[SMEM] + [VMEM] * len(pieces) + [ANY],
        out_specs=VMEM,
        out_shape=jax.ShapeDtypeStruct((rows, columns), jnp.bfloat16),
        compiler_params=params(8),
        cost_estimate=cost(2 * len(pieces) * rows * LANES * columns, 4 * rows * columns),
        name="panel",
    )(place, *pieces, after)


def relay_kernel(part, data_ref, after_ref, out_ref, token_ref, held, sems):
    token_ref[...] = jnp.zeros_like(token_ref)
    step_rows = held.shape[1]

    def source(step):
        return data_ref.at[part, pl.ds(pl.multiple_of(step * step_rows, step_rows), step_rows)]

    def work(step, data):
        rows = pl.ds(pl.multiple_of(step * step_rows, step_rows), step_rows)
        out_ref[:, rows, :] = jnp.swapaxes(data[...], 0, 1)

    streamed(data_ref.shape[1] // step_rows, source, held, sems, work)


def relay(slice_data, part, after):
    _, block_rows, blocks, offsets = slice_data.shape
    step_rows = min(block_rows, 128)
    return pl.pallas_call(
        functools.partial(relay_kernel, part),
        in_specs=[ANY, ANY],
        out_specs=[VMEM] * 2,
        out_shape=[
            jax.ShapeDtypeStruct((blocks, block_rows, offsets), jnp.bfloat16),
            jax.ShapeDtypeStruct((8, LANES), jnp.float32),
        ],
        scratch_shapes=[
            pltpu.VMEM((BUFFERS, step_rows, blocks, offsets), jnp.bfloat16),
            pltpu.SemaphoreType.DMA((BUFFERS,)),
        ],
        compiler_params=params(12),
        cost_estimate=cost(0, 2 * slice_data.size),
        name="relay",
    )(slice_data, after)


def terms_kernel(turns, numbers, begun, place_ref, real_ref, imag_ref, *refs):
    pieces = refs[: len(numbers)]
    partial = refs[len(numbers) : len(numbers) + begun]
    out_refs = refs[len(numbers) + begun :]
    columns = pieces[0].shape[1]
    kept = columns // 2
    size = out_refs[0].shape[0]
    each = len(out_refs) // len(turns)
    for index, turn in enumerate(turns):
        rows = pl.ds(pl.multiple_of((place_ref[1] ^ turn) * size, size), size)
        total = jnp.zeros((2 * size, columns), jnp.float32)
        for number, piece in zip(numbers, pieces):
            block = place_ref[0] ^ number
            both = jnp.concatenate([real_ref[block, rows, :], imag_ref[block, rows, :]], axis=0)
            total += jnp.dot(both, piece[...], preferred_element_type=jnp.float32)
        by_real, by_imag = total[:size], total[size:]
        real = by_real[:, :kept] - by_imag[:, kept:]
        imag = by_real[:, kept:] + by_imag[:, :kept]
        if begun:
            real += partial[index][:, :kept]
            imag += partial[index][:, kept:]
        for out_ref in out_refs[index * each : (index + 1) * each]:
            out_ref[:, :kept] = real.astype(out_ref.dtype)
            out_ref[:, kept:] = imag.astype(out_ref.dtype)


def make_terms(data, place, pieces, turns, partial, slice_rows, types):
    real_data, imag_data = data
    numbers = tuple(pieces)
    offsets, columns = pieces[numbers[0]].shape
    size = len(turns) * slice_rows * len(numbers) * offsets
    return pl.pallas_call(
        functools.partial(terms_kernel, turns, numbers, len(partial)),
        in_specs=[SMEM] + [VMEM] * (2 + len(numbers) + len(partial)),
        out_specs=[VMEM] * len(types) * len(turns),
        out_shape=[jax.ShapeDtypeStruct((slice_rows, columns), kind) for kind in types] * len(turns),
        compiler_params=params(8),
        cost_estimate=cost(4 * size * columns, 4 * size),
        name="terms",
    )(place, real_data, imag_data, *pieces.values(), *partial)


def add_kernel(own_ref, other_ref, out_ref):
    out_ref[...] = (own_ref[...] + other_ref[...].astype(jnp.float32)).astype(out_ref.dtype)


def make_sum(own, other):
    return pl.pallas_call(
        add_kernel,
        in_specs=[VMEM] * 2,
        out_specs=VMEM,
        out_shape=jax.ShapeDtypeStruct(other.shape, other.dtype),
        compiler_params=params(8),
        cost_estimate=cost(other.size, 8 * other.size),
        name="sum",
    )(own, other)


def update(place_ref, wave_ref, own_ref, others, panel_ref, folded):
    predicted = own_ref[...]
    for number, other in enumerate(others):
        term = other[...].astype(jnp.float32)
        if folded and number == 0:
            inner = place_ref[1] % 2 != place_ref[1] // 2 % 2
            term = jnp.where(inner, 0.0, term)
        predicted += term
    kept = predicted.shape[1] // 2
    turned = jnp.concatenate([-predicted[:, kept:], predicted[:, :kept]], axis=1)
    scaled = wave_ref[0] * predicted + wave_ref[1] * turned
    return predicted, panel_ref[...].astype(jnp.float32) - scaled


def estimate_kernel(folded, place_ref, wave_ref, own_ref, *refs):
    *others, panel_ref, out_ref = refs
    primaries = update(place_ref, wave_ref, own_ref, others, panel_ref, folded)[1]
    out_ref[...] = primaries.astype(jnp.bfloat16)


def last_kernel(folded, place_ref, wave_ref, own_ref, *refs):
    *others, panel_ref, multiples_ref, primaries_ref = refs
    predicted, primaries = update(place_ref, wave_ref, own_ref, others, panel_ref, folded)
    kept = predicted.shape[1] // 2
    multiples_ref[:, 0, :] = predicted[:, :kept]
    multiples_ref[:, 1, :] = predicted[:, kept:]
    primaries_ref[:, 0, :] = primaries[:, :kept]
    primaries_ref[:, 1, :] = primaries[:, kept:]


def make_update(place, wavelet, own, others, panel, folded, last):
    rows, columns = panel.shape
    if last:
        shape = [jax.ShapeDtypeStruct((rows, 2, columns // 2), jnp.float32)] * 2
    else:
        shape = jax.ShapeDtypeStruct((rows, columns), jnp.bfloat16)
    return pl.pallas_call(
        functools.partial(last_kernel if last else estimate_kernel, folded),
        in_specs=[SMEM] * 2 + [VMEM] * (2 + len(others)),
        out_specs=[VMEM] * 2 if last else VMEM,
        out_shape=shape,
        compiler_params=params(8),
        cost_estimate=cost(16 * rows * columns, 16 * rows * columns),
        name="update",
    )(place, wavelet, own, *others, panel)


def swap(array, axis, bits):
    size = lax.axis_size(axis)
    return lax.ppermute(array, axis, [(index, index ^ bits) for index in range(size)])


def exchange(n_src, make):
    bf16, f32 = jnp.bfloat16, jnp.float32
    if n_src != 4:
        arriving = [swap(make(turn, [bf16])[0], "src", turn) for turn in range(n_src - 1, 0, -1)]
        return make(0, [f32])[0], arriving, False
    first = lax.ppermute(make(2, [bf16])[0], "src", [(0, 1), (1, 3), (3, 2), (2, 0)])
    sent, kept = make(3, [bf16, f32])
    beside = swap(make(1, [bf16])[0], "src", 1)
    outer = lax.ppermute(sent, "src", [(0, 3), (3, 0)])
    inner = lax.ppermute(make_sum(kept, first), "src", [(1, 2), (2, 1)])
    return make(0, [f32])[0], [first, beside, outer, inner], True


def iterate(estimate, data, place, n_row, n_src, slice_rows, fresh):
    turns = range(2, n_row, 2)
    direct = {turn: swap(estimate, "row", turn) for turn in (reversed(turns) if fresh else turns)}
    if fresh:
        real_data, *held = lax.optimization_barrier((data[0], *direct.values()))
        data, direct = (real_data, data[1]), dict(zip(direct, held))
    passed = {turn + 1: swap(piece, "row", 1) for turn, piece in {0: estimate, **direct}.items()}
    early = {0: estimate, 1: passed[1], **direct}
    late = {turn: passed[turn] for turn in range(n_row - 1, 1, -2)}
    begun = make_terms(data, place, early, (n_src // 2,), [], slice_rows, [jnp.float32])

    def make(turn, types):
        if turn == n_src // 2:
            return make_terms(data, place, late, (turn,), begun, slice_rows, types)
        return make_terms(data, place, {**early, **late}, (turn,), [], slice_rows, types)

    return *exchange(n_src, make), data


def body(traces, row_source, slice_data, wavelet_inverse):
    block_rows, shots, _ = traces.shape
    n_row, n_src = lax.axis_size("row"), lax.axis_size("src")
    row, src = lax.axis_index("row"), lax.axis_index("src")
    place = jnp.stack([row, src]).astype(jnp.int32)
    packs = LANES // (2 * shots)
    group_rows = block_rows // n_row
    slice_rows = block_rows // n_src
    block = min(group_rows, 128)
    short = block // packs

    spectra = make_spectra(traces, place, n_row, packs, block)
    arrived = [spectra[0]] + [swap(spectra[turn], "row", turn) for turn in range(1, n_row)]

    inside = row_source % group_rows
    position = (row_source // block_rows ^ row) * (group_rows // packs) + inside // block * short + inside % short
    code = position * packs + inside % block // short
    code = jnp.broadcast_to(code[:, None], (block_rows, LANES))
    real_data, _ = relay(slice_data, 0, spectra[0])
    hits = make_hits(code, block_rows // packs, packs, spectra[0])
    ordered = make_order(code, hits, arrived, place, n_src, packs)
    located = [ordered[0]] + [swap(ordered[turn], "src", turn) for turn in range(1, n_src)]
    imag_data, token = relay(slice_data, 1, ordered[0])
    panel = make_panel(located, place, packs, token)

    estimate = panel
    data = real_data, imag_data
    for iteration in range(ITERS):
        own, arriving, folded, data = iterate(estimate, data, place, n_row, n_src, slice_rows, iteration == 0)
        estimate = make_update(place, wavelet_inverse, own, arriving, panel, folded, iteration == ITERS - 1)
    return tuple(estimate)


def solution(mesh):
    in_specs = (P("row", "src", None), P("row"), P(None, "row", None, "src"), P())
    out_specs = (P(("row", "src"), None, None), P(("row", "src"), None, None))
    return jax.shard_map(body, mesh=mesh, in_specs=in_specs, out_specs=out_specs, check_vma=False)
```

```python
import functools

import jax
import jax.numpy as jnp
import ml_dtypes
import numpy as np
from jax import lax
from jax.experimental import pallas as pl
from jax.experimental.pallas import tpu as pltpu
from jax.sharding import PartitionSpec as P

FREQ = 61
ITERS = 3
LANES = 128
BUFFERS = 4
VMEM = pl.BlockSpec(memory_space=pltpu.VMEM)
ANY = pl.BlockSpec(memory_space=pl.ANY)
SMEM = pl.BlockSpec(memory_space=pltpu.SMEM)


def dft_table(samples):
    ticks = np.arange(samples, dtype=np.int32)
    moment = ticks.astype(np.float32)
    ramp_len = samples // 8
    pi = np.float32(np.pi)
    half = np.float32(0.5)
    rising = half - half * np.cos(pi * (moment + half) / np.float32(ramp_len))
    falling = half - half * np.cos(pi * (np.float32(samples) - moment - half) / np.float32(ramp_len))
    taper = np.where(
        ticks < ramp_len, rising, np.where(ticks >= samples - ramp_len, falling, np.ones_like(rising))
    )
    wrapped = ticks * FREQ % samples
    angles = np.float32(2.0 * np.pi / samples) * wrapped.astype(np.float32)
    factor = np.float32(1.0) / np.sqrt(np.float32(samples))
    table = np.stack([taper * np.cos(angles) * factor, -taper * np.sin(angles) * factor], axis=1)
    return table.astype(ml_dtypes.bfloat16)


def params(megabytes):
    return pltpu.CompilerParams(vmem_limit_bytes=megabytes * 2**20)


def cost(flops, moved):
    return pl.CostEstimate(flops=int(flops), bytes_accessed=int(moved), transcendentals=0)


def streamed(steps, source, held, sems, work, ready=None):
    slots = held.shape[0]

    def copy(step):
        slot = step % slots
        return pltpu.make_async_copy(source(step), held.at[slot], sems.at[slot])

    for step in range(min(slots - 1, steps)):
        copy(step).start()
    if ready is not None:
        ready()

    @pl.loop(0, steps)
    def _(step):
        @pl.when(step + slots - 1 < steps)
        def _():
            copy(step + slots - 1).start()

        copy(step).wait()
        work(step, held.at[step % slots])


def spectra_kernel(packs, n_row, place_ref, traces_ref, table_ref, *refs):
    out_refs = refs[:n_row]
    held, sems, wide, table, table_sem = refs[n_row:]
    block = held.shape[1]
    steps = traces_ref.shape[0] // n_row // block

    def source(step):
        first = ((place_ref[0] ^ (step // steps)) * steps + step % steps) * block
        return traces_ref.at[pl.ds(pl.multiple_of(first, block), block)]

    def work(step, traces):
        packed = spectra_of(packs, traces, table)
        for turn, out_ref in enumerate(out_refs):

            @pl.when(step // steps == turn)
            def _():
                out_ref[step % steps] = packed

    def ready():
        copy = pltpu.make_async_copy(table_ref, wide, table_sem)
        copy.start()
        copy.wait()
        table[...] = wide[...].astype(table.dtype)

    streamed(n_row * steps, source, held, sems, work, ready)


def spectra_of(packs, traces_ref, table_ref):
    block, shots, samples = traces_ref.shape
    width = 2 * shots
    shot = lax.broadcasted_iota(jnp.int32, (1, shots, LANES), 1)
    lane = lax.broadcasted_iota(jnp.int32, (1, shots, LANES), 2)
    own = lane % shots == shot
    traces = traces_ref[...].reshape(block * shots, samples)
    terms = jnp.dot(traces, table_ref[...], preferred_element_type=jnp.float32)
    spectra = jnp.sum(jnp.where(own, terms.reshape(block, shots, LANES), 0.0), axis=1)
    short = block // packs
    column = lax.broadcasted_iota(jnp.int32, (short, LANES), 1)
    packed = spectra[:short]
    for part in range(1, packs):
        packed = jnp.where(column // width == part, spectra[part * short : (part + 1) * short], packed)
    return packed.astype(jnp.bfloat16)


def make_spectra(traces, place, n_row, packs, block):
    block_rows, shots, samples = traces.shape
    steps = block_rows // n_row // block
    short = block // packs
    columns = np.tile(np.repeat(dft_table(samples), shots, axis=1), (1, packs))
    table = jnp.asarray(columns.astype(np.float32))

    outs = pl.pallas_call(
        functools.partial(spectra_kernel, packs, n_row),
        in_specs=[SMEM, ANY, pl.BlockSpec(memory_space=pltpu.HBM)],
        out_specs=[VMEM] * n_row,
        out_shape=[jax.ShapeDtypeStruct((steps, short, LANES), jnp.bfloat16)] * n_row,
        scratch_shapes=[
            pltpu.VMEM((BUFFERS, block, shots, samples), jnp.bfloat16),
            pltpu.SemaphoreType.DMA((BUFFERS,)),
            pltpu.VMEM(table.shape, jnp.float32),
            pltpu.VMEM(table.shape, jnp.bfloat16),
            pltpu.SemaphoreType.DMA,
        ],
        compiler_params=params(48),
        cost_estimate=cost(2 * traces.size * LANES, 2 * traces.size),
        name="spectra",
    )(place, traces, table)
    return [out.reshape(steps * short, LANES) for out in outs]


def hits_kernel(packs, code_ref, after_ref, out_ref):
    rows, depth = out_ref.shape
    step = min(rows, 256)
    column = lax.broadcasted_iota(jnp.int32, (step, LANES), 1)
    for first in range(0, rows, step):
        position = code_ref[first : first + step, :] // packs
        for start in range(0, depth, LANES):
            size = min(LANES, depth - start)
            hit = jnp.where(position == column + start, 1.0, 0.0).astype(out_ref.dtype)
            out_ref[first : first + step, start : start + size] = hit[:, :size]


def make_hits(code, depth, packs, after):
    rows = code.shape[0]
    return pl.pallas_call(
        functools.partial(hits_kernel, packs),
        in_specs=[VMEM, ANY],
        out_specs=VMEM,
        out_shape=jax.ShapeDtypeStruct((rows, depth), jnp.bfloat16),
        compiler_params=params(12),
        cost_estimate=cost(rows * depth, 2 * rows * depth),
        name="hits",
    )(code, after)


def order_kernel(packs, n_src, place_ref, code_ref, hits_ref, *refs):
    pieces, out_refs, found = refs[: -n_src - 1], refs[-n_src - 1 : -1], refs[-1]
    width = LANES // packs
    held = jnp.concatenate([ref[...] for ref in pieces], axis=0)
    rolled = [held] + [
        pltpu.roll(held.astype(jnp.float32), turn * width, 1).astype(jnp.bfloat16) for turn in range(1, packs)
    ]
    table = jnp.concatenate(rolled, axis=1)
    found[...] = jnp.dot(hits_ref[...], table, preferred_element_type=jnp.float32)
    slice_rows = code_ref.shape[0] // n_src
    short = slice_rows // packs
    column = lax.broadcasted_iota(jnp.int32, (short, LANES), 1)
    for turn, out_ref in enumerate(out_refs):
        first = pl.multiple_of((place_ref[1] ^ turn) * slice_rows, slice_rows)
        packed = None
        for part in range(packs):
            chosen = pl.ds(pl.multiple_of(first + part * short, short), short)
            side = code_ref[chosen, :] % packs
            rows = found[chosen, :]
            moved = rows[:, :LANES]
            for turned in range(1, packs):
                moved = jnp.where(
                    (part - side + packs) % packs == turned, rows[:, turned * LANES : (turned + 1) * LANES], moved
                )
            packed = moved if packed is None else jnp.where(column // width == part, moved, packed)
        out_ref[...] = packed.astype(jnp.bfloat16)


def make_order(code, hits, pieces, place, n_src, packs):
    slice_rows = code.shape[0] // n_src
    return pl.pallas_call(
        functools.partial(order_kernel, packs, n_src),
        in_specs=[SMEM] + [VMEM] * (2 + len(pieces)),
        out_specs=[VMEM] * n_src,
        out_shape=[jax.ShapeDtypeStruct((slice_rows // packs, LANES), jnp.bfloat16)] * n_src,
        scratch_shapes=[pltpu.VMEM((code.shape[0], LANES * packs), jnp.float32)],
        compiler_params=params(12),
        cost_estimate=cost(2 * hits.size * LANES * packs, 4 * code.size),
        name="order",
    )(place, code, hits, *pieces)


def panel_kernel(packs, place_ref, *refs):
    pieces, panel_ref = refs[:-2], refs[-1]
    short = pieces[0].shape[0]
    width = LANES // packs
    shots = width // 2
    columns = panel_ref.shape[1]
    lane = lax.broadcasted_iota(jnp.int32, (LANES, packs * columns), 0)
    target = lax.broadcasted_iota(jnp.int32, (LANES, packs * columns), 1)
    total = None
    for turn, piece in enumerate(pieces):
        shot = (place_ref[1] ^ turn) * shots + lane % shots
        goes = lane // width * columns + lane % width // shots * (columns // 2) + shot
        chosen = jnp.where(target == goes, 1.0, 0.0).astype(jnp.bfloat16)
        term = jnp.dot(piece[...], chosen, preferred_element_type=jnp.float32)
        total = term if total is None else total + term
    for part in range(packs):
        panel_ref[part * short : (part + 1) * short, :] = total[:, part * columns : (part + 1) * columns].astype(
            jnp.bfloat16
        )


def make_panel(pieces, place, packs, after):
    rows = pieces[0].shape[0] * packs
    columns = len(pieces) * (LANES // packs)
    return pl.pallas_call(
        functools.partial(panel_kernel, packs),
        in_specs=[SMEM] + [VMEM] * len(pieces) + [ANY],
        out_specs=VMEM,
        out_shape=jax.ShapeDtypeStruct((rows, columns), jnp.bfloat16),
        compiler_params=params(8),
        cost_estimate=cost(2 * len(pieces) * rows * LANES * columns, 4 * rows * columns),
        name="panel",
    )(place, *pieces, after)


def relay_kernel(part, data_ref, after_ref, out_ref, token_ref, held, sems):
    token_ref[...] = jnp.zeros_like(token_ref)
    step_rows = held.shape[1]

    def source(step):
        return data_ref.at[part, pl.ds(pl.multiple_of(step * step_rows, step_rows), step_rows)]

    def work(step, data):
        rows = pl.ds(pl.multiple_of(step * step_rows, step_rows), step_rows)
        out_ref[:, rows, :] = jnp.swapaxes(data[...], 0, 1)

    streamed(data_ref.shape[1] // step_rows, source, held, sems, work)


def relay(slice_data, part, after):
    _, block_rows, blocks, offsets = slice_data.shape
    step_rows = min(block_rows, 128)
    return pl.pallas_call(
        functools.partial(relay_kernel, part),
        in_specs=[ANY, ANY],
        out_specs=[VMEM] * 2,
        out_shape=[
            jax.ShapeDtypeStruct((blocks, block_rows, offsets), jnp.bfloat16),
            jax.ShapeDtypeStruct((8, LANES), jnp.float32),
        ],
        scratch_shapes=[
            pltpu.VMEM((BUFFERS, step_rows, blocks, offsets), jnp.bfloat16),
            pltpu.SemaphoreType.DMA((BUFFERS,)),
        ],
        compiler_params=params(12),
        cost_estimate=cost(0, 2 * slice_data.size),
        name="relay",
    )(slice_data, after)


def terms_kernel(turns, numbers, begun, place_ref, real_ref, imag_ref, *refs):
    pieces = refs[: len(numbers)]
    partial = refs[len(numbers) : len(numbers) + begun]
    out_refs = refs[len(numbers) + begun :]
    columns = pieces[0].shape[1]
    kept = columns // 2
    size = out_refs[0].shape[0]
    each = len(out_refs) // len(turns)
    for index, turn in enumerate(turns):
        rows = pl.ds(pl.multiple_of((place_ref[1] ^ turn) * size, size), size)
        total = jnp.zeros((2 * size, columns), jnp.float32)
        for number, piece in zip(numbers, pieces):
            block = place_ref[0] ^ number
            both = jnp.concatenate([real_ref[block, rows, :], imag_ref[block, rows, :]], axis=0)
            total += jnp.dot(both, piece[...], preferred_element_type=jnp.float32)
        by_real, by_imag = total[:size], total[size:]
        real = by_real[:, :kept] - by_imag[:, kept:]
        imag = by_real[:, kept:] + by_imag[:, :kept]
        if begun:
            real += partial[index][:, :kept]
            imag += partial[index][:, kept:]
        for out_ref in out_refs[index * each : (index + 1) * each]:
            out_ref[:, :kept] = real.astype(out_ref.dtype)
            out_ref[:, kept:] = imag.astype(out_ref.dtype)


def make_terms(data, place, pieces, turns, partial, slice_rows, types):
    real_data, imag_data = data
    numbers = tuple(pieces)
    offsets, columns = pieces[numbers[0]].shape
    size = len(turns) * slice_rows * len(numbers) * offsets
    return pl.pallas_call(
        functools.partial(terms_kernel, turns, numbers, len(partial)),
        in_specs=[SMEM] + [VMEM] * (2 + len(numbers) + len(partial)),
        out_specs=[VMEM] * len(types) * len(turns),
        out_shape=[jax.ShapeDtypeStruct((slice_rows, columns), kind) for kind in types] * len(turns),
        compiler_params=params(8),
        cost_estimate=cost(4 * size * columns, 4 * size),
        name="terms",
    )(place, real_data, imag_data, *pieces.values(), *partial)


def add_kernel(own_ref, other_ref, out_ref):
    out_ref[...] = (own_ref[...] + other_ref[...].astype(jnp.float32)).astype(out_ref.dtype)


def make_sum(own, other):
    return pl.pallas_call(
        add_kernel,
        in_specs=[VMEM] * 2,
        out_specs=VMEM,
        out_shape=jax.ShapeDtypeStruct(other.shape, other.dtype),
        compiler_params=params(8),
        cost_estimate=cost(other.size, 8 * other.size),
        name="sum",
    )(own, other)


def update(wave_ref, own_ref, others, panel_ref):
    predicted = own_ref[...]
    for other in others:
        predicted += other[...].astype(jnp.float32)
    kept = predicted.shape[1] // 2
    turned = jnp.concatenate([-predicted[:, kept:], predicted[:, :kept]], axis=1)
    scaled = wave_ref[0] * predicted + wave_ref[1] * turned
    return predicted, panel_ref[...].astype(jnp.float32) - scaled


def estimate_kernel(wave_ref, own_ref, *refs):
    *others, panel_ref, out_ref = refs
    out_ref[...] = update(wave_ref, own_ref, others, panel_ref)[1].astype(jnp.bfloat16)


def last_kernel(wave_ref, own_ref, *refs):
    *others, panel_ref, multiples_ref, primaries_ref = refs
    predicted, primaries = update(wave_ref, own_ref, others, panel_ref)
    kept = predicted.shape[1] // 2
    multiples_ref[:, 0, :] = predicted[:, :kept]
    multiples_ref[:, 1, :] = predicted[:, kept:]
    primaries_ref[:, 0, :] = primaries[:, :kept]
    primaries_ref[:, 1, :] = primaries[:, kept:]


def make_update(wavelet, own, others, panel, last):
    rows, columns = panel.shape
    if last:
        shape = [jax.ShapeDtypeStruct((rows, 2, columns // 2), jnp.float32)] * 2
    else:
        shape = jax.ShapeDtypeStruct((rows, columns), jnp.bfloat16)
    return pl.pallas_call(
        last_kernel if last else estimate_kernel,
        in_specs=[SMEM] + [VMEM] * (2 + len(others)),
        out_specs=[VMEM] * 2 if last else VMEM,
        out_shape=shape,
        compiler_params=params(8),
        cost_estimate=cost(16 * rows * columns, 16 * rows * columns),
        name="update",
    )(wavelet, own, *others, panel)


def swap(array, axis, bits):
    size = lax.axis_size(axis)
    return lax.ppermute(array, axis, [(index, index ^ bits) for index in range(size)])


def exchange(n_src, make):
    bf16, f32 = jnp.bfloat16, jnp.float32
    if n_src != 4:
        arriving = [swap(make(turn, [bf16])[0], "src", turn) for turn in range(n_src - 1, 0, -1)]
        return make(0, [f32])[0], arriving
    farthest = make(3, [bf16])[0]
    passed = lax.ppermute(farthest, "src", [(0, 1), (3, 2)])
    middle = lax.ppermute(farthest, "src", [(1, 2), (2, 1)])
    sent, kept = make(2, [bf16, f32])
    beside = swap(make(1, [bf16])[0], "src", 1)
    inward = lax.ppermute(sent, "src", [(0, 2), (3, 1)])
    outward = lax.ppermute(make_sum(kept, passed), "src", [(1, 3), (2, 0)])
    return make(0, [f32])[0], [middle, beside, inward, outward]


def iterate(estimate, data, place, n_row, n_src, slice_rows, fresh):
    turns = range(2, n_row, 2)
    direct = {turn: swap(estimate, "row", turn) for turn in (reversed(turns) if fresh else turns)}
    if fresh:
        real_data, *held = lax.optimization_barrier((data[0], *direct.values()))
        data, direct = (real_data, data[1]), dict(zip(direct, held))
    passed = {turn + 1: swap(piece, "row", 1) for turn, piece in {0: estimate, **direct}.items()}
    early = {0: estimate, 1: passed[1], **direct}
    late = {turn: passed[turn] for turn in range(n_row - 1, 1, -2)}
    begun = make_terms(data, place, early, (n_src - 1,), [], slice_rows, [jnp.float32])

    def make(turn, types):
        if turn == n_src - 1:
            return make_terms(data, place, late, (turn,), begun, slice_rows, types)
        return make_terms(data, place, {**early, **late}, (turn,), [], slice_rows, types)

    return *exchange(n_src, make), data


def body(traces, row_source, slice_data, wavelet_inverse):
    block_rows, shots, _ = traces.shape
    n_row, n_src = lax.axis_size("row"), lax.axis_size("src")
    row, src = lax.axis_index("row"), lax.axis_index("src")
    place = jnp.stack([row, src]).astype(jnp.int32)
    packs = LANES // (2 * shots)
    group_rows = block_rows // n_row
    slice_rows = block_rows // n_src
    block = min(group_rows, 128)
    short = block // packs

    spectra = make_spectra(traces, place, n_row, packs, block)
    arrived = [spectra[0]] + [swap(spectra[turn], "row", turn) for turn in range(1, n_row)]

    inside = row_source % group_rows
    position = (row_source // block_rows ^ row) * (group_rows // packs) + inside // block * short + inside % short
    code = position * packs + inside % block // short
    code = jnp.broadcast_to(code[:, None], (block_rows, LANES))
    real_data, _ = relay(slice_data, 0, spectra[0])
    hits = make_hits(code, block_rows // packs, packs, spectra[0])
    ordered = make_order(code, hits, arrived, place, n_src, packs)
    located = [ordered[0]] + [swap(ordered[turn], "src", turn) for turn in range(1, n_src)]
    imag_data, token = relay(slice_data, 1, ordered[0])
    panel = make_panel(located, place, packs, token)

    estimate = panel
    data = real_data, imag_data
    for iteration in range(ITERS):
        own, arriving, data = iterate(estimate, data, place, n_row, n_src, slice_rows, iteration == 0)
        estimate = make_update(wavelet_inverse, own, arriving, panel, iteration == ITERS - 1)
    return tuple(estimate)


def solution(mesh):
    in_specs = (P("row", "src", None), P("row"), P(None, "row", None, "src"), P())
    out_specs = (P(("row", "src"), None, None), P(("row", "src"), None, None))
    return jax.shard_map(body, mesh=mesh, in_specs=in_specs, out_specs=out_specs, check_vma=False)
```

```python
import functools

import jax
import jax.numpy as jnp
import ml_dtypes
import numpy as np
from jax import lax
from jax.experimental import pallas as pl
from jax.experimental.pallas import tpu as pltpu
from jax.sharding import PartitionSpec as P

FREQ = 61
ITERS = 3
LANES = 128
BUFFERS = 4
VMEM = pl.BlockSpec(memory_space=pltpu.VMEM)
ANY = pl.BlockSpec(memory_space=pl.ANY)
SMEM = pl.BlockSpec(memory_space=pltpu.SMEM)


def dft_table(samples):
    ticks = np.arange(samples, dtype=np.int32)
    moment = ticks.astype(np.float32)
    ramp_len = samples // 8
    pi = np.float32(np.pi)
    half = np.float32(0.5)
    rising = half - half * np.cos(pi * (moment + half) / np.float32(ramp_len))
    falling = half - half * np.cos(pi * (np.float32(samples) - moment - half) / np.float32(ramp_len))
    taper = np.where(
        ticks < ramp_len, rising, np.where(ticks >= samples - ramp_len, falling, np.ones_like(rising))
    )
    wrapped = ticks * FREQ % samples
    angles = np.float32(2.0 * np.pi / samples) * wrapped.astype(np.float32)
    factor = np.float32(1.0) / np.sqrt(np.float32(samples))
    table = np.stack([taper * np.cos(angles) * factor, -taper * np.sin(angles) * factor], axis=1)
    return table.astype(ml_dtypes.bfloat16)


def params(megabytes):
    return pltpu.CompilerParams(vmem_limit_bytes=megabytes * 2**20)


def cost(flops, moved):
    return pl.CostEstimate(flops=int(flops), bytes_accessed=int(moved), transcendentals=0)


def streamed(steps, source, held, sems, work, ready=None):
    slots = held.shape[0]

    def copy(step):
        slot = step % slots
        return pltpu.make_async_copy(source(step), held.at[slot], sems.at[slot])

    for step in range(min(slots - 1, steps)):
        copy(step).start()
    if ready is not None:
        ready()

    @pl.loop(0, steps)
    def _(step):
        @pl.when(step + slots - 1 < steps)
        def _():
            copy(step + slots - 1).start()

        copy(step).wait()
        work(step, held.at[step % slots])


def spectra_kernel(packs, n_row, place_ref, traces_ref, table_ref, *refs):
    out_refs = refs[:n_row]
    held, sems, wide, table, table_sem = refs[n_row:]
    block = held.shape[1]
    steps = traces_ref.shape[0] // n_row // block

    def source(step):
        first = ((place_ref[0] ^ (step // steps)) * steps + step % steps) * block
        return traces_ref.at[pl.ds(pl.multiple_of(first, block), block)]

    def work(step, traces):
        packed = spectra_of(packs, traces, table)
        for turn, out_ref in enumerate(out_refs):

            @pl.when(step // steps == turn)
            def _():
                out_ref[step % steps] = packed

    def ready():
        copy = pltpu.make_async_copy(table_ref, wide, table_sem)
        copy.start()
        copy.wait()
        table[...] = wide[...].astype(table.dtype)

    streamed(n_row * steps, source, held, sems, work, ready)


def spectra_of(packs, traces_ref, table_ref):
    block, shots, samples = traces_ref.shape
    width = 2 * shots
    shot = lax.broadcasted_iota(jnp.int32, (1, shots, LANES), 1)
    lane = lax.broadcasted_iota(jnp.int32, (1, shots, LANES), 2)
    own = lane % shots == shot
    traces = traces_ref[...].reshape(block * shots, samples)
    terms = jnp.dot(traces, table_ref[...], preferred_element_type=jnp.float32)
    spectra = jnp.sum(jnp.where(own, terms.reshape(block, shots, LANES), 0.0), axis=1)
    short = block // packs
    column = lax.broadcasted_iota(jnp.int32, (short, LANES), 1)
    packed = spectra[:short]
    for part in range(1, packs):
        packed = jnp.where(column // width == part, spectra[part * short : (part + 1) * short], packed)
    return packed.astype(jnp.bfloat16)


def make_spectra(traces, place, n_row, packs, block):
    block_rows, shots, samples = traces.shape
    steps = block_rows // n_row // block
    short = block // packs
    columns = np.tile(np.repeat(dft_table(samples), shots, axis=1), (1, packs))
    table = jnp.asarray(columns.astype(np.float32))

    outs = pl.pallas_call(
        functools.partial(spectra_kernel, packs, n_row),
        in_specs=[SMEM, ANY, pl.BlockSpec(memory_space=pltpu.HBM)],
        out_specs=[VMEM] * n_row,
        out_shape=[jax.ShapeDtypeStruct((steps, short, LANES), jnp.bfloat16)] * n_row,
        scratch_shapes=[
            pltpu.VMEM((BUFFERS, block, shots, samples), jnp.bfloat16),
            pltpu.SemaphoreType.DMA((BUFFERS,)),
            pltpu.VMEM(table.shape, jnp.float32),
            pltpu.VMEM(table.shape, jnp.bfloat16),
            pltpu.SemaphoreType.DMA,
        ],
        compiler_params=params(48),
        cost_estimate=cost(2 * traces.size * LANES, 2 * traces.size),
        name="spectra",
    )(place, traces, table)
    return [out.reshape(steps * short, LANES) for out in outs]


def hits_kernel(packs, code_ref, after_ref, out_ref):
    rows, depth = out_ref.shape
    step = min(rows, 256)
    column = lax.broadcasted_iota(jnp.int32, (step, LANES), 1)
    for first in range(0, rows, step):
        position = code_ref[first : first + step, :] // packs
        for start in range(0, depth, LANES):
            size = min(LANES, depth - start)
            hit = jnp.where(position == column + start, 1.0, 0.0).astype(out_ref.dtype)
            out_ref[first : first + step, start : start + size] = hit[:, :size]


def make_hits(code, depth, packs, after):
    rows = code.shape[0]
    return pl.pallas_call(
        functools.partial(hits_kernel, packs),
        in_specs=[VMEM, ANY],
        out_specs=VMEM,
        out_shape=jax.ShapeDtypeStruct((rows, depth), jnp.bfloat16),
        compiler_params=params(12),
        cost_estimate=cost(rows * depth, 2 * rows * depth),
        name="hits",
    )(code, after)


def order_kernel(packs, n_src, place_ref, code_ref, hits_ref, *refs):
    pieces, out_refs = refs[:-n_src], refs[-n_src:]
    width = LANES // packs
    held = jnp.concatenate([ref[...] for ref in pieces], axis=0)
    rolled = [held] + [
        pltpu.roll(held.astype(jnp.float32), turn * width, 1).astype(jnp.bfloat16) for turn in range(1, packs)
    ]
    table = jnp.concatenate(rolled, axis=1)
    slice_rows = code_ref.shape[0] // n_src
    short = slice_rows // packs
    column = lax.broadcasted_iota(jnp.int32, (short, LANES), 1)
    for turn, out_ref in enumerate(out_refs):
        first = pl.multiple_of((place_ref[1] ^ turn) * slice_rows, slice_rows)
        packed = None
        found = jnp.dot(hits_ref[pl.ds(first, slice_rows), :], table, preferred_element_type=jnp.float32)
        for part in range(packs):
            side = code_ref[pl.ds(pl.multiple_of(first + part * short, short), short), :] % packs
            rows = found[part * short : (part + 1) * short]
            moved = rows[:, :LANES]
            for turned in range(1, packs):
                moved = jnp.where(
                    (part - side + packs) % packs == turned, rows[:, turned * LANES : (turned + 1) * LANES], moved
                )
            packed = moved if packed is None else jnp.where(column // width == part, moved, packed)
        out_ref[...] = packed.astype(jnp.bfloat16)


def make_order(code, hits, pieces, place, n_src, packs):
    slice_rows = code.shape[0] // n_src
    return pl.pallas_call(
        functools.partial(order_kernel, packs, n_src),
        in_specs=[SMEM] + [VMEM] * (2 + len(pieces)),
        out_specs=[VMEM] * n_src,
        out_shape=[jax.ShapeDtypeStruct((slice_rows // packs, LANES), jnp.bfloat16)] * n_src,
        compiler_params=params(12),
        cost_estimate=cost(2 * hits.size * LANES * packs, 4 * code.size),
        name="order",
    )(place, code, hits, *pieces)


def panel_kernel(packs, place_ref, *refs):
    pieces, panel_ref = refs[:-2], refs[-1]
    short = pieces[0].shape[0]
    width = LANES // packs
    shots = width // 2
    columns = panel_ref.shape[1]
    lane = lax.broadcasted_iota(jnp.int32, (LANES, packs * columns), 0)
    target = lax.broadcasted_iota(jnp.int32, (LANES, packs * columns), 1)
    total = None
    for turn, piece in enumerate(pieces):
        shot = (place_ref[1] ^ turn) * shots + lane % shots
        goes = lane // width * columns + lane % width // shots * (columns // 2) + shot
        chosen = jnp.where(target == goes, 1.0, 0.0).astype(jnp.bfloat16)
        term = jnp.dot(piece[...], chosen, preferred_element_type=jnp.float32)
        total = term if total is None else total + term
    for part in range(packs):
        panel_ref[part * short : (part + 1) * short, :] = total[:, part * columns : (part + 1) * columns].astype(
            jnp.bfloat16
        )


def make_panel(pieces, place, packs, after):
    rows = pieces[0].shape[0] * packs
    columns = len(pieces) * (LANES // packs)
    return pl.pallas_call(
        functools.partial(panel_kernel, packs),
        in_specs=[SMEM] + [VMEM] * len(pieces) + [ANY],
        out_specs=VMEM,
        out_shape=jax.ShapeDtypeStruct((rows, columns), jnp.bfloat16),
        compiler_params=params(8),
        cost_estimate=cost(2 * len(pieces) * rows * LANES * columns, 4 * rows * columns),
        name="panel",
    )(place, *pieces, after)


def relay_kernel(part, data_ref, after_ref, out_ref, token_ref, held, sems):
    token_ref[...] = jnp.zeros_like(token_ref)
    step_rows = held.shape[1]

    def source(step):
        return data_ref.at[part, pl.ds(pl.multiple_of(step * step_rows, step_rows), step_rows)]

    def work(step, data):
        rows = pl.ds(pl.multiple_of(step * step_rows, step_rows), step_rows)
        out_ref[:, rows, :] = jnp.swapaxes(data[...], 0, 1)

    streamed(data_ref.shape[1] // step_rows, source, held, sems, work)


def relay(slice_data, part, after):
    _, block_rows, blocks, offsets = slice_data.shape
    step_rows = min(block_rows, 128)
    return pl.pallas_call(
        functools.partial(relay_kernel, part),
        in_specs=[ANY, ANY],
        out_specs=[VMEM] * 2,
        out_shape=[
            jax.ShapeDtypeStruct((blocks, block_rows, offsets), jnp.bfloat16),
            jax.ShapeDtypeStruct((8, LANES), jnp.float32),
        ],
        scratch_shapes=[
            pltpu.VMEM((BUFFERS, step_rows, blocks, offsets), jnp.bfloat16),
            pltpu.SemaphoreType.DMA((BUFFERS,)),
        ],
        compiler_params=params(12),
        cost_estimate=cost(0, 2 * slice_data.size),
        name="relay",
    )(slice_data, after)


def terms_kernel(turns, numbers, begun, place_ref, real_ref, imag_ref, *refs):
    pieces = refs[: len(numbers)]
    partial = refs[len(numbers) : len(numbers) + begun]
    out_refs = refs[len(numbers) + begun :]
    columns = pieces[0].shape[1]
    kept = columns // 2
    size = out_refs[0].shape[0]
    each = len(out_refs) // len(turns)
    for index, turn in enumerate(turns):
        rows = pl.ds(pl.multiple_of((place_ref[1] ^ turn) * size, size), size)
        total = jnp.zeros((2 * size, columns), jnp.float32)
        for number, piece in zip(numbers, pieces):
            block = place_ref[0] ^ number
            both = jnp.concatenate([real_ref[block, rows, :], imag_ref[block, rows, :]], axis=0)
            total += jnp.dot(both, piece[...], preferred_element_type=jnp.float32)
        by_real, by_imag = total[:size], total[size:]
        real = by_real[:, :kept] - by_imag[:, kept:]
        imag = by_real[:, kept:] + by_imag[:, :kept]
        if begun:
            real += partial[index][:, :kept]
            imag += partial[index][:, kept:]
        for out_ref in out_refs[index * each : (index + 1) * each]:
            out_ref[:, :kept] = real.astype(out_ref.dtype)
            out_ref[:, kept:] = imag.astype(out_ref.dtype)


def make_terms(data, place, pieces, turns, partial, slice_rows, types):
    real_data, imag_data = data
    numbers = tuple(pieces)
    offsets, columns = pieces[numbers[0]].shape
    size = len(turns) * slice_rows * len(numbers) * offsets
    return pl.pallas_call(
        functools.partial(terms_kernel, turns, numbers, len(partial)),
        in_specs=[SMEM] + [VMEM] * (2 + len(numbers) + len(partial)),
        out_specs=[VMEM] * len(types) * len(turns),
        out_shape=[jax.ShapeDtypeStruct((slice_rows, columns), kind) for kind in types] * len(turns),
        compiler_params=params(8),
        cost_estimate=cost(4 * size * columns, 4 * size),
        name="terms",
    )(place, real_data, imag_data, *pieces.values(), *partial)


def add_kernel(own_ref, other_ref, out_ref):
    out_ref[...] = (own_ref[...] + other_ref[...].astype(jnp.float32)).astype(out_ref.dtype)


def make_sum(own, other):
    return pl.pallas_call(
        add_kernel,
        in_specs=[VMEM] * 2,
        out_specs=VMEM,
        out_shape=jax.ShapeDtypeStruct(other.shape, other.dtype),
        compiler_params=params(8),
        cost_estimate=cost(other.size, 8 * other.size),
        name="sum",
    )(own, other)


def update(place_ref, wave_ref, own_ref, others, panel_ref, folded):
    predicted = own_ref[...]
    for number, other in enumerate(others):
        term = other[...].astype(jnp.float32)
        if folded and number == 0:
            inner = place_ref[1] % 2 != place_ref[1] // 2 % 2
            term = jnp.where(inner, 0.0, term)
        predicted += term
    kept = predicted.shape[1] // 2
    turned = jnp.concatenate([-predicted[:, kept:], predicted[:, :kept]], axis=1)
    scaled = wave_ref[0] * predicted + wave_ref[1] * turned
    return predicted, panel_ref[...].astype(jnp.float32) - scaled


def estimate_kernel(folded, place_ref, wave_ref, own_ref, *refs):
    *others, panel_ref, out_ref = refs
    primaries = update(place_ref, wave_ref, own_ref, others, panel_ref, folded)[1]
    out_ref[...] = primaries.astype(jnp.bfloat16)


def last_kernel(folded, place_ref, wave_ref, own_ref, *refs):
    *others, panel_ref, multiples_ref, primaries_ref = refs
    predicted, primaries = update(place_ref, wave_ref, own_ref, others, panel_ref, folded)
    kept = predicted.shape[1] // 2
    multiples_ref[:, 0, :] = predicted[:, :kept]
    multiples_ref[:, 1, :] = predicted[:, kept:]
    primaries_ref[:, 0, :] = primaries[:, :kept]
    primaries_ref[:, 1, :] = primaries[:, kept:]


def make_update(place, wavelet, own, others, panel, folded, last):
    rows, columns = panel.shape
    if last:
        shape = [jax.ShapeDtypeStruct((rows, 2, columns // 2), jnp.float32)] * 2
    else:
        shape = jax.ShapeDtypeStruct((rows, columns), jnp.bfloat16)
    return pl.pallas_call(
        functools.partial(last_kernel if last else estimate_kernel, folded),
        in_specs=[SMEM] * 2 + [VMEM] * (2 + len(others)),
        out_specs=[VMEM] * 2 if last else VMEM,
        out_shape=shape,
        compiler_params=params(8),
        cost_estimate=cost(16 * rows * columns, 16 * rows * columns),
        name="update",
    )(place, wavelet, own, *others, panel)


def swap(array, axis, bits):
    size = lax.axis_size(axis)
    return lax.ppermute(array, axis, [(index, index ^ bits) for index in range(size)])


def exchange(n_src, make):
    bf16, f32 = jnp.bfloat16, jnp.float32
    if n_src != 4:
        arriving = [swap(make(turn, [bf16])[0], "src", turn) for turn in range(n_src - 1, 0, -1)]
        return make(0, [f32])[0], arriving, False
    first = lax.ppermute(make(2, [bf16])[0], "src", [(0, 1), (1, 3), (3, 2), (2, 0)])
    sent, kept = make(3, [bf16, f32])
    outer = lax.ppermute(sent, "src", [(0, 3), (3, 0)])
    inner = lax.ppermute(make_sum(kept, first), "src", [(1, 2), (2, 1)])
    beside = swap(make(1, [bf16])[0], "src", 1)
    return make(0, [f32])[0], [first, outer, inner, beside], True


def iterate(estimate, data, place, n_row, n_src, slice_rows, fresh):
    turns = range(2, n_row, 2)
    direct = {turn: swap(estimate, "row", turn) for turn in turns}
    if fresh:
        real_data, *held = lax.optimization_barrier((data[0], *direct.values()))
        data, direct = (real_data, data[1]), dict(zip(direct, held))
    passed = {turn + 1: swap(piece, "row", 1) for turn, piece in {0: estimate, **direct}.items()}
    early = {0: estimate, 1: passed[1], **direct}
    late = {turn: passed[turn] for turn in range(n_row - 1, 1, -2)}
    begun = make_terms(data, place, early, (n_src // 2,), [], slice_rows, [jnp.float32])

    def make(turn, types):
        if turn == n_src // 2:
            return make_terms(data, place, late, (turn,), begun, slice_rows, types)
        return make_terms(data, place, {**early, **late}, (turn,), [], slice_rows, types)

    return *exchange(n_src, make), data


def body(traces, row_source, slice_data, wavelet_inverse):
    block_rows, shots, _ = traces.shape
    n_row, n_src = lax.axis_size("row"), lax.axis_size("src")
    row, src = lax.axis_index("row"), lax.axis_index("src")
    place = jnp.stack([row, src]).astype(jnp.int32)
    packs = LANES // (2 * shots)
    group_rows = block_rows // n_row
    slice_rows = block_rows // n_src
    block = min(group_rows, 128)
    short = block // packs

    spectra = make_spectra(traces, place, n_row, packs, block)
    arrived = [spectra[0]] + [swap(spectra[turn], "row", turn) for turn in range(1, n_row)]

    inside = row_source % group_rows
    position = (row_source // block_rows ^ row) * (group_rows // packs) + inside // block * short + inside % short
    code = position * packs + inside % block // short
    code = jnp.broadcast_to(code[:, None], (block_rows, LANES))
    real_data, _ = relay(slice_data, 0, spectra[0])
    hits = make_hits(code, block_rows // packs, packs, spectra[0])
    ordered = make_order(code, hits, arrived, place, n_src, packs)
    located = [ordered[0]] + [swap(ordered[turn], "src", turn) for turn in range(1, n_src)]
    imag_data, token = relay(slice_data, 1, ordered[0])
    panel = make_panel(located, place, packs, token)

    estimate = panel
    data = real_data, imag_data
    for iteration in range(ITERS):
        own, arriving, folded, data = iterate(estimate, data, place, n_row, n_src, slice_rows, iteration == 0)
        estimate = make_update(place, wavelet_inverse, own, arriving, panel, folded, iteration == ITERS - 1)
    return tuple(estimate)


def solution(mesh):
    in_specs = (P("row", "src", None), P("row"), P(None, "row", None, "src"), P())
    out_specs = (P(("row", "src"), None, None), P(("row", "src"), None, None))
    return jax.shard_map(body, mesh=mesh, in_specs=in_specs, out_specs=out_specs, check_vma=False)
```

```python
import functools

import jax
import jax.numpy as jnp
import ml_dtypes
import numpy as np
from jax import lax
from jax.experimental import pallas as pl
from jax.experimental.pallas import tpu as pltpu
from jax.sharding import PartitionSpec as P

FREQ = 61
ITERS = 3
LANES = 128
BUFFERS = 4
VMEM = pl.BlockSpec(memory_space=pltpu.VMEM)
ANY = pl.BlockSpec(memory_space=pl.ANY)
SMEM = pl.BlockSpec(memory_space=pltpu.SMEM)


def dft_table(samples):
    ticks = np.arange(samples, dtype=np.int32)
    moment = ticks.astype(np.float32)
    ramp_len = samples // 8
    pi = np.float32(np.pi)
    half = np.float32(0.5)
    rising = half - half * np.cos(pi * (moment + half) / np.float32(ramp_len))
    falling = half - half * np.cos(pi * (np.float32(samples) - moment - half) / np.float32(ramp_len))
    taper = np.where(
        ticks < ramp_len, rising, np.where(ticks >= samples - ramp_len, falling, np.ones_like(rising))
    )
    wrapped = ticks * FREQ % samples
    angles = np.float32(2.0 * np.pi / samples) * wrapped.astype(np.float32)
    factor = np.float32(1.0) / np.sqrt(np.float32(samples))
    table = np.stack([taper * np.cos(angles) * factor, -taper * np.sin(angles) * factor], axis=1)
    return table.astype(ml_dtypes.bfloat16)


def params(megabytes):
    return pltpu.CompilerParams(vmem_limit_bytes=megabytes * 2**20)


def cost(flops, moved):
    return pl.CostEstimate(flops=int(flops), bytes_accessed=int(moved), transcendentals=0)


def streamed(steps, source, held, sems, work, ready=None):
    slots = held.shape[0]

    def copy(step):
        slot = step % slots
        return pltpu.make_async_copy(source(step), held.at[slot], sems.at[slot])

    for step in range(min(slots - 1, steps)):
        copy(step).start()
    if ready is not None:
        ready()

    @pl.loop(0, steps)
    def _(step):
        @pl.when(step + slots - 1 < steps)
        def _():
            copy(step + slots - 1).start()

        copy(step).wait()
        work(step, held.at[step % slots])


def spectra_kernel(packs, n_row, place_ref, traces_ref, table_ref, *refs):
    out_refs = refs[:n_row]
    held, sems, wide, table, table_sem = refs[n_row:]
    block = held.shape[1]
    steps = traces_ref.shape[0] // n_row // block

    def source(step):
        first = ((place_ref[0] ^ (step // steps)) * steps + step % steps) * block
        return traces_ref.at[pl.ds(pl.multiple_of(first, block), block)]

    def work(step, traces):
        packed = spectra_of(packs, traces, table)
        for turn, out_ref in enumerate(out_refs):

            @pl.when(step // steps == turn)
            def _():
                out_ref[step % steps] = packed

    def ready():
        copy = pltpu.make_async_copy(table_ref, wide, table_sem)
        copy.start()
        copy.wait()
        table[...] = wide[...].astype(table.dtype)

    streamed(n_row * steps, source, held, sems, work, ready)


def spectra_of(packs, traces_ref, table_ref):
    block, shots, samples = traces_ref.shape
    width = 2 * shots
    shot = lax.broadcasted_iota(jnp.int32, (1, shots, LANES), 1)
    lane = lax.broadcasted_iota(jnp.int32, (1, shots, LANES), 2)
    own = lane % shots == shot
    traces = traces_ref[...].reshape(block * shots, samples)
    terms = jnp.dot(traces, table_ref[...], preferred_element_type=jnp.float32)
    spectra = jnp.sum(jnp.where(own, terms.reshape(block, shots, LANES), 0.0), axis=1)
    short = block // packs
    column = lax.broadcasted_iota(jnp.int32, (short, LANES), 1)
    packed = spectra[:short]
    for part in range(1, packs):
        packed = jnp.where(column // width == part, spectra[part * short : (part + 1) * short], packed)
    return packed.astype(jnp.bfloat16)


def make_spectra(traces, place, n_row, packs, block):
    block_rows, shots, samples = traces.shape
    steps = block_rows // n_row // block
    short = block // packs
    columns = np.tile(np.repeat(dft_table(samples), shots, axis=1), (1, packs))
    table = jnp.asarray(columns.astype(np.float32))

    outs = pl.pallas_call(
        functools.partial(spectra_kernel, packs, n_row),
        in_specs=[SMEM, ANY, pl.BlockSpec(memory_space=pltpu.HBM)],
        out_specs=[VMEM] * n_row,
        out_shape=[jax.ShapeDtypeStruct((steps, short, LANES), jnp.bfloat16)] * n_row,
        scratch_shapes=[
            pltpu.VMEM((BUFFERS + 2, block, shots, samples), jnp.bfloat16),
            pltpu.SemaphoreType.DMA((BUFFERS + 2,)),
            pltpu.VMEM(table.shape, jnp.float32),
            pltpu.VMEM(table.shape, jnp.bfloat16),
            pltpu.SemaphoreType.DMA,
        ],
        compiler_params=params(48),
        cost_estimate=cost(2 * traces.size * LANES, 2 * traces.size),
        name="spectra",
    )(place, traces, table)
    return [out.reshape(steps * short, LANES) for out in outs]


def hits_kernel(packs, code_ref, after_ref, out_ref):
    rows, depth = out_ref.shape
    step = min(rows, 256)
    column = lax.broadcasted_iota(jnp.int32, (step, LANES), 1)
    for first in range(0, rows, step):
        position = code_ref[first : first + step, :] // packs
        for start in range(0, depth, LANES):
            size = min(LANES, depth - start)
            hit = jnp.where(position == column + start, 1.0, 0.0).astype(out_ref.dtype)
            out_ref[first : first + step, start : start + size] = hit[:, :size]


def make_hits(code, depth, packs, after):
    rows = code.shape[0]
    return pl.pallas_call(
        functools.partial(hits_kernel, packs),
        in_specs=[VMEM, ANY],
        out_specs=VMEM,
        out_shape=jax.ShapeDtypeStruct((rows, depth), jnp.bfloat16),
        compiler_params=params(12),
        cost_estimate=cost(rows * depth, 2 * rows * depth),
        name="hits",
    )(code, after)


def order_kernel(packs, n_src, place_ref, code_ref, hits_ref, *refs):
    pieces, out_refs = refs[:-n_src], refs[-n_src:]
    width = LANES // packs
    held = jnp.concatenate([ref[...] for ref in reversed(pieces)], axis=0)
    rolled = [held] + [
        pltpu.roll(held.astype(jnp.float32), turn * width, 1).astype(jnp.bfloat16) for turn in range(1, packs)
    ]
    table = jnp.concatenate(rolled, axis=1)
    slice_rows = code_ref.shape[0] // n_src
    short = slice_rows // packs
    column = lax.broadcasted_iota(jnp.int32, (short, LANES), 1)
    for turn, out_ref in enumerate(out_refs):
        first = pl.multiple_of((place_ref[1] ^ turn) * slice_rows, slice_rows)
        packed = None
        for part in range(packs):
            chosen = pl.ds(pl.multiple_of(first + part * short, short), short)
            side = code_ref[chosen, :] % packs
            rows = jnp.dot(hits_ref[chosen, :], table, preferred_element_type=jnp.float32)
            moved = rows[:, :LANES]
            for turned in range(1, packs):
                moved = jnp.where(
                    (part - side + packs) % packs == turned, rows[:, turned * LANES : (turned + 1) * LANES], moved
                )
            packed = moved if packed is None else jnp.where(column // width == part, moved, packed)
        out_ref[...] = packed.astype(jnp.bfloat16)


def make_order(code, hits, pieces, place, n_src, packs):
    slice_rows = code.shape[0] // n_src
    return pl.pallas_call(
        functools.partial(order_kernel, packs, n_src),
        in_specs=[SMEM] + [VMEM] * (2 + len(pieces)),
        out_specs=[VMEM] * n_src,
        out_shape=[jax.ShapeDtypeStruct((slice_rows // packs, LANES), jnp.bfloat16)] * n_src,
        compiler_params=params(12),
        cost_estimate=cost(2 * hits.size * LANES * packs, 4 * code.size),
        name="order",
    )(place, code, hits, *pieces)


def panel_kernel(packs, place_ref, *refs):
    pieces, panel_ref = refs[:-2], refs[-1]
    short = pieces[0].shape[0]
    width = LANES // packs
    shots = width // 2
    columns = panel_ref.shape[1]
    lane = lax.broadcasted_iota(jnp.int32, (LANES, packs * columns), 0)
    target = lax.broadcasted_iota(jnp.int32, (LANES, packs * columns), 1)
    total = None
    for turn, piece in enumerate(pieces):
        shot = (place_ref[1] ^ turn) * shots + lane % shots
        goes = lane // width * columns + lane % width // shots * (columns // 2) + shot
        chosen = jnp.where(target == goes, 1.0, 0.0).astype(jnp.bfloat16)
        term = jnp.dot(piece[...], chosen, preferred_element_type=jnp.float32)
        total = term if total is None else total + term
    for part in range(packs):
        panel_ref[part * short : (part + 1) * short, :] = total[:, part * columns : (part + 1) * columns].astype(
            jnp.bfloat16
        )


def make_panel(pieces, place, packs, after):
    rows = pieces[0].shape[0] * packs
    columns = len(pieces) * (LANES // packs)
    return pl.pallas_call(
        functools.partial(panel_kernel, packs),
        in_specs=[SMEM] + [VMEM] * len(pieces) + [ANY],
        out_specs=VMEM,
        out_shape=jax.ShapeDtypeStruct((rows, columns), jnp.bfloat16),
        compiler_params=params(8),
        cost_estimate=cost(2 * len(pieces) * rows * LANES * columns, 4 * rows * columns),
        name="panel",
    )(place, *pieces, after)


def relay_kernel(part, data_ref, after_ref, out_ref, token_ref, held, sems):
    token_ref[...] = jnp.zeros_like(token_ref)
    step_rows = held.shape[1]

    def source(step):
        return data_ref.at[part, pl.ds(pl.multiple_of(step * step_rows, step_rows), step_rows)]

    def work(step, data):
        rows = pl.ds(pl.multiple_of(step * step_rows, step_rows), step_rows)
        out_ref[:, rows, :] = jnp.swapaxes(data[...], 0, 1)

    streamed(data_ref.shape[1] // step_rows, source, held, sems, work)


def relay(slice_data, part, after):
    _, block_rows, blocks, offsets = slice_data.shape
    step_rows = min(block_rows, 128)
    return pl.pallas_call(
        functools.partial(relay_kernel, part),
        in_specs=[ANY, ANY],
        out_specs=[VMEM] * 2,
        out_shape=[
            jax.ShapeDtypeStruct((blocks, block_rows, offsets), jnp.bfloat16),
            jax.ShapeDtypeStruct((8, LANES), jnp.float32),
        ],
        scratch_shapes=[
            pltpu.VMEM((BUFFERS, step_rows, blocks, offsets), jnp.bfloat16),
            pltpu.SemaphoreType.DMA((BUFFERS,)),
        ],
        compiler_params=params(12),
        cost_estimate=cost(0, 2 * slice_data.size),
        name="relay",
    )(slice_data, after)


def terms_kernel(turns, numbers, begun, place_ref, real_ref, imag_ref, *refs):
    pieces = refs[: len(numbers)]
    partial = refs[len(numbers) : len(numbers) + begun]
    out_refs = refs[len(numbers) + begun :]
    columns = pieces[0].shape[1]
    kept = columns // 2
    size = out_refs[0].shape[0]
    each = len(out_refs) // len(turns)
    for index, turn in enumerate(turns):
        rows = pl.ds(pl.multiple_of((place_ref[1] ^ turn) * size, size), size)
        total = jnp.zeros((2 * size, columns), jnp.float32)
        for number, piece in zip(numbers, pieces):
            block = place_ref[0] ^ number
            both = jnp.concatenate([real_ref[block, rows, :], imag_ref[block, rows, :]], axis=0)
            total += jnp.dot(both, piece[...], preferred_element_type=jnp.float32)
        by_real, by_imag = total[:size], total[size:]
        real = by_real[:, :kept] - by_imag[:, kept:]
        imag = by_real[:, kept:] + by_imag[:, :kept]
        if begun:
            real += partial[index][:, :kept]
            imag += partial[index][:, kept:]
        for out_ref in out_refs[index * each : (index + 1) * each]:
            out_ref[:, :kept] = real.astype(out_ref.dtype)
            out_ref[:, kept:] = imag.astype(out_ref.dtype)


def make_terms(data, place, pieces, turns, partial, slice_rows, types):
    real_data, imag_data = data
    numbers = tuple(pieces)
    offsets, columns = pieces[numbers[0]].shape
    size = len(turns) * slice_rows * len(numbers) * offsets
    return pl.pallas_call(
        functools.partial(terms_kernel, turns, numbers, len(partial)),
        in_specs=[SMEM] + [VMEM] * (2 + len(numbers) + len(partial)),
        out_specs=[VMEM] * len(types) * len(turns),
        out_shape=[jax.ShapeDtypeStruct((slice_rows, columns), kind) for kind in types] * len(turns),
        compiler_params=params(8),
        cost_estimate=cost(4 * size * columns, 4 * size),
        name="terms",
    )(place, real_data, imag_data, *pieces.values(), *partial)


def add_kernel(own_ref, other_ref, out_ref):
    out_ref[...] = (own_ref[...] + other_ref[...].astype(jnp.float32)).astype(out_ref.dtype)


def make_sum(own, other):
    return pl.pallas_call(
        add_kernel,
        in_specs=[VMEM] * 2,
        out_specs=VMEM,
        out_shape=jax.ShapeDtypeStruct(other.shape, other.dtype),
        compiler_params=params(8),
        cost_estimate=cost(other.size, 8 * other.size),
        name="sum",
    )(own, other)


def update(place_ref, wave_ref, own_ref, others, panel_ref, folded):
    predicted = own_ref[...]
    for number, other in enumerate(others):
        term = other[...].astype(jnp.float32)
        if folded and number == 0:
            inner = place_ref[1] % 2 != place_ref[1] // 2 % 2
            term = jnp.where(inner, 0.0, term)
        predicted += term
    kept = predicted.shape[1] // 2
    turned = jnp.concatenate([-predicted[:, kept:], predicted[:, :kept]], axis=1)
    scaled = wave_ref[0] * predicted + wave_ref[1] * turned
    return predicted, panel_ref[...].astype(jnp.float32) - scaled


def estimate_kernel(folded, place_ref, wave_ref, own_ref, *refs):
    *others, panel_ref, out_ref = refs
    primaries = update(place_ref, wave_ref, own_ref, others, panel_ref, folded)[1]
    out_ref[...] = primaries.astype(jnp.bfloat16)


def last_kernel(folded, place_ref, wave_ref, own_ref, *refs):
    *others, panel_ref, multiples_ref, primaries_ref = refs
    predicted, primaries = update(place_ref, wave_ref, own_ref, others, panel_ref, folded)
    kept = predicted.shape[1] // 2
    multiples_ref[:, 0, :] = predicted[:, :kept]
    multiples_ref[:, 1, :] = predicted[:, kept:]
    primaries_ref[:, 0, :] = primaries[:, :kept]
    primaries_ref[:, 1, :] = primaries[:, kept:]


def make_update(place, wavelet, own, others, panel, folded, last):
    rows, columns = panel.shape
    if last:
        shape = [jax.ShapeDtypeStruct((rows, 2, columns // 2), jnp.float32)] * 2
    else:
        shape = jax.ShapeDtypeStruct((rows, columns), jnp.bfloat16)
    return pl.pallas_call(
        functools.partial(last_kernel if last else estimate_kernel, folded),
        in_specs=[SMEM] * 2 + [VMEM] * (2 + len(others)),
        out_specs=[VMEM] * 2 if last else VMEM,
        out_shape=shape,
        compiler_params=params(8),
        cost_estimate=cost(16 * rows * columns, 16 * rows * columns),
        name="update",
    )(place, wavelet, own, *others, panel)


def swap(array, axis, bits):
    size = lax.axis_size(axis)
    return lax.ppermute(array, axis, [(index, index ^ bits) for index in range(size)])


def exchange(n_src, make):
    bf16, f32 = jnp.bfloat16, jnp.float32
    if n_src != 4:
        arriving = [swap(make(turn, [bf16])[0], "src", turn) for turn in range(n_src - 1, 0, -1)]
        return make(0, [f32])[0], arriving, False
    first = lax.ppermute(make(2, [bf16])[0], "src", [(0, 1), (1, 3), (3, 2), (2, 0)])
    sent, kept = make(3, [bf16, f32])
    beside = swap(make(1, [bf16])[0], "src", 1)
    outer = lax.ppermute(sent, "src", [(0, 3), (3, 0)])
    inner = lax.ppermute(make_sum(kept, first), "src", [(1, 2), (2, 1)])
    return make(0, [f32])[0], [first, beside, outer, inner], True


def iterate(estimate, data, place, n_row, n_src, slice_rows, fresh):
    turns = range(2, n_row, 2)
    direct = {turn: swap(estimate, "row", turn) for turn in (reversed(turns) if fresh else turns)}
    if fresh:
        real_data, *held = lax.optimization_barrier((data[0], *direct.values()))
        data, direct = (real_data, data[1]), dict(zip(direct, held))
    passed = {turn + 1: swap(piece, "row", 1) for turn, piece in {0: estimate, **direct}.items()}
    early = {0: estimate, 1: passed[1], **direct}
    late = {turn: passed[turn] for turn in range(n_row - 1, 1, -2)}
    begun = make_terms(data, place, early, (n_src // 2,), [], slice_rows, [jnp.float32])

    def make(turn, types):
        if turn == n_src // 2:
            return make_terms(data, place, late, (turn,), begun, slice_rows, types)
        return make_terms(data, place, {**early, **late}, (turn,), [], slice_rows, types)

    return *exchange(n_src, make), data


def body(traces, row_source, slice_data, wavelet_inverse):
    block_rows, shots, _ = traces.shape
    n_row, n_src = lax.axis_size("row"), lax.axis_size("src")
    row, src = lax.axis_index("row"), lax.axis_index("src")
    place = jnp.stack([row, src]).astype(jnp.int32)
    packs = LANES // (2 * shots)
    group_rows = block_rows // n_row
    slice_rows = block_rows // n_src
    block = min(group_rows, 128)
    short = block // packs

    spectra = make_spectra(traces, place, n_row, packs, block)
    arrived = [swap(spectra[turn], "row", turn) for turn in range(n_row - 1, 0, -1)] + [spectra[0]]

    inside = row_source % group_rows
    position = (row_source // block_rows ^ row) * (group_rows // packs) + inside // block * short + inside % short
    code = position * packs + inside % block // short
    code = jnp.broadcast_to(code[:, None], (block_rows, LANES))
    real_data, _ = relay(slice_data, 0, spectra[0])
    hits = make_hits(code, block_rows // packs, packs, spectra[0])
    ordered = make_order(code, hits, arrived, place, n_src, packs)
    located = [ordered[0]] + [swap(ordered[turn], "src", turn) for turn in range(1, n_src)]
    imag_data, token = relay(slice_data, 1, ordered[0])
    panel = make_panel(located, place, packs, token)

    estimate = panel
    data = real_data, imag_data
    for iteration in range(ITERS):
        own, arriving, folded, data = iterate(estimate, data, place, n_row, n_src, slice_rows, iteration == 0)
        estimate = make_update(place, wavelet_inverse, own, arriving, panel, folded, iteration == ITERS - 1)
    return tuple(estimate)


def solution(mesh):
    in_specs = (P("row", "src", None), P("row"), P(None, "row", None, "src"), P())
    out_specs = (P(("row", "src"), None, None), P(("row", "src"), None, None))
    return jax.shard_map(body, mesh=mesh, in_specs=in_specs, out_specs=out_specs, check_vma=False)
```

```python
import functools

import jax
import jax.numpy as jnp
import ml_dtypes
import numpy as np
from jax import lax
from jax.experimental import pallas as pl
from jax.experimental.pallas import tpu as pltpu
from jax.sharding import PartitionSpec as P

FREQ = 61
ITERS = 3
LANES = 128
BUFFERS = 4
SPARE_ROWS = 2**14
VMEM = pl.BlockSpec(memory_space=pltpu.VMEM)
ANY = pl.BlockSpec(memory_space=pl.ANY)
SMEM = pl.BlockSpec(memory_space=pltpu.SMEM)


def dft_table(samples):
    ticks = np.arange(samples, dtype=np.int32)
    moment = ticks.astype(np.float32)
    ramp_len = samples // 8
    pi = np.float32(np.pi)
    half = np.float32(0.5)
    rising = half - half * np.cos(pi * (moment + half) / np.float32(ramp_len))
    falling = half - half * np.cos(pi * (np.float32(samples) - moment - half) / np.float32(ramp_len))
    taper = np.where(
        ticks < ramp_len, rising, np.where(ticks >= samples - ramp_len, falling, np.ones_like(rising))
    )
    wrapped = ticks * FREQ % samples
    angles = np.float32(2.0 * np.pi / samples) * wrapped.astype(np.float32)
    factor = np.float32(1.0) / np.sqrt(np.float32(samples))
    table = np.stack([taper * np.cos(angles) * factor, -taper * np.sin(angles) * factor], axis=1)
    return table.astype(ml_dtypes.bfloat16)


def params(megabytes):
    return pltpu.CompilerParams(vmem_limit_bytes=megabytes * 2**20)


def cost(flops, moved):
    return pl.CostEstimate(flops=int(flops), bytes_accessed=int(moved), transcendentals=0)


def streamed(steps, source, held, sems, work, ready=None):
    slots = held.shape[0]

    def copy(step):
        slot = step % slots
        return pltpu.make_async_copy(source(step), held.at[slot], sems.at[slot])

    for step in range(min(slots - 1, steps)):
        copy(step).start()
    if ready is not None:
        ready()

    @pl.loop(0, steps)
    def _(step):
        @pl.when(step + slots - 1 < steps)
        def _():
            copy(step + slots - 1).start()

        copy(step).wait()
        work(step, held.at[step % slots])


def spectra_kernel(packs, n_row, place_ref, traces_ref, table_ref, *refs):
    out_refs = refs[:n_row]
    held, sems, wide, table, table_sem = refs[n_row:]
    block = held.shape[1]
    steps = traces_ref.shape[0] // n_row // block

    def source(step):
        first = ((place_ref[0] ^ (step // steps)) * steps + step % steps) * block
        return traces_ref.at[pl.ds(pl.multiple_of(first, block), block)]

    def work(step, traces):
        packed = spectra_of(packs, traces, table)
        for turn, out_ref in enumerate(out_refs):

            @pl.when(step // steps == turn)
            def _():
                out_ref[step % steps] = packed

    def ready():
        copy = pltpu.make_async_copy(table_ref.at[pl.ds(0, wide.shape[0])], wide, table_sem)
        copy.start()
        copy.wait()
        table[...] = wide[...].astype(table.dtype)

    streamed(n_row * steps, source, held, sems, work, ready)


def spectra_of(packs, traces_ref, table_ref):
    block, shots, samples = traces_ref.shape
    width = 2 * shots
    shot = lax.broadcasted_iota(jnp.int32, (1, shots, LANES), 1)
    lane = lax.broadcasted_iota(jnp.int32, (1, shots, LANES), 2)
    own = lane % shots == shot
    traces = traces_ref[...].reshape(block * shots, samples)
    terms = jnp.dot(traces, table_ref[...], preferred_element_type=jnp.float32)
    spectra = jnp.sum(jnp.where(own, terms.reshape(block, shots, LANES), 0.0), axis=1)
    short = block // packs
    column = lax.broadcasted_iota(jnp.int32, (short, LANES), 1)
    packed = spectra[:short]
    for part in range(1, packs):
        packed = jnp.where(column // width == part, spectra[part * short : (part + 1) * short], packed)
    return packed.astype(jnp.bfloat16)


def make_spectra(traces, place, n_row, packs, block):
    block_rows, shots, samples = traces.shape
    steps = block_rows // n_row // block
    short = block // packs
    columns = np.tile(np.repeat(dft_table(samples), shots, axis=1), (1, packs))
    table = jnp.asarray(np.pad(columns.astype(np.float32), ((0, SPARE_ROWS), (0, 0))))

    outs = pl.pallas_call(
        functools.partial(spectra_kernel, packs, n_row),
        in_specs=[SMEM, ANY, pl.BlockSpec(memory_space=pltpu.HBM)],
        out_specs=[VMEM] * n_row,
        out_shape=[jax.ShapeDtypeStruct((steps, short, LANES), jnp.bfloat16)] * n_row,
        scratch_shapes=[
            pltpu.VMEM((BUFFERS + 2, block, shots, samples), jnp.bfloat16),
            pltpu.SemaphoreType.DMA((BUFFERS + 2,)),
            pltpu.VMEM(columns.shape, jnp.float32),
            pltpu.VMEM(columns.shape, jnp.bfloat16),
            pltpu.SemaphoreType.DMA,
        ],
        compiler_params=params(50),
        cost_estimate=cost(2 * traces.size * LANES, 2 * traces.size),
        name="spectra",
    )(place, traces, table)
    return [out.reshape(steps * short, LANES) for out in outs]


def hits_kernel(packs, code_ref, after_ref, out_ref):
    rows, depth = out_ref.shape
    step = min(rows, 256)
    column = lax.broadcasted_iota(jnp.int32, (step, LANES), 1)
    for first in range(0, rows, step):
        position = code_ref[first : first + step, :] // packs
        for start in range(0, depth, LANES):
            size = min(LANES, depth - start)
            hit = jnp.where(position == column + start, 1.0, 0.0).astype(out_ref.dtype)
            out_ref[first : first + step, start : start + size] = hit[:, :size]


def make_hits(code, depth, packs, after):
    rows = code.shape[0]
    return pl.pallas_call(
        functools.partial(hits_kernel, packs),
        in_specs=[VMEM, ANY],
        out_specs=VMEM,
        out_shape=jax.ShapeDtypeStruct((rows, depth), jnp.bfloat16),
        compiler_params=params(12),
        cost_estimate=cost(rows * depth, 2 * rows * depth),
        name="hits",
    )(code, after)


def order_kernel(packs, n_src, place_ref, code_ref, hits_ref, *refs):
    pieces, out_refs = refs[:-n_src], refs[-n_src:]
    width = LANES // packs
    held = jnp.concatenate([ref[...] for ref in reversed(pieces)], axis=0)
    rolled = [held] + [
        pltpu.roll(held.astype(jnp.float32), turn * width, 1).astype(jnp.bfloat16) for turn in range(1, packs)
    ]
    table = jnp.concatenate(rolled, axis=1)
    slice_rows = code_ref.shape[0] // n_src
    short = slice_rows // packs
    column = lax.broadcasted_iota(jnp.int32, (short, LANES), 1)
    for turn, out_ref in enumerate(out_refs):
        first = pl.multiple_of((place_ref[1] ^ turn) * slice_rows, slice_rows)
        packed = None
        for part in range(packs):
            chosen = pl.ds(pl.multiple_of(first + part * short, short), short)
            side = code_ref[chosen, :] % packs
            rows = jnp.dot(hits_ref[chosen, :], table, preferred_element_type=jnp.float32)
            moved = rows[:, :LANES]
            for turned in range(1, packs):
                moved = jnp.where(
                    (part - side + packs) % packs == turned, rows[:, turned * LANES : (turned + 1) * LANES], moved
                )
            packed = moved if packed is None else jnp.where(column // width == part, moved, packed)
        out_ref[...] = packed.astype(jnp.bfloat16)


def make_order(code, hits, pieces, place, n_src, packs):
    slice_rows = code.shape[0] // n_src
    return pl.pallas_call(
        functools.partial(order_kernel, packs, n_src),
        in_specs=[SMEM] + [VMEM] * (2 + len(pieces)),
        out_specs=[VMEM] * n_src,
        out_shape=[jax.ShapeDtypeStruct((slice_rows // packs, LANES), jnp.bfloat16)] * n_src,
        compiler_params=params(12),
        cost_estimate=cost(2 * hits.size * LANES * packs, 4 * code.size),
        name="order",
    )(place, code, hits, *pieces)


def panel_kernel(packs, place_ref, *refs):
    pieces, panel_ref = refs[:-2], refs[-1]
    short = pieces[0].shape[0]
    width = LANES // packs
    shots = width // 2
    columns = panel_ref.shape[1]
    lane = lax.broadcasted_iota(jnp.int32, (LANES, packs * columns), 0)
    target = lax.broadcasted_iota(jnp.int32, (LANES, packs * columns), 1)
    total = None
    for turn, piece in enumerate(reversed(pieces)):
        shot = (place_ref[1] ^ turn) * shots + lane % shots
        goes = lane // width * columns + lane % width // shots * (columns // 2) + shot
        chosen = jnp.where(target == goes, 1.0, 0.0).astype(jnp.bfloat16)
        term = jnp.dot(piece[...], chosen, preferred_element_type=jnp.float32)
        total = term if total is None else total + term
    for part in range(packs):
        panel_ref[part * short : (part + 1) * short, :] = total[:, part * columns : (part + 1) * columns].astype(
            jnp.bfloat16
        )


def make_panel(pieces, place, packs, after):
    rows = pieces[0].shape[0] * packs
    columns = len(pieces) * (LANES // packs)
    return pl.pallas_call(
        functools.partial(panel_kernel, packs),
        in_specs=[SMEM] + [VMEM] * len(pieces) + [ANY],
        out_specs=VMEM,
        out_shape=jax.ShapeDtypeStruct((rows, columns), jnp.bfloat16),
        compiler_params=params(8),
        cost_estimate=cost(2 * len(pieces) * rows * LANES * columns, 4 * rows * columns),
        name="panel",
    )(place, *pieces, after)


def relay_kernel(part, data_ref, after_ref, out_ref, token_ref, held, sems):
    token_ref[...] = jnp.zeros_like(token_ref)
    step_rows = held.shape[1]

    def source(step):
        return data_ref.at[part, pl.ds(pl.multiple_of(step * step_rows, step_rows), step_rows)]

    def work(step, data):
        rows = pl.ds(pl.multiple_of(step * step_rows, step_rows), step_rows)
        out_ref[:, rows, :] = jnp.swapaxes(data[...], 0, 1)

    streamed(data_ref.shape[1] // step_rows, source, held, sems, work)


def relay(slice_data, part, after):
    _, block_rows, blocks, offsets = slice_data.shape
    step_rows = min(block_rows, 128)
    return pl.pallas_call(
        functools.partial(relay_kernel, part),
        in_specs=[ANY, ANY],
        out_specs=[VMEM] * 2,
        out_shape=[
            jax.ShapeDtypeStruct((blocks, block_rows, offsets), jnp.bfloat16),
            jax.ShapeDtypeStruct((8, LANES), jnp.float32),
        ],
        scratch_shapes=[
            pltpu.VMEM((BUFFERS, step_rows, blocks, offsets), jnp.bfloat16),
            pltpu.SemaphoreType.DMA((BUFFERS,)),
        ],
        compiler_params=params(12),
        cost_estimate=cost(0, 2 * slice_data.size),
        name="relay",
    )(slice_data, after)


def terms_kernel(turns, numbers, begun, place_ref, real_ref, imag_ref, *refs):
    pieces = refs[: len(numbers)]
    partial = refs[len(numbers) : len(numbers) + begun]
    out_refs = refs[len(numbers) + begun :]
    columns = pieces[0].shape[1]
    kept = columns // 2
    size = out_refs[0].shape[0]
    each = len(out_refs) // len(turns)
    for index, turn in enumerate(turns):
        rows = pl.ds(pl.multiple_of((place_ref[1] ^ turn) * size, size), size)
        total = jnp.zeros((2 * size, columns), jnp.float32)
        for number, piece in zip(numbers, pieces):
            block = place_ref[0] ^ number
            both = jnp.concatenate([real_ref[block, rows, :], imag_ref[block, rows, :]], axis=0)
            total += jnp.dot(both, piece[...], preferred_element_type=jnp.float32)
        by_real, by_imag = total[:size], total[size:]
        real = by_real[:, :kept] - by_imag[:, kept:]
        imag = by_real[:, kept:] + by_imag[:, :kept]
        if begun:
            real += partial[index][:, :kept]
            imag += partial[index][:, kept:]
        for out_ref in out_refs[index * each : (index + 1) * each]:
            out_ref[:, :kept] = real.astype(out_ref.dtype)
            out_ref[:, kept:] = imag.astype(out_ref.dtype)


def make_terms(data, place, pieces, turns, partial, slice_rows, types):
    real_data, imag_data = data
    numbers = tuple(pieces)
    offsets, columns = pieces[numbers[0]].shape
    size = len(turns) * slice_rows * len(numbers) * offsets
    return pl.pallas_call(
        functools.partial(terms_kernel, turns, numbers, len(partial)),
        in_specs=[SMEM] + [VMEM] * (2 + len(numbers) + len(partial)),
        out_specs=[VMEM] * len(types) * len(turns),
        out_shape=[jax.ShapeDtypeStruct((slice_rows, columns), kind) for kind in types] * len(turns),
        compiler_params=params(8),
        cost_estimate=cost(4 * size * columns, 4 * size),
        name="terms",
    )(place, real_data, imag_data, *pieces.values(), *partial)


def add_kernel(own_ref, other_ref, out_ref):
    out_ref[...] = (own_ref[...] + other_ref[...].astype(jnp.float32)).astype(out_ref.dtype)


def make_sum(own, other):
    return pl.pallas_call(
        add_kernel,
        in_specs=[VMEM] * 2,
        out_specs=VMEM,
        out_shape=jax.ShapeDtypeStruct(other.shape, other.dtype),
        compiler_params=params(8),
        cost_estimate=cost(other.size, 8 * other.size),
        name="sum",
    )(own, other)


def update(place_ref, wave_ref, own_ref, others, panel_ref, folded):
    predicted = own_ref[...]
    for number, other in enumerate(others):
        term = other[...].astype(jnp.float32)
        if folded and number == 0:
            inner = place_ref[1] % 2 != place_ref[1] // 2 % 2
            term = jnp.where(inner, 0.0, term)
        predicted += term
    kept = predicted.shape[1] // 2
    turned = jnp.concatenate([-predicted[:, kept:], predicted[:, :kept]], axis=1)
    scaled = wave_ref[0] * predicted + wave_ref[1] * turned
    return predicted, panel_ref[...].astype(jnp.float32) - scaled


def estimate_kernel(folded, place_ref, wave_ref, own_ref, *refs):
    *others, panel_ref, out_ref = refs
    primaries = update(place_ref, wave_ref, own_ref, others, panel_ref, folded)[1]
    out_ref[...] = primaries.astype(jnp.bfloat16)


def last_kernel(folded, place_ref, wave_ref, own_ref, *refs):
    *others, panel_ref, multiples_ref, primaries_ref = refs
    predicted, primaries = update(place_ref, wave_ref, own_ref, others, panel_ref, folded)
    kept = predicted.shape[1] // 2
    multiples_ref[:, 0, :] = predicted[:, :kept]
    multiples_ref[:, 1, :] = predicted[:, kept:]
    primaries_ref[:, 0, :] = primaries[:, :kept]
    primaries_ref[:, 1, :] = primaries[:, kept:]


def make_update(place, wavelet, own, others, panel, folded, last):
    rows, columns = panel.shape
    if last:
        shape = [jax.ShapeDtypeStruct((rows, 2, columns // 2), jnp.float32)] * 2
    else:
        shape = jax.ShapeDtypeStruct((rows, columns), jnp.bfloat16)
    return pl.pallas_call(
        functools.partial(last_kernel if last else estimate_kernel, folded),
        in_specs=[SMEM] * 2 + [VMEM] * (2 + len(others)),
        out_specs=[VMEM] * 2 if last else VMEM,
        out_shape=shape,
        compiler_params=params(8),
        cost_estimate=cost(16 * rows * columns, 16 * rows * columns),
        name="update",
    )(place, wavelet, own, *others, panel)


def swap(array, axis, bits):
    size = lax.axis_size(axis)
    return lax.ppermute(array, axis, [(index, index ^ bits) for index in range(size)])


def exchange(n_src, make):
    bf16, f32 = jnp.bfloat16, jnp.float32
    if n_src != 4:
        arriving = [swap(make(turn, [bf16])[0], "src", turn) for turn in range(n_src - 1, 0, -1)]
        return make(0, [f32])[0], arriving, False
    first = lax.ppermute(make(2, [bf16])[0], "src", [(0, 1), (1, 3), (3, 2), (2, 0)])
    sent, kept = make(3, [bf16, f32])
    beside = swap(make(1, [bf16])[0], "src", 1)
    outer = lax.ppermute(sent, "src", [(0, 3), (3, 0)])
    inner = lax.ppermute(make_sum(kept, first), "src", [(1, 2), (2, 1)])
    return make(0, [f32])[0], [first, beside, outer, inner], True


def iterate(estimate, data, place, n_row, n_src, slice_rows, fresh):
    turns = range(2, n_row, 2)
    direct = {turn: swap(estimate, "row", turn) for turn in (reversed(turns) if fresh else turns)}
    if fresh:
        real_data, *held = lax.optimization_barrier((data[0], *direct.values()))
        data, direct = (real_data, data[1]), dict(zip(direct, held))
    passed = {turn + 1: swap(piece, "row", 1) for turn, piece in {0: estimate, **direct}.items()}
    early = {0: estimate, 1: passed[1], **direct}
    late = {turn: passed[turn] for turn in range(n_row - 1, 1, -2)}
    begun = make_terms(data, place, early, (n_src // 2,), [], slice_rows, [jnp.float32])

    def make(turn, types):
        if turn == n_src // 2:
            return make_terms(data, place, late, (turn,), begun, slice_rows, types)
        return make_terms(data, place, {**early, **late}, (turn,), [], slice_rows, types)

    return *exchange(n_src, make), data


def body(traces, row_source, slice_data, wavelet_inverse):
    block_rows, shots, _ = traces.shape
    n_row, n_src = lax.axis_size("row"), lax.axis_size("src")
    row, src = lax.axis_index("row"), lax.axis_index("src")
    place = jnp.stack([row, src]).astype(jnp.int32)
    packs = LANES // (2 * shots)
    group_rows = block_rows // n_row
    slice_rows = block_rows // n_src
    block = min(group_rows, 128)
    short = block // packs

    spectra = make_spectra(traces, place, n_row, packs, block)
    arrived = [swap(spectra[turn], "row", turn) for turn in range(n_row - 1, 0, -1)] + [spectra[0]]

    inside = row_source % group_rows
    position = (row_source // block_rows ^ row) * (group_rows // packs) + inside // block * short + inside % short
    code = position * packs + inside % block // short
    code = jnp.broadcast_to(code[:, None], (block_rows, LANES))
    real_data, _ = relay(slice_data, 0, spectra[0])
    hits = make_hits(code, block_rows // packs, packs, spectra[0])
    ordered = make_order(code, hits, arrived, place, n_src, packs)
    located = [swap(ordered[turn], "src", turn) for turn in range(n_src - 1, 0, -1)] + [ordered[0]]
    imag_data, token = relay(slice_data, 1, ordered[0])
    panel = make_panel(located, place, packs, token)

    estimate = panel
    data = real_data, imag_data
    for iteration in range(ITERS):
        own, arriving, folded, data = iterate(estimate, data, place, n_row, n_src, slice_rows, iteration == 0)
        estimate = make_update(place, wavelet_inverse, own, arriving, panel, folded, iteration == ITERS - 1)
    return tuple(estimate)


def solution(mesh):
    in_specs = (P("row", "src", None), P("row"), P(None, "row", None, "src"), P())
    out_specs = (P(("row", "src"), None, None), P(("row", "src"), None, None))
    return jax.shard_map(body, mesh=mesh, in_specs=in_specs, out_specs=out_specs, check_vma=False)
```
